32 devices in a mesh: dp: 8 (over z, x), mp: 4 (over y, core).
Axes of the slice: x: 2, y: 2, z: 4, core: 2. Of those that a mesh axis runs over, the one named last changes fastest.
Arguments:
- images: bfloat16 [2, 8, 608, 1024], P(None, 'dp', 'mp'), may hold values from -6 to 6
- counts: int32 [2, 8], P(None, 'dp'), may hold values from 0 to 1, as said below
- first_gain: bfloat16 [1024], P('dp'), may hold values from 0.5 to 1.5
- first_shift: bfloat16 [1024], P('dp'), may hold values from -1.796875 to 1.796875
- query_weight: bfloat16 [1024, 1024], P('dp', 'mp'), may hold values from -0.375 to 0.375
- query_bias: bfloat16 [4, 256], P('mp', 'dp'), may hold values from -3 to 3
- key_weight: bfloat16 [1024, 1024], P('dp', 'mp'), may hold values from -0.1875 to 0.1875
- value_weight: bfloat16 [1024, 1024], P('dp', 'mp'), may hold values from -0.1875 to 0.1875
- value_bias: bfloat16 [4, 256], P('mp', 'dp'), may hold values from -3 to 3
- out_weight: bfloat16 [1024, 1024], P('dp', 'mp'), may hold values from -1 to 1
- out_bias: bfloat16 [1024], P('dp'), may hold values from -1.796875 to 1.796875
- second_gain: bfloat16 [1024], P('dp'), may hold values from 0.5 to 1.5
- second_shift: bfloat16 [1024], P('dp'), may hold values from -1.796875 to 1.796875
- up_weight: bfloat16 [1024, 4096], P('dp', 'mp'), may hold values from -0.1875 to 0.1875
- up_bias: bfloat16 [4, 1024], P('mp', 'dp'), may hold values from -3 to 3
- down_weight: bfloat16 [1024, 4096], P('dp', 'mp'), may hold values from -0.09375 to 0.09375
- down_bias: bfloat16 [1024], P('dp'), may hold values from -1.796875 to 1.796875
- clip_tau: float32 [], replicated, may hold values from 3.5 to 5.5
- out_grad: bfloat16 [2, 8, 608, 1024], P(None, 'dp', 'mp'), may hold values from -6 to 6
Outputs:
- result: bfloat16 [2, 8, 608, 1024], P(None, 'dp', 'mp')
- input_grad: bfloat16 [2, 8, 608, 1024], P(None, 'dp', 'mp')
- first_gain_grad: float32 [1024], P('dp')
- first_shift_grad: float32 [1024], P('dp')
- query_weight_grad: float32 [1024, 1024], P('dp', 'mp')
- query_bias_grad: float32 [4, 256], P('mp', 'dp')
- key_weight_grad: float32 [1024, 1024], P('dp', 'mp')
- value_weight_grad: float32 [1024, 1024], P('dp', 'mp')
- value_bias_grad: float32 [4, 256], P('mp', 'dp')
- out_weight_grad: float32 [1024, 1024], P('dp', 'mp')
- out_bias_grad: float32 [1024], P('dp')
- second_gain_grad: float32 [1024], P('dp')
- second_shift_grad: float32 [1024], P('dp')
- up_weight_grad: float32 [1024, 4096], P('dp', 'mp')
- up_bias_grad: float32 [4, 1024], P('mp', 'dp')
- down_weight_grad: float32 [1024, 4096], P('dp', 'mp')
- down_bias_grad: float32 [1024], P('dp')
- logit_peaks: float32 [16], P('mp')
- clipped_query: float32 [1024, 1024], P('dp', 'mp')
- clipped_key: float32 [1024, 1024], P('dp', 'mp')
- clipped_bias: float32 [4, 256], P('mp', 'dp')
The draws below stay inside these ranges and needn't reach their ends.
Inputs may be any that keep to these rules, and one draw needn't show every extreme that they name: The first counts[b, j] slots of index j hold images; in every micro-batch some index holds an image and some holds none.
All inputs are finite; a program needn't handle non-finite values.
Results may differ from the reference program's by a relative error of at most 0.012.
The reference program's roundings to bfloat16 on the way count: a program that leaves them out, or rounds other values in their place, can miss the bound.
Values may be sent and summed in bfloat16 or wider, within the bound.
A program may use at most 192 MiB of HBM per device.

```python
import jax
import jax.numpy as jnp
from jax import lax

D = 1024
H = 16
HD = 64
FF = 4096
IMG_LEN = 577
PAD_LEN = 608
MB = 2
SLOTS = 1
IMAGES = 8
N_DP = 8
N_MP = 4


def draw_counts(key, part):
    base_counts = jnp.minimum(jax.random.randint(jax.random.fold_in(key, 11), (MB, N_DP), 0, SLOTS + 2), SLOTS)
    full_at = jax.random.randint(jax.random.fold_in(key, 12), (MB,), 0, N_DP)
    step_away = jax.random.randint(jax.random.fold_in(key, 13), (MB,), 0, N_DP - 1)
    empty_at = (full_at + 1 + step_away) % N_DP
    columns = jnp.arange(N_DP)[None, :]
    base_counts = jnp.where(columns == full_at[:, None], SLOTS, base_counts)
    base_counts = jnp.where(columns == empty_at[:, None], 0, base_counts)
    return base_counts.astype(jnp.int32)


def draw_query_weight(key, part):
    head_order = jax.random.permutation(jax.random.fold_in(key, 21), H)
    head_ratio = head_order.astype(jnp.float32) / jnp.float32(max(H - 1, 1))
    head_scale = 0.3 * jnp.exp(head_ratio * jnp.log(jnp.float32(2.0 / 0.3)))
    column_scale = jnp.repeat(head_scale, HD)
    entries = jnp.clip(jax.random.normal(jax.random.fold_in(key, 22), (D, D), jnp.float32), -6.0, 6.0)
    return (entries * jnp.float32(D ** (-0.5)) * column_scale[None, :]).astype(jnp.bfloat16)


def level_of(rng, dims, pieces, smallest, largest):
    level = 1.0
    for position, shards_of in pieces:
        draws = jax.random.uniform(jax.random.fold_in(jax.random.fold_in(rng, 6), position), (shards_of,), jnp.float32, smallest / len(pieces), largest / len(pieces))
        level = level * jnp.repeat(jnp.exp(draws), dims[position] // shards_of).reshape((-1,) + (1,) * (len(dims) - 1 - position))
    return level


def normal_values(own_key, extent, width, reach, pieces=(), held_as=jnp.bfloat16):
    values = jax.random.normal(own_key, extent, jnp.float32) * width
    if len(pieces) > 0:
        values = level_of(own_key, extent, pieces, -0.22, 0.18) * values
    return jnp.clip(values, min=-reach, max=reach).astype(held_as)


def setup_inputs(seed: int = 0) -> dict:
    key_list = jax.random.split(jax.random.key(seed), 20)
    return {
        "images": normal_values(key_list[0], (MB, IMAGES, PAD_LEN, D), 1.0, 6.0, ((1, 8), (2, 4))),
        "counts": draw_counts(jax.random.fold_in(key_list[19], 71), 0),
        "first_gain": jnp.clip(1.0 + 0.1 * jax.random.normal(key_list[2], (D,), jnp.float32), 0.5, 1.5).astype(jnp.bfloat16),
        "first_shift": normal_values(key_list[3], (D,), 0.3, 1.796875, ((0, 8),)),
        "query_weight": draw_query_weight(jax.random.fold_in(key_list[19], 71), 0),
        "query_bias": normal_values(key_list[5], (N_MP, D // N_MP), 0.5, 3.0, ((0, 4), (1, 8))),
        "key_weight": normal_values(key_list[6], (D, D), D ** -0.5, 0.1875, ((0, 8), (1, 4))),
        "value_weight": normal_values(key_list[7], (D, D), D ** -0.5, 0.1875, ((0, 8), (1, 4))),
        "value_bias": normal_values(key_list[8], (N_MP, D // N_MP), 0.5, 3.0, ((0, 4), (1, 8))),
        "out_weight": normal_values(key_list[9], (D, D), (D // 32) ** -0.5, 1.0, ((0, 8), (1, 4))),
        "out_bias": normal_values(key_list[10], (D,), 0.3, 1.796875, ((0, 8),)),
        "second_gain": jnp.clip(1.0 + 0.1 * jax.random.normal(key_list[11], (D,), jnp.float32), 0.5, 1.5).astype(jnp.bfloat16),
        "second_shift": normal_values(key_list[12], (D,), 0.3, 1.796875, ((0, 8),)),
        "up_weight": normal_values(key_list[13], (D, FF), D ** -0.5, 0.1875, ((0, 8), (1, 4))),
        "up_bias": normal_values(key_list[14], (N_MP, FF // N_MP), 0.5, 3.0, ((0, 4), (1, 8))),
        "down_weight": normal_values(key_list[15], (D, FF), FF ** -0.5, 0.09375, ((0, 8), (1, 4))),
        "down_bias": normal_values(key_list[16], (D,), 0.3, 1.796875, ((0, 8),)),
        "clip_tau": jnp.clip(jax.random.uniform(key_list[17], (), jnp.float32, 3.5, 5.5), 3.5, 5.5),
        "out_grad": normal_values(key_list[18], (MB, IMAGES, PAD_LEN, D), 1.0, 6.0, ((1, 8), (2, 4))),
    }


@jax.custom_vjp
def low(v):
    return lax.optimization_barrier(v.astype(jnp.bfloat16)).astype(jnp.float32)

@jax.custom_vjp
def low_back(v):
    return v

def low_keep(v):
    return (low(v), None)

def low_pass(kept, grad):
    return (grad,)

def back_keep(v):
    return (v, None)

def back_low(kept, grad):
    return (low(grad),)
low.defvjp(low_keep, low_pass)
low_back.defvjp(back_keep, back_low)

def matmul_high(left_side, right_side):
    return jnp.dot(left_side, right_side, precision=lax.Precision.HIGHEST)

def norm_rows(features, norm_gain, shift):
    center = features - lax.optimization_barrier(jnp.mean(features, axis=-1, keepdims=True))
    spread_sq = lax.optimization_barrier(jnp.mean(center * center, axis=-1, keepdims=True))
    return center * lax.rsqrt(spread_sq + 1e-05) * norm_gain + shift

def image_layer(params, picture_rows, live_flag):
    first_gain, first_shift, query_weight, query_bias, key_weight, value_weight, value_bias, out_weight, out_bias, second_gain, second_shift, up_weight, up_bias, down_weight, down_bias = params
    positions = jnp.arange(PAD_LEN)
    key_keep = positions < IMG_LEN
    row_keep = key_keep & live_flag
    normed_one = low(norm_rows(picture_rows, first_gain, first_shift))
    queries = low(low_back(matmul_high(normed_one, query_weight) + query_bias.reshape(-1)))
    key_rows = low(low_back(matmul_high(normed_one, key_weight)))
    value_rows = low(low_back(matmul_high(normed_one, value_weight) + value_bias.reshape(-1)))
    head_query = queries.reshape(PAD_LEN, H, HD)
    head_key = key_rows.reshape(PAD_LEN, H, HD)
    head_value = value_rows.reshape(PAD_LEN, H, HD)
    raw_scores = jnp.einsum('qhc,khc->hqk', head_query, head_key, precision=lax.Precision.HIGHEST) * HD ** (-0.5)
    scores = low_back(raw_scores)
    masked = jnp.where(key_keep[None, None, :], scores, -1e+30)
    probs = jax.nn.softmax(masked, axis=-1)
    mixed = jnp.einsum('hqk,khc->qhc', low(probs), head_value, precision=lax.Precision.HIGHEST).reshape(PAD_LEN, D)
    mixed = low(low_back(mixed))
    attended = low_back(matmul_high(mixed, out_weight.T) + out_bias)
    after_attention_rows = picture_rows + attended
    normed_two = low(norm_rows(after_attention_rows, second_gain, second_shift))
    hidden_pre = low_back(matmul_high(normed_two, up_weight) + up_bias.reshape(-1))
    activated = low(hidden_pre * jax.nn.sigmoid(1.702 * hidden_pre))
    projected = low_back(matmul_high(activated, down_weight.T) + down_bias)
    output_rows = row_keep.astype(jnp.float32)[:, None] * (after_attention_rows + projected)
    pair_keep = row_keep[:, None] & key_keep[None, :]
    peaks = lax.optimization_barrier(jnp.max(jnp.where(pair_keep[None], raw_scores, -1e+30), axis=(1, 2)))
    return (output_rows, peaks)

def add_pair(first_term, second_term):
    return first_term + second_term

def reference(images, counts, first_gain, first_shift, query_weight, query_bias, key_weight, value_weight, value_bias, out_weight, out_bias, second_gain, second_shift, up_weight, up_bias, down_weight, down_bias, clip_tau, out_grad):
    params = tuple((item.astype(jnp.float32) for item in (first_gain, first_shift, query_weight, query_bias, key_weight, value_weight, value_bias, out_weight, out_bias, second_gain, second_shift, up_weight, up_bias, down_weight, down_bias)))
    image_flat = images.astype(jnp.float32).reshape(MB * IMAGES, PAD_LEN, D)
    grad_flat = out_grad.astype(jnp.float32).reshape(MB * IMAGES, PAD_LEN, D)
    slot_index = jnp.arange(MB * IMAGES)
    micro_index = slot_index // IMAGES
    image_index = slot_index % IMAGES
    live_flags = image_index % SLOTS < counts[micro_index, image_index // SLOTS]

    def one_image(carry, item):
        grad_sums, peak_now = carry
        picture_rows, grad_rows, live_flag = item

        def layer_of(param_set, rows_in):
            return image_layer(param_set, rows_in, live_flag)
        output_rows, pull_back, peaks = jax.vjp(layer_of, params, picture_rows, has_aux=True)
        param_grads, rows_grad = pull_back(grad_rows)
        grad_sums = jax.tree.map(add_pair, grad_sums, param_grads)
        return ((grad_sums, jnp.maximum(peak_now, peaks)), (output_rows.astype(jnp.bfloat16), rows_grad.astype(jnp.bfloat16)))
    zero_grads = tuple((jnp.zeros_like(item) for item in params))
    start_peak = jnp.full((H,), -1e+30, jnp.float32)
    (grad_sums, peak_all), (outputs, input_grads) = lax.scan(one_image, (zero_grads, start_peak), (image_flat, grad_flat, live_flags))
    head_root = jnp.sqrt(clip_tau / jnp.maximum(peak_all, clip_tau))
    column_root = jnp.repeat(head_root, HD)
    clipped_query = params[2] * column_root[None, :]
    clipped_key = params[4] * column_root[None, :]
    clipped_bias = params[3] * column_root.reshape(N_MP, D // N_MP)
    return (outputs.reshape(MB, IMAGES, PAD_LEN, D), input_grads.reshape(MB, IMAGES, PAD_LEN, D), grad_sums[0], grad_sums[1], grad_sums[2], grad_sums[3], grad_sums[4], grad_sums[5], grad_sums[6], grad_sums[7], grad_sums[8], grad_sums[9], grad_sums[10], grad_sums[11], grad_sums[12], grad_sums[13], grad_sums[14], peak_all, clipped_query, clipped_key, clipped_bias)
```

```python
import functools
import math

import jax
import jax.numpy as jnp
from jax import lax
from jax.experimental import pallas as pl
from jax.experimental.pallas import tpu as pltpu
from jax.sharding import PartitionSpec as P

HD = 64
IMG_LEN = 577
F32 = jnp.float32
BF16 = jnp.bfloat16
MESH = pl.DeviceIdType.MESH
TILE = 256
PQ, PK, PV, PO = 0, 1, 2, 3
G1, S1, OB, G2, S2, DB, UB, QB, VB = 0, 1, 2, 3, 4, 5, 6, 8, 9
DG1, DS1, DOB, DG2, DS2, DDB, DUB, DQB, DVB, PEAK = 0, 1, 2, 3, 4, 5, 6, 7, 8, 9


def dot_nn(left, right):
    return lax.dot_general(left, right, (((1,), (0,)), ((), ())), preferred_element_type=F32)


def dot_nt(left, right):
    return lax.dot_general(left, right, (((1,), (1,)), ((), ())), preferred_element_type=F32)


def dot_tn(left, right):
    return lax.dot_general(left, right, (((0,), (0,)), ((), ())), preferred_element_type=F32)


def standardize(rows):
    center = rows - jnp.mean(rows, axis=-1, keepdims=True)
    inverse = lax.rsqrt(jnp.mean(center * center, axis=-1, keepdims=True) + 1e-05)
    return center * inverse, inverse


def norm_back(incoming, scaled, inverse, gain):
    upward = incoming * gain
    return inverse * (
        upward
        - jnp.mean(upward, axis=-1, keepdims=True)
        - scaled * jnp.mean(upward * scaled, axis=-1, keepdims=True)
    )


def each(low, high, body):
    if high - low <= 8:
        for at in range(low, high):
            body(at)
    else:

        def step(at, carry):
            body(at)
            return carry

        lax.fori_loop(low, high, step, 0)


def sum_rows(rows):
    return jnp.sum(rows, axis=0, keepdims=True)


class Layer:
    def __init__(self, size, refs):
        self.__dict__.update(size)
        self.__dict__.update(refs)
        self.dp_at = lax.axis_index("dp")
        self.mp_at = lax.axis_index("mp")
        self.line_at = self.dp_at // 2
        self.pair_at = lax.rem(self.dp_at, 2)
        self.chip_at = self.mp_at // 2
        self.core_at = lax.rem(self.mp_at, 2)
        self.sib = (self.dp_at, self.chip_at * 2 + 1 - self.core_at)
        self.across = (self.dp_at, (1 - self.chip_at) * 2 + self.core_at)
        self.pair = (self.line_at * 2 + 1 - self.pair_at, self.mp_at)
        self.stage_sends = [[], []]
        self.spread_sends = [[], [], [], []]
        self.late = []

    def line_of(self, step):
        return lax.rem(self.line_at + step + self.lines, self.lines)

    def line_peer(self, step):
        return (self.line_of(step) * 2 + self.pair_at, self.mp_at)

    def slot(self, line, pair):
        return pl.ds(pl.multiple_of((line * 2 + pair) * self.shard, self.shard), self.shard)

    def block(self, micro, chip, core):
        start = micro * self.rows + (chip * 2 + core) * self.pad
        return pl.ds(pl.multiple_of(start, 16), self.pad)

    def own_block(self, micro):
        return self.block(micro, self.chip_at, self.core_at)

    def source(self, piece):
        if piece < 4:
            return (self.query_w, self.key_w, self.value_w, self.out_w)[piece]
        which, chunk = (piece - 4) % 2, (piece - 4) // 2
        return (self.up_w, self.down_w)[which].at[:, pl.ds(chunk * TILE, TILE)]

    def copy(self, src, dst, send_sem, recv_sem, device):
        return pltpu.make_async_remote_copy(
            src_ref=src,
            dst_ref=dst,
            send_sem=send_sem,
            recv_sem=recv_sem,
            device_id=device,
            device_id_type=MESH,
        )

    def weight_line(self, piece, step):
        return self.copy(
            self.source(piece),
            self.weights.at[piece, self.slot(self.line_at, self.pair_at)],
            self.wz_send.at[piece, step - 1],
            self.wz_recv.at[piece, step - 1],
            self.line_peer(step),
        )

    def weight_line_in(self, piece, step):
        place = self.weights.at[piece, self.slot(self.line_of(-step), self.pair_at)]
        return self.copy(
            place,
            place,
            self.wz_send.at[piece, step - 1],
            self.wz_recv.at[piece, step - 1],
            self.line_peer(-step),
        )

    def weight_pair(self, piece, step, own):
        place = self.weights.at[piece, self.slot(self.line_of(-step), self.pair_at)]
        return self.copy(
            self.source(piece) if own else place,
            place,
            self.wx_send.at[piece, step],
            self.wx_recv.at[piece, step],
            self.pair,
        )

    def weight_pair_in(self, piece, step):
        place = self.weights.at[piece, self.slot(self.line_of(-step), 1 - self.pair_at)]
        return self.copy(
            place, place, self.wx_send.at[piece, step], self.wx_recv.at[piece, step], self.pair
        )

    def weight_local(self, piece):
        return pltpu.make_async_copy(
            self.source(piece),
            self.weights.at[piece, self.slot(self.line_at, self.pair_at)],
            self.wl_sem.at[piece],
        )

    def send_weight(self, piece):
        self.weight_pair(piece, 0, True).start()
        each(1, self.lines, lambda step: self.weight_line(piece, step).start())
        self.weight_local(piece).start()

    def pass_weight(self, piece):
        def one(step):
            self.weight_line_in(piece, step).wait_recv()
            self.weight_pair(piece, step, False).start()

        each(1, self.lines, one)

    def await_weight(self, piece):
        self.weight_local(piece).wait()
        each(0, self.lines, lambda step: self.weight_pair_in(piece, step).wait_recv())

    def spread_copy(self, kind, micro, ref, which):
        place = ref.at[self.own_block(micro)]
        if which == 2:
            place = ref.at[self.block(micro, 1 - self.chip_at, self.core_at)]
        return self.copy(
            place,
            place,
            self.ag_send.at[kind, micro, which],
            self.ag_recv.at[kind, micro, which],
            self.across if which == 0 else self.sib,
        )

    def spread_in(self, kind, micro, ref, which):
        chip = self.chip_at if which == 1 else 1 - self.chip_at
        core = self.core_at if which == 0 else 1 - self.core_at
        place = ref.at[self.block(micro, chip, core)]
        return self.copy(
            place,
            place,
            self.ag_send.at[kind, micro, which],
            self.ag_recv.at[kind, micro, which],
            self.across if which == 0 else self.sib,
        )

    def spread(self, kind, micro, ref):
        for which in (0, 1):
            one = self.spread_copy(kind, micro, ref, which)
            one.start()
            self.spread_sends[kind].append(one)

    def spread_on(self, kind, micro, ref):
        self.spread_in(kind, micro, ref, 0).wait_recv()
        one = self.spread_copy(kind, micro, ref, 2)
        one.start()
        self.spread_sends[kind].append(one)

    def spread_sent(self, kind):
        for one in self.spread_sends[kind]:
            one.wait_send()
        self.spread_sends[kind] = []

    def spread_end(self, kind, micro, ref):
        self.spread_in(kind, micro, ref, 1).wait_recv()
        self.spread_in(kind, micro, ref, 2).wait_recv()

    def collect(self, kind, micro, terms):
        for one in self.stage_sends[micro]:
            one.wait_send()
        self.stage_sends[micro] = []
        stage, keep = self.stage, self.keep_own.at[1 if kind == 1 else 0, micro]

        def fill(ref, at, chip, core):
            def step(tile, carry):
                cols = pl.ds(pl.multiple_of(tile * TILE, TILE), TILE)
                product = terms(self.block(micro, chip, core), cols)
                ref[at + (slice(None), cols)] = product.astype(ref.dtype)
                return carry

            lax.fori_loop(0, self.width // TILE, step, 0)

        for half in (0, 1):
            chip = 1 - self.chip_at if half == 0 else self.chip_at
            fill(stage, (micro, half), chip, 1 - self.core_at)
            one = self.copy(
                stage.at[micro, half],
                self.sib_in.at[kind, micro, half],
                self.rs_send.at[kind, micro, half],
                self.rs_recv.at[kind, micro, half],
                self.sib,
            )
            one.start()
            self.stage_sends[micro].append(one)
            if half == 0:
                fill(self.keep_far, (), chip, self.core_at)
        incoming = self.sib_in.at[kind, micro, 0]
        self.copy(
            stage.at[micro, 0],
            incoming,
            self.rs_send.at[kind, micro, 0],
            self.rs_recv.at[kind, micro, 0],
            self.sib,
        ).wait_recv()
        incoming[...] = (self.keep_far[...] + incoming[...].astype(F32)).astype(BF16)
        one = self.copy(
            incoming,
            self.far_in.at[kind, micro],
            self.rs_send.at[kind, micro, 2],
            self.rs_recv.at[kind, micro, 2],
            self.across,
        )
        one.start()
        self.late.append(one)
        fill(keep, (), self.chip_at, self.core_at)

    def collected(self, kind, micro):
        near, far = self.sib_in.at[kind, micro, 1], self.far_in.at[kind, micro]
        self.copy(
            near, near, self.rs_send.at[kind, micro, 1], self.rs_recv.at[kind, micro, 1], self.sib
        ).wait_recv()
        self.copy(
            far, far, self.rs_send.at[kind, micro, 2], self.rs_recv.at[kind, micro, 2], self.across
        ).wait_recv()
        total = self.keep_own[1 if kind == 1 else 0, micro] + near[...].astype(F32)
        return (total + far[...].astype(F32))[: self.part]

    def summed(self, piece):
        return self.weights.at[piece] if piece < 4 else self.wide_sums.at[piece - 4]

    def grad_pair(self, piece, line):
        return self.copy(
            self.summed(piece).at[self.slot(line, 1 - self.pair_at)],
            self.pair_in.at[piece, line],
            self.gx_send.at[piece, line],
            self.gx_recv.at[piece, line],
            self.pair,
        )

    def grad_line(self, piece, step):
        return self.copy(
            self.pair_in.at[piece, self.line_of(step)],
            self.line_in.at[piece, step - 1],
            self.gz_send.at[piece, step - 1],
            self.gz_recv.at[piece, step - 1],
            self.line_peer(step),
        )

    def grad_start(self, piece, left, right):
        out = self.summed(piece)
        lines_in_tile = TILE // (2 * self.shard)

        def step(tile, carry):
            cols = pl.ds(pl.multiple_of(tile * TILE, TILE), TILE)
            out[cols, :] = dot_tn(left[:, cols], right).astype(BF16)
            for at in range(lines_in_tile):
                self.grad_pair(piece, tile * lines_in_tile + at).start()
            return carry

        lax.fori_loop(0, self.width // TILE, step, 0)

    def grad_pass(self, piece):
        def one(step):
            line = self.line_of(step)
            self.grad_pair(piece, line).wait_recv()
            mine = self.summed(piece)[self.slot(line, self.pair_at), :].astype(F32)
            mine = mine + self.pair_in[piece, line].astype(F32)
            self.pair_in[piece, line] = mine.astype(BF16)
            self.grad_line(piece, step).start()

        each(1, self.lines, one)

    def grad_end(self, piece):
        self.grad_pair(piece, self.line_at).wait_recv()
        total = self.summed(piece)[self.slot(self.line_at, self.pair_at), :].astype(F32)
        total = total + self.pair_in[piece, self.line_at].astype(F32)
        for step in range(1, self.lines):
            self.grad_line(piece, step).wait_recv()
            total = total + self.line_in[piece, step - 1].astype(F32)
        if piece < 4:
            (self.query_g, self.key_g, self.value_g, self.out_g)[piece][...] = total
        else:
            which, chunk = (piece - 4) % 2, (piece - 4) // 2
            (self.up_g, self.down_g)[which][:, chunk * TILE : (chunk + 1) * TILE] = total

    def vector_copy(self, step):
        return self.copy(
            self.packed,
            self.vectors_in.at[self.dp_at],
            self.v_send.at[0, step - 1],
            self.v_recv.at[0, step - 1],
            (lax.rem(self.dp_at + step, self.dps), self.mp_at),
        )

    def vector_copy_in(self, step):
        origin = lax.rem(self.dp_at - step + self.dps, self.dps)
        place = self.vectors_in.at[origin]
        return self.copy(
            place,
            place,
            self.v_send.at[0, step - 1],
            self.v_recv.at[0, step - 1],
            (origin, self.mp_at),
        )

    def share_copy(self, step):
        target = lax.rem(self.dp_at + step, self.dps)
        return self.copy(
            self.shares.at[target],
            self.shares_in.at[step - 1],
            self.v_send.at[1, step - 1],
            self.v_recv.at[1, step - 1],
            (target, self.mp_at),
        )

    def group_copy(self, step):
        return self.copy(
            self.group.at[0],
            self.group.at[step],
            self.m_send.at[step - 1],
            self.m_recv.at[step - 1],
            (self.dp_at, lax.rem(self.mp_at + step, 4)),
        )

    def take_vectors(self):
        if not self.own_vectors:
            self.vectors[...] = self.packed[...]
            return
        self.vectors_in[self.dp_at] = self.packed[...]
        for step in range(1, self.dps):
            self.vector_copy_in(step).wait_recv()
        rest = self.vectors_in[0, 8:16, :]
        for at in range(1, self.dps):
            rest = rest + self.vectors_in[at, 8:16, :]
        for at in range(self.dps):
            self.vectors[0:8, at * 128 : (at + 1) * 128] = self.vectors_in[at, 0:8, :]
        for row, first in ((QB, 0), (VB, 2)):
            self.vectors[row : row + 1, 0:128] = rest[first : first + 1]
            self.vectors[row : row + 1, 128:256] = rest[first + 1 : first + 2]

    def give_vectors(self):
        if not self.own_vectors:
            self.vector_g[...] = self.sums[...]
            return
        for at in range(self.dps):
            half = (at * 32 // 128) * 128
            self.shares[at, 0:7, :] = self.sums[0:7, at * 128 : (at + 1) * 128]
            self.shares[at, 7:9, :] = self.sums[7:9, half : half + 128]
            self.shares[at, 9:16, :] = self.sums[9:16, 0:128]
        for step in range(1, self.dps):
            self.share_copy(step).start()

    def end_vectors(self):
        if not self.own_vectors:
            return
        total = self.shares[self.dp_at]
        most = total[PEAK : PEAK + 1]
        for step in range(1, self.dps):
            self.share_copy(step).wait_recv()
            came = self.shares_in[step - 1]
            total = total + came
            most = jnp.maximum(most, came[PEAK : PEAK + 1])
        self.group[0] = total
        for step in range(1, 4):
            self.group_copy(step).start()
        whole = total[0:6]
        for step in range(1, 4):
            self.group_copy(step).wait_recv()
            whole = whole + self.group[step, 0:6, :]
        self.vector_g[0:6, :] = whole
        self.vector_g[6:9, :] = total[6:9]
        self.vector_g[9:10, :] = most
        self.vector_g[10:16, :] = jnp.zeros((6, 128), F32)

    def vector(self, row, start=0, size=None):
        size = self.width if size is None else size
        return self.vectors[row : row + 1, pl.ds(start, size)]

    def add_sum(self, row, value, start=0):
        cols = pl.ds(start, value.shape[1])
        self.sums[row : row + 1, cols] = self.sums[row : row + 1, cols] + value

    def mask(self, micro):
        row = self.mp_at * self.part + lax.broadcasted_iota(jnp.int32, (self.part, 1), 0)
        live = jnp.where(self.counts[micro, 0] > 0, 1.0, 0.0).astype(F32)
        return jnp.where(row < IMG_LEN, live, 0.0)

    def put_rows(self, ref, micro, rows):
        filler = jnp.zeros((self.pad - self.part, self.width), F32)
        ref[self.own_block(micro), :] = jnp.concatenate([rows, filler], axis=0).astype(BF16)

    def first_norm(self, micro):
        scaled, _ = standardize(self.images[micro, 0].astype(F32))
        self.put_rows(self.normed_one, micro, scaled * self.vector(G1) + self.vector(S1))
        self.spread(0, micro, self.normed_one)

    def out_rows(self, micro):
        return self.out_grad[micro, 0].astype(F32) * self.mask(micro)

    def project_back(self, micro):
        rows = self.out_rows(micro)
        self.put_rows(self.proj_back, micro, rows)
        self.add_sum(DDB, sum_rows(rows.astype(BF16).astype(F32)))
        self.spread(2, micro, self.proj_back)

    def second_norm(self, micro):
        rows = self.images[micro, 0].astype(F32) + self.collected(0, micro) + self.vector(OB)
        self.after_attn[micro] = rows
        scaled, _ = standardize(rows)
        self.put_rows(self.normed_two, micro, scaled * self.vector(G2) + self.vector(S2))
        self.spread(1, micro, self.normed_two)

    def give_result(self, micro):
        rows = self.after_attn[micro] + self.collected(1, micro) + self.vector(DB)
        self.result[micro, 0] = (self.mask(micro) * rows).astype(BF16)

    def second_norm_back(self, micro):
        incoming = self.collected(2, micro)
        scaled, inverse = standardize(self.after_attn[micro])
        rows = self.out_rows(micro) + norm_back(incoming, scaled, inverse, self.vector(G2))
        self.attn_back[micro] = rows
        self.add_sum(DOB, sum_rows(rows.astype(BF16).astype(F32)))
        self.add_sum(DG2, sum_rows(incoming * scaled))
        self.add_sum(DS2, sum_rows(incoming))
        self.put_rows(self.attended_back, micro, rows)
        self.spread(3, micro, self.attended_back)

    def first_norm_back(self, micro):
        incoming = self.collected(3, micro)
        scaled, inverse = standardize(self.images[micro, 0].astype(F32))
        self.add_sum(DG1, sum_rows(incoming * scaled))
        self.add_sum(DS1, sum_rows(incoming))
        rows = self.attn_back[micro] + norm_back(incoming, scaled, inverse, self.vector(G1))
        self.input_grad[micro, 0] = rows.astype(BF16)

    def image_rows(self, micro):
        return pl.ds(micro * self.rows, self.rows)

    def counted(self, axis):
        shape = (self.rows, 1) if axis == 0 else (1, self.rows)
        row = lax.broadcasted_iota(jnp.int32, shape, axis)
        block = row // self.pad
        inside = row - block * self.pad
        return (inside < self.part) & (block * self.part + inside < IMG_LEN)

    def head_columns(self, head):
        column = lax.broadcasted_iota(jnp.int32, (self.rows, TILE), 1)
        return column // HD == head

    def project_heads(self, micro):
        rows = self.image_rows(micro)
        normed = self.normed_one[rows, :]
        scale = 1.0 / math.sqrt(HD)
        query = dot_nn(normed, self.weights[PQ]) + self.vector(QB, 0, TILE)
        self.queries[rows, :] = (query.astype(BF16).astype(F32) * scale).astype(BF16)
        self.keys[rows, :] = dot_nn(normed, self.weights[PK]).astype(BF16)
        value = dot_nn(normed, self.weights[PV]) + self.vector(VB, 0, TILE)
        self.values[rows, :] = value.astype(BF16)

    def attend(self, micro):
        rows = self.image_rows(micro)
        self.turned[...] = self.values[rows, :].T
        live = jnp.where(self.counts[micro, 0] > 0, 0.0, -1e30).astype(F32)

        def one_head(head, carry):
            query = jnp.where(self.head_columns(head), self.queries[rows, :], jnp.zeros((), BF16))
            scores = dot_nt(self.keys[rows, :], query)
            scores = jnp.where(self.counted(0), scores, -1e30)
            top = jnp.max(scores, axis=0, keepdims=True)
            expo = jnp.exp(scores - top)
            total = jnp.sum(expo, axis=0, keepdims=True)
            self.log_total[micro, head] = top + jnp.log(total)
            cols = pl.ds(pl.multiple_of(head * HD, HD), HD)
            mixed = dot_nn(self.turned[cols, :], expo.astype(BF16))
            self.mixed_turned[micro, cols, :] = mixed * (1.0 / total)
            peak = jnp.max(jnp.where(self.counted(1), top, -1e30), axis=1, keepdims=True)
            peak = jnp.where(live < 0.0, -1e30, peak)
            lane = lax.broadcasted_iota(jnp.int32, (1, 128), 1)
            seen = self.sums[PEAK : PEAK + 1, 0:128]
            self.sums[PEAK : PEAK + 1, 0:128] = jnp.where(
                lane == head, jnp.maximum(seen, peak), seen
            )
            return carry

        lax.fori_loop(0, self.heads, one_head, 0)
        self.mixed[rows, :] = self.mixed_turned[micro].T.astype(BF16)

    def attend_back(self, micro):
        rows = self.image_rows(micro)
        self.mixed_back[...] = dot_nn(self.attended_back[rows, :], self.weights[PO]).astype(BF16)
        self.turned[...] = self.keys[rows, :].T
        self.mixed_back_turned[...] = self.mixed_back[...].T
        self.key_sum[...] = jnp.zeros_like(self.key_sum)
        self.value_sum[...] = jnp.zeros_like(self.value_sum)
        chunk = self.rows // 2

        def one_head(head, carry):
            columns = self.head_columns(head)
            none = jnp.zeros((), BF16)
            query = jnp.where(columns, self.queries[rows, :], none)
            outward = jnp.where(columns, self.mixed_back[...], none)
            cols = pl.ds(pl.multiple_of(head * HD, HD), HD)
            dots = self.mixed_back_turned[cols, :].astype(F32) * self.mixed_turned[micro, cols, :]
            delta = jnp.sum(dots, axis=0, keepdims=True)
            log_total = self.log_total[micro, head]
            for at in range(2):
                part = pl.ds(micro * self.rows + at * chunk, chunk)
                here = pl.ds(at * chunk, chunk)
                scores = dot_nt(self.keys[part, :], query)
                counted = self.counted(0)[at * chunk : (at + 1) * chunk]
                probs = jnp.where(counted, jnp.exp(scores - log_total), 0.0)
                prob_back = dot_nt(self.values[part, :], outward)
                self.probs[here, :] = probs.astype(BF16)
                self.score_back[here, :] = (probs * (prob_back - delta)).astype(BF16)
            self.value_sum[...] += dot_nn(self.probs[...], outward)
            self.key_sum[...] += dot_nn(self.score_back[...], query)
            self.query_turned[cols, :] = dot_nn(self.turned[cols, :], self.score_back[...])
            return carry

        lax.fori_loop(0, self.heads, one_head, 0)
        scale = 1.0 / math.sqrt(HD)
        query_back = (self.query_turned[...] * scale).T.astype(BF16)
        value_back = self.value_sum[...].astype(BF16)
        self.queries[rows, :] = query_back
        self.keys[rows, :] = self.key_sum[...].astype(BF16)
        self.values[rows, :] = value_back
        self.add_sum(DQB, sum_rows(query_back.astype(F32)))
        self.add_sum(DVB, sum_rows(value_back.astype(F32)))

    def feed(self, micro, chunk):
        cols = pl.ds(chunk * TILE, TILE)
        up, down = self.weights.at[4 + 2 * chunk], self.weights.at[5 + 2 * chunk]
        part = self.rows // 2
        total = jnp.zeros((1, TILE), F32)
        for at in range(2):
            rows = pl.ds(micro * self.rows + at * part, part)
            hidden = dot_nn(self.normed_two[rows, :], up[...])
            hidden = hidden + self.vector(UB, chunk * TILE, TILE)
            gate = jax.nn.sigmoid(1.702 * hidden)
            self.activated[rows, cols] = (hidden * gate).astype(BF16)
            back = dot_nn(self.proj_back[rows, :], down[...])
            back = back * (gate + 1.702 * hidden * gate * (1.0 - gate))
            back = back.astype(BF16)
            self.pre_back[rows, cols] = back
            total = total + sum_rows(back.astype(F32))
        self.add_sum(DUB, total, chunk * TILE)

    def out_terms(self, rows, cols):
        return dot_nt(self.mixed[rows, :], self.weights[PO, cols, :])

    def wide_terms(self, ref, first):
        def terms(rows, cols):
            total = None
            for chunk in range(self.chunks):
                one = dot_nt(
                    ref[rows, chunk * TILE : (chunk + 1) * TILE],
                    self.weights[first + 2 * chunk, cols, :],
                )
                total = one if total is None else total + one
            return total

        return terms

    def input_terms(self, rows, cols):
        total = dot_nt(self.queries[rows, :], self.weights[PQ, cols, :])
        total = total + dot_nt(self.keys[rows, :], self.weights[PK, cols, :])
        return total + dot_nt(self.values[rows, :], self.weights[PV, cols, :])

    def enter(self):
        barrier = pltpu.get_barrier_semaphore()
        peers = [self.sib, self.across]
        if self.own_vectors:
            peers.append((self.dp_at, (1 - self.chip_at) * 2 + 1 - self.core_at))
        for peer in peers:
            pl.semaphore_signal(barrier, inc=1, device_id=peer, device_id_type=MESH)
        if self.own_vectors:

            def hail(step):
                peer = (lax.rem(self.dp_at + step, self.dps), self.mp_at)
                pl.semaphore_signal(barrier, inc=1, device_id=peer, device_id_type=MESH)

            each(1, self.dps, hail)
            pl.semaphore_wait(barrier, 3 + self.dps - 1)
        else:
            pl.semaphore_signal(barrier, inc=1, device_id=self.pair, device_id_type=MESH)

            def hail(step):
                peer = self.line_peer(step)
                pl.semaphore_signal(barrier, inc=1, device_id=peer, device_id_type=MESH)

            each(1, self.lines, hail)
            pl.semaphore_wait(barrier, 2 + self.lines)

    def run(self):
        pieces = 4 + 2 * self.chunks
        self.enter()
        if self.own_vectors:
            for step in range(1, self.dps):
                self.vector_copy(step).start()
        for piece in range(4):
            self.send_weight(piece)
        self.sums[...] = jnp.zeros_like(self.sums)
        self.sums[PEAK : PEAK + 1, :] = jnp.full((1, self.width), -1e30, F32)
        self.take_vectors()
        for micro in (0, 1):
            self.first_norm(micro)
        for micro in (0, 1):
            self.project_back(micro)
        for piece in range(3):
            self.pass_weight(piece)
        for piece in range(4, pieces):
            self.send_weight(piece)
        for micro in (0, 1):
            self.spread_on(0, micro, self.normed_one)
        self.pass_weight(3)
        for piece in range(3):
            self.await_weight(piece)
        waiting = list(range(4, pieces))
        for micro in (0, 1):
            self.spread_end(0, micro, self.normed_one)
            self.project_heads(micro)
            self.attend(micro)
            if micro == 0:
                self.await_weight(PO)
            else:
                self.second_norm(0)
            self.collect(0, micro, self.out_terms)
            self.spread_on(2, micro, self.proj_back)
            self.pass_weight(waiting.pop(0))
        self.spread_on(1, 0, self.normed_two)
        self.second_norm(1)
        self.pass_weight(waiting.pop(0))
        self.pass_weight(waiting.pop(0))
        self.spread_on(1, 1, self.normed_two)
        for micro in (0, 1):
            self.spread_end(1, micro, self.normed_two)
            self.spread_end(2, micro, self.proj_back)
        for chunk in range(self.chunks):
            up, down = 4 + 2 * chunk, 5 + 2 * chunk
            self.await_weight(up)
            self.await_weight(down)
            for micro in (0, 1):
                self.feed(micro, chunk)
            cols = slice(chunk * TILE, (chunk + 1) * TILE)
            self.grad_start(up, self.normed_two, self.pre_back[:, cols])
            self.grad_start(down, self.proj_back, self.activated[:, cols])
            for _ in range(2):
                if waiting:
                    self.pass_weight(waiting.pop(0))
            if chunk:
                self.grad_pass(up - 2)
                self.grad_pass(down - 2)
        self.spread_sent(1)
        for micro in (0, 1):
            self.collect(2, micro, self.wide_terms(self.pre_back, 4))
        self.grad_pass(pieces - 2)
        self.grad_pass(pieces - 1)
        for micro in (0, 1):
            self.collect(1, micro, self.wide_terms(self.activated, 5))
            self.second_norm_back(micro)
        for micro in (0, 1):
            self.spread_on(3, micro, self.attended_back)
            self.spread_end(3, micro, self.attended_back)
            self.attend_back(micro)
            self.collect(3, micro, self.input_terms)
        for piece in range(4):
            each(1, self.lines, lambda step: self.weight_pair(piece, step, False).wait_send())
        self.grad_start(PO, self.attended_back, self.mixed[...])
        self.grad_start(PQ, self.normed_one, self.queries[...])
        self.grad_start(PK, self.normed_one, self.keys[...])
        self.grad_start(PV, self.normed_one, self.values[...])
        for micro in (0, 1):
            self.first_norm_back(micro)
        self.give_vectors()
        for piece in (PO, PQ, PK, PV):
            self.grad_pass(piece)
        for micro in (0, 1):
            self.give_result(micro)
        for piece in range(4, pieces):
            self.grad_end(piece)
        self.end_vectors()
        for piece in (PO, PQ, PK, PV):
            self.grad_end(piece)
        for kind in (0, 2, 3):
            self.spread_sent(kind)
        for one in self.late + self.stage_sends[0] + self.stage_sends[1]:
            one.wait_send()
        for piece in range(pieces):
            self.weight_pair(piece, 0, True).wait_send()
            each(1, self.lines, lambda step: self.weight_line(piece, step).wait_send())
            if piece >= 4:
                each(1, self.lines, lambda step: self.weight_pair(piece, step, False).wait_send())
            each(0, self.lines, lambda line: self.grad_pair(piece, line).wait_send())
            each(1, self.lines, lambda step: self.grad_line(piece, step).wait_send())
        if self.own_vectors:
            for step in range(1, self.dps):
                self.vector_copy(step).wait_send()
                self.share_copy(step).wait_send()
            for step in range(1, 4):
                self.group_copy(step).wait_send()


def layer_kernel(size, names, *refs):
    named = dict(zip(names, refs))
    named["attended_back"] = named["normed_two"]
    Layer(size, named).run()


def fused_layer(size, counts, images, out_grad, packed, weights):
    width, shard, part, rows, pad = (size[key] for key in ("width", "shard", "part", "rows", "pad"))
    lines, dps, pieces = size["lines"], size["dps"], 4 + 2 * size["chunks"]
    units = size["chunks"] * TILE
    vmem = pl.BlockSpec(memory_space=pltpu.VMEM)
    anywhere = pl.BlockSpec(memory_space=pl.ANY)
    vector_shape = (16, 128) if size["own_vectors"] else (16, width)
    outputs = {
        "result": (images.shape, BF16),
        "input_grad": (images.shape, BF16),
        "query_g": ((shard, TILE), F32),
        "key_g": ((shard, TILE), F32),
        "value_g": ((shard, TILE), F32),
        "out_g": ((shard, TILE), F32),
        "up_g": ((shard, units), F32),
        "down_g": ((shard, units), F32),
        "vector_g": (vector_shape, F32),
    }
    dma = pltpu.SemaphoreType.DMA
    vm = pltpu.VMEM
    scratch = {
        "weights": vm((pieces, width, TILE), BF16),
        "normed_one": vm((2 * rows, width), BF16),
        "normed_two": vm((2 * rows, width), BF16),
        "proj_back": vm((2 * rows, width), BF16),
        "queries": vm((2 * rows, TILE), BF16),
        "keys": vm((2 * rows, TILE), BF16),
        "values": vm((2 * rows, TILE), BF16),
        "mixed": vm((2 * rows, TILE), BF16),
        "mixed_turned": vm((2, TILE, rows), F32),
        "log_total": vm((2, size["heads"], 1, rows), F32),
        "activated": vm((2 * rows, units), BF16),
        "pre_back": vm((2 * rows, units), BF16),
        "turned": vm((TILE, rows), BF16),
        "mixed_back": vm((rows, TILE), BF16),
        "mixed_back_turned": vm((TILE, rows), BF16),
        "query_turned": vm((TILE, rows), F32),
        "key_sum": vm((rows, TILE), F32),
        "value_sum": vm((rows, TILE), F32),
        "probs": vm((rows, rows), BF16),
        "score_back": vm((rows, rows), BF16),
        "stage": vm((2, 2, pad, width), BF16),
        "keep_far": vm((pad, width), F32),
        "keep_own": vm((2, 2, pad, width), F32),
        "sib_in": vm((4, 2, 2, pad, width), BF16),
        "far_in": vm((4, 2, pad, width), BF16),
        "after_attn": vm((2, part, width), F32),
        "attn_back": vm((2, part, width), F32),
        "wide_sums": vm((pieces - 4, width, TILE), BF16),
        "pair_in": vm((pieces, lines, shard, TILE), BF16),
        "line_in": vm((pieces, lines - 1, shard, TILE), BF16),
        "vectors": vm((16, width), F32),
        "sums": vm((16, width), F32),
        "wz_send": dma((pieces, lines - 1)),
        "wz_recv": dma((pieces, lines - 1)),
        "wx_send": dma((pieces, lines)),
        "wx_recv": dma((pieces, lines)),
        "wl_sem": dma((pieces,)),
        "ag_send": dma((4, 2, 3)),
        "ag_recv": dma((4, 2, 3)),
        "rs_send": dma((4, 2, 3)),
        "rs_recv": dma((4, 2, 3)),
        "gx_send": dma((pieces, lines)),
        "gx_recv": dma((pieces, lines)),
        "gz_send": dma((pieces, lines - 1)),
        "gz_recv": dma((pieces, lines - 1)),
    }
    if size["own_vectors"]:
        scratch |= {
            "vectors_in": vm((dps, 16, 128), F32),
            "shares": vm((dps, 16, 128), F32),
            "shares_in": vm((dps - 1, 16, 128), F32),
            "group": vm((4, 16, 128), F32),
            "v_send": dma((2, dps - 1)),
            "v_recv": dma((2, dps - 1)),
            "m_send": dma((3,)),
            "m_recv": dma((3,)),
        }
    inputs = ["counts", "images", "out_grad", "packed"]
    inputs += ["query_w", "key_w", "value_w", "out_w", "up_w", "down_w"]
    names = inputs + list(outputs) + list(scratch)
    return pl.pallas_call(
        functools.partial(layer_kernel, size, names),
        out_shape=[jax.ShapeDtypeStruct(*spec) for spec in outputs.values()],
        in_specs=[pl.BlockSpec(memory_space=pltpu.SMEM)] + [vmem] * 3 + [anywhere] * 6,
        out_specs=[vmem] * len(outputs),
        scratch_shapes=list(scratch.values()),
        compiler_params=pltpu.CompilerParams(
            collective_id=0, has_side_effects=True, vmem_limit_bytes=63 * 2**20
        ),
    )(counts, images, out_grad, packed, *weights)


def on_device(
    images,
    counts,
    first_gain,
    first_shift,
    query_weight,
    query_bias,
    key_weight,
    value_weight,
    value_bias,
    out_weight,
    out_bias,
    second_gain,
    second_shift,
    up_weight,
    up_bias,
    down_weight,
    down_bias,
    clip_tau,
    out_grad,
):
    part, width = images.shape[2:]
    dps = lax.axis_size("dp")
    dp_at = lax.axis_index("dp")
    shard = query_weight.shape[0]
    pad = (part + 15) // 16 * 16
    size = {
        "width": width,
        "shard": shard,
        "part": part,
        "pad": pad,
        "rows": pad * lax.axis_size("mp"),
        "dps": dps,
        "lines": dps // 2,
        "heads": query_weight.shape[1] // HD,
        "chunks": up_weight.shape[1] // TILE,
        "own_vectors": shard == 128,
    }
    bias_cols = query_bias.shape[1]
    parts = [first_gain, first_shift, out_bias, second_gain, second_shift, down_bias, up_bias[0]]
    if size["own_vectors"]:
        place = jnp.zeros((2, TILE), F32)
        biases = jnp.concatenate([query_bias, value_bias]).astype(F32)
        place = lax.dynamic_update_slice(place, biases, (0, dp_at * bias_cols))
        packed = jnp.concatenate(
            [
                jnp.stack(parts).astype(F32),
                jnp.zeros((1, 128), F32),
                place.reshape(4, 128),
                jnp.zeros((4, 128), F32),
            ]
        )
    else:
        whole = [lax.all_gather(one, "dp", axis=0, tiled=True) for one in parts]
        rest = [
            jnp.pad(lax.all_gather(one[0], "dp", axis=0, tiled=True), (0, width - TILE))
            for one in (query_bias, value_bias)
        ]
        filler = jnp.zeros((width,), BF16)
        packed = jnp.stack(whole + [filler] + rest + [filler] * 6).astype(F32)
    weights = (query_weight, key_weight, value_weight, out_weight, up_weight, down_weight)
    outs = fused_layer(size, counts, images, out_grad, packed, weights)
    result, input_grad, query_g, key_g, value_g, out_g, up_g, down_g, vector_g = outs
    if size["own_vectors"]:
        vectors = [vector_g[row] for row in range(7)]
        start = lax.rem(dp_at * bias_cols, 128)
        query_bias_g = lax.dynamic_slice(vector_g, (DQB, start), (1, bias_cols))
        value_bias_g = lax.dynamic_slice(vector_g, (DVB, start), (1, bias_cols))
        peaks = vector_g[PEAK, : size["heads"]]
    else:
        mine = vector_g[:DUB]
        mine = lax.psum(mine, "mp")
        mine = lax.psum_scatter(mine, "dp", scatter_dimension=1, tiled=True)
        up_bias_g = lax.psum_scatter(vector_g[DUB], "dp", scatter_dimension=0, tiled=True)
        vectors = [mine[row] for row in range(6)] + [up_bias_g]
        both = vector_g[DQB : DVB + 1, :TILE]
        both = lax.psum_scatter(both, "dp", scatter_dimension=1, tiled=True)
        query_bias_g, value_bias_g = both[0:1], both[1:2]
        peaks = lax.pmax(vector_g[PEAK, : size["heads"]], "dp")
    head_root = jnp.sqrt(clip_tau / jnp.maximum(peaks, clip_tau))
    column_root = jnp.repeat(head_root, HD)
    clipped_query = query_weight.astype(F32) * column_root[None, :]
    clipped_key = key_weight.astype(F32) * column_root[None, :]
    bias_root = lax.dynamic_slice(column_root, (dp_at * bias_cols,), (bias_cols,))
    clipped_bias = query_bias.astype(F32) * bias_root[None, :]
    return (
        result,
        input_grad,
        vectors[DG1],
        vectors[DS1],
        query_g,
        query_bias_g,
        key_g,
        value_g,
        value_bias_g,
        out_g,
        vectors[DOB],
        vectors[DG2],
        vectors[DS2],
        up_g,
        vectors[DUB][None, :],
        down_g,
        vectors[DDB],
        peaks,
        clipped_query,
        clipped_key,
        clipped_bias,
    )


def solution(mesh):
    rows = P(None, "dp", "mp", None)
    wide, small, bias = P("dp", "mp"), P("dp"), P("mp", "dp")
    return jax.shard_map(
        on_device,
        mesh=mesh,
        in_specs=(
            rows,
            P(None, "dp"),
            small,
            small,
            wide,
            bias,
            wide,
            wide,
            bias,
            wide,
            small,
            small,
            small,
            wide,
            bias,
            wide,
            small,
            P(),
            rows,
        ),
        out_specs=(
            rows,
            rows,
            small,
            small,
            wide,
            bias,
            wide,
            wide,
            bias,
            wide,
            small,
            small,
            small,
            wide,
            bias,
            wide,
            small,
            P("mp"),
            wide,
            wide,
            bias,
        ),
        check_vma=False,
    )
```

```python
import functools
import math

import jax
import jax.numpy as jnp
from jax import lax
from jax.experimental import pallas as pl
from jax.experimental.pallas import tpu as pltpu
from jax.sharding import PartitionSpec as P

HD = 64
IMG_LEN = 577
F32 = jnp.float32
BF16 = jnp.bfloat16
MESH = pl.DeviceIdType.MESH
TILE = 256
PQ, PK, PV, PO = 0, 1, 2, 3
G1, S1, OB, G2, S2, DB, UB, QB, VB = 0, 1, 2, 3, 4, 5, 6, 8, 9
DG1, DS1, DOB, DG2, DS2, DDB, DUB, DQB, DVB, PEAK = 0, 1, 2, 3, 4, 5, 6, 7, 8, 9


def dot_nn(left, right):
    return lax.dot_general(left, right, (((1,), (0,)), ((), ())), preferred_element_type=F32)


def dot_nt(left, right):
    return lax.dot_general(left, right, (((1,), (1,)), ((), ())), preferred_element_type=F32)


def dot_tn(left, right):
    return lax.dot_general(left, right, (((0,), (0,)), ((), ())), preferred_element_type=F32)


def standardize(rows):
    center = rows - jnp.mean(rows, axis=-1, keepdims=True)
    inverse = lax.rsqrt(jnp.mean(center * center, axis=-1, keepdims=True) + 1e-05)
    return center * inverse, inverse


def norm_back(incoming, scaled, inverse, gain):
    upward = incoming * gain
    return inverse * (
        upward
        - jnp.mean(upward, axis=-1, keepdims=True)
        - scaled * jnp.mean(upward * scaled, axis=-1, keepdims=True)
    )


def each(low, high, body):
    if high - low <= 8:
        for at in range(low, high):
            body(at)
    else:

        def step(at, carry):
            body(at)
            return carry

        lax.fori_loop(low, high, step, 0)


def sum_rows(rows):
    return jnp.sum(rows, axis=0, keepdims=True)


class Layer:
    def __init__(self, size, refs):
        self.__dict__.update(size)
        self.__dict__.update(refs)
        self.dp_at = lax.axis_index("dp")
        self.mp_at = lax.axis_index("mp")
        self.line_at = self.dp_at // 2
        self.pair_at = lax.rem(self.dp_at, 2)
        self.chip_at = self.mp_at // 2
        self.core_at = lax.rem(self.mp_at, 2)
        self.sib = (self.dp_at, self.chip_at * 2 + 1 - self.core_at)
        self.across = (self.dp_at, (1 - self.chip_at) * 2 + self.core_at)
        self.pair = (self.line_at * 2 + 1 - self.pair_at, self.mp_at)
        self.stage_sends = [[], []]
        self.spread_sends = [[], [], [], []]
        self.late = []

    def line_of(self, step):
        return lax.rem(self.line_at + step + self.lines, self.lines)

    def line_peer(self, step):
        return (self.line_of(step) * 2 + self.pair_at, self.mp_at)

    def slot(self, line, pair):
        return pl.ds(pl.multiple_of((line * 2 + pair) * self.shard, self.shard), self.shard)

    def block(self, micro, chip, core):
        start = micro * self.rows + (chip * 2 + core) * self.pad
        return pl.ds(pl.multiple_of(start, 16), self.pad)

    def own_block(self, micro):
        return self.block(micro, self.chip_at, self.core_at)

    def source(self, piece):
        if piece < 4:
            return (self.query_w, self.key_w, self.value_w, self.out_w)[piece]
        which, chunk = (piece - 4) % 2, (piece - 4) // 2
        return (self.up_w, self.down_w)[which].at[:, pl.ds(chunk * TILE, TILE)]

    def copy(self, src, dst, send_sem, recv_sem, device):
        return pltpu.make_async_remote_copy(
            src_ref=src,
            dst_ref=dst,
            send_sem=send_sem,
            recv_sem=recv_sem,
            device_id=device,
            device_id_type=MESH,
        )

    def weight_line(self, piece, step):
        return self.copy(
            self.source(piece),
            self.weights.at[piece, self.slot(self.line_at, self.pair_at)],
            self.wz_send.at[piece, step - 1],
            self.wz_recv.at[piece, step - 1],
            self.line_peer(step),
        )

    def weight_line_in(self, piece, step):
        place = self.weights.at[piece, self.slot(self.line_of(-step), self.pair_at)]
        return self.copy(
            place,
            place,
            self.wz_send.at[piece, step - 1],
            self.wz_recv.at[piece, step - 1],
            self.line_peer(-step),
        )

    def weight_pair(self, piece, step, own):
        place = self.weights.at[piece, self.slot(self.line_of(-step), self.pair_at)]
        return self.copy(
            self.source(piece) if own else place,
            place,
            self.wx_send.at[piece, step],
            self.wx_recv.at[piece, step],
            self.pair,
        )

    def weight_pair_in(self, piece, step):
        place = self.weights.at[piece, self.slot(self.line_of(-step), 1 - self.pair_at)]
        return self.copy(
            place, place, self.wx_send.at[piece, step], self.wx_recv.at[piece, step], self.pair
        )

    def weight_local(self, piece):
        return pltpu.make_async_copy(
            self.source(piece),
            self.weights.at[piece, self.slot(self.line_at, self.pair_at)],
            self.wl_sem.at[piece],
        )

    def send_weight(self, piece):
        self.weight_pair(piece, 0, True).start()
        each(1, self.lines, lambda step: self.weight_line(piece, step).start())
        self.weight_local(piece).start()

    def pass_weight(self, piece):
        def one(step):
            self.weight_line_in(piece, step).wait_recv()
            self.weight_pair(piece, step, False).start()

        each(1, self.lines, one)

    def await_weight(self, piece):
        self.weight_local(piece).wait()
        each(0, self.lines, lambda step: self.weight_pair_in(piece, step).wait_recv())

    def spread_copy(self, kind, micro, ref, which):
        place = ref.at[self.own_block(micro)]
        if which == 2:
            place = ref.at[self.block(micro, 1 - self.chip_at, self.core_at)]
        return self.copy(
            place,
            place,
            self.ag_send.at[kind, micro, which],
            self.ag_recv.at[kind, micro, which],
            self.across if which == 0 else self.sib,
        )

    def spread_in(self, kind, micro, ref, which):
        chip = self.chip_at if which == 1 else 1 - self.chip_at
        core = self.core_at if which == 0 else 1 - self.core_at
        place = ref.at[self.block(micro, chip, core)]
        return self.copy(
            place,
            place,
            self.ag_send.at[kind, micro, which],
            self.ag_recv.at[kind, micro, which],
            self.across if which == 0 else self.sib,
        )

    def spread(self, kind, micro, ref):
        for which in (0, 1):
            one = self.spread_copy(kind, micro, ref, which)
            one.start()
            self.spread_sends[kind].append(one)

    def spread_on(self, kind, micro, ref):
        self.spread_in(kind, micro, ref, 0).wait_recv()
        one = self.spread_copy(kind, micro, ref, 2)
        one.start()
        self.spread_sends[kind].append(one)

    def spread_sent(self, kind):
        for one in self.spread_sends[kind]:
            one.wait_send()
        self.spread_sends[kind] = []

    def spread_end(self, kind, micro, ref):
        self.spread_in(kind, micro, ref, 1).wait_recv()
        self.spread_in(kind, micro, ref, 2).wait_recv()

    def collect(self, kind, micro, terms):
        for one in self.stage_sends[micro]:
            one.wait_send()
        self.stage_sends[micro] = []
        stage, keep = self.stage, self.keep_own.at[1 if kind == 1 else 0, micro]

        def fill(ref, at, chip, core):
            def step(tile, carry):
                cols = pl.ds(pl.multiple_of(tile * TILE, TILE), TILE)
                product = terms(self.block(micro, chip, core), cols)
                ref[at + (slice(None), cols)] = product.astype(ref.dtype)
                return carry

            lax.fori_loop(0, self.width // TILE, step, 0)

        for half in (0, 1):
            chip = 1 - self.chip_at if half == 0 else self.chip_at
            fill(stage, (micro, half), chip, 1 - self.core_at)
            one = self.copy(
                stage.at[micro, half],
                self.sib_in.at[kind, micro, half],
                self.rs_send.at[kind, micro, half],
                self.rs_recv.at[kind, micro, half],
                self.sib,
            )
            one.start()
            self.stage_sends[micro].append(one)
            if half == 0:
                fill(self.keep_far, (), chip, self.core_at)
        incoming = self.sib_in.at[kind, micro, 0]
        self.copy(
            stage.at[micro, 0],
            incoming,
            self.rs_send.at[kind, micro, 0],
            self.rs_recv.at[kind, micro, 0],
            self.sib,
        ).wait_recv()
        incoming[...] = (self.keep_far[...] + incoming[...].astype(F32)).astype(BF16)
        one = self.copy(
            incoming,
            self.far_in.at[kind, micro],
            self.rs_send.at[kind, micro, 2],
            self.rs_recv.at[kind, micro, 2],
            self.across,
        )
        one.start()
        self.late.append(one)
        fill(keep, (), self.chip_at, self.core_at)

    def collected(self, kind, micro):
        near, far = self.sib_in.at[kind, micro, 1], self.far_in.at[kind, micro]
        self.copy(
            near, near, self.rs_send.at[kind, micro, 1], self.rs_recv.at[kind, micro, 1], self.sib
        ).wait_recv()
        self.copy(
            far, far, self.rs_send.at[kind, micro, 2], self.rs_recv.at[kind, micro, 2], self.across
        ).wait_recv()
        total = self.keep_own[1 if kind == 1 else 0, micro] + near[...].astype(F32)
        return (total + far[...].astype(F32))[: self.part]

    def summed(self, piece):
        if piece < 4:
            return self.proj_back.at[: self.width, piece * TILE : (piece + 1) * TILE]
        return self.wide_sums.at[piece - 4]

    def grad_pair(self, piece, line):
        return self.copy(
            self.summed(piece).at[self.slot(line, 1 - self.pair_at)],
            self.pair_in.at[piece, line],
            self.gx_send.at[piece, line],
            self.gx_recv.at[piece, line],
            self.pair,
        )

    def grad_line(self, piece, step):
        return self.copy(
            self.pair_in.at[piece, self.line_of(step)],
            self.line_in.at[piece, step - 1],
            self.gz_send.at[piece, step - 1],
            self.gz_recv.at[piece, step - 1],
            self.line_peer(step),
        )

    def grad_make(self, piece, left, right, send=True):
        out = self.summed(piece)
        lines_in_tile = TILE // (2 * self.shard)

        def step(tile, carry):
            cols = pl.ds(pl.multiple_of(tile * TILE, TILE), TILE)
            out[cols, :] = dot_tn(left[:, cols], right).astype(BF16)
            if send:
                for at in range(lines_in_tile):
                    self.grad_pair(piece, tile * lines_in_tile + at).start()
            return carry

        lax.fori_loop(0, self.width // TILE, step, 0)

    def grad_send(self, piece):
        each(0, self.lines, lambda line: self.grad_pair(piece, line).start())

    def grad_pass(self, piece):
        def one(step):
            line = self.line_of(step)
            self.grad_pair(piece, line).wait_recv()
            mine = self.summed(piece)[self.slot(line, self.pair_at), :].astype(F32)
            mine = mine + self.pair_in[piece, line].astype(F32)
            self.pair_in[piece, line] = mine.astype(BF16)
            self.grad_line(piece, step).start()

        each(1, self.lines, one)

    def grad_end(self, piece):
        self.grad_pair(piece, self.line_at).wait_recv()
        total = self.summed(piece)[self.slot(self.line_at, self.pair_at), :].astype(F32)
        total = total + self.pair_in[piece, self.line_at].astype(F32)
        for step in range(1, self.lines):
            self.grad_line(piece, step).wait_recv()
            total = total + self.line_in[piece, step - 1].astype(F32)
        at = piece if piece < 4 else 4 + self.chunks * ((piece - 4) % 2) + (piece - 4) // 2
        self.weight_g[:, at * TILE : (at + 1) * TILE] = total

    def clip(self, peaks):
        root = jnp.sqrt(self.tau[0, 0] / jnp.maximum(peaks, self.tau[0, 0]))
        head = lax.broadcasted_iota(jnp.int32, (1, TILE), 1) // HD
        roots = jnp.zeros((1, TILE), F32)
        for at in range(self.heads):
            roots = jnp.where(head == at, root[:, at : at + 1], roots)
        first = (4 + 2 * self.chunks) * TILE
        mine = self.slot(self.line_at, self.pair_at)
        for at, piece in enumerate((PQ, PK)):
            cols = slice(first + at * TILE, first + (at + 1) * TILE)
            self.weight_g[:, cols] = self.weights[piece, mine, :].astype(F32) * roots
        bias = self.packed[8:9, :] * roots[:, 0:128] + self.packed[9:10, :] * roots[:, 128:256]
        return bias

    def vector_copy(self, step):
        return self.copy(
            self.packed,
            self.vectors_in.at[self.dp_at],
            self.v_send.at[0, step - 1],
            self.v_recv.at[0, step - 1],
            (lax.rem(self.dp_at + step, self.dps), self.mp_at),
        )

    def vector_copy_in(self, step):
        origin = lax.rem(self.dp_at - step + self.dps, self.dps)
        place = self.vectors_in.at[origin]
        return self.copy(
            place,
            place,
            self.v_send.at[0, step - 1],
            self.v_recv.at[0, step - 1],
            (origin, self.mp_at),
        )

    def share_copy(self, step):
        target = lax.rem(self.dp_at + step, self.dps)
        return self.copy(
            self.shares.at[target],
            self.shares_in.at[step - 1],
            self.v_send.at[1, step - 1],
            self.v_recv.at[1, step - 1],
            (target, self.mp_at),
        )

    def group_copy(self, step):
        return self.copy(
            self.group.at[0],
            self.group.at[step],
            self.m_send.at[step - 1],
            self.m_recv.at[step - 1],
            (self.dp_at, lax.rem(self.mp_at + step, 4)),
        )

    def take_vectors(self):
        if not self.own_vectors:
            self.vectors[...] = self.packed[...]
            return
        self.vectors_in[self.dp_at] = self.packed[...]
        for step in range(1, self.dps):
            self.vector_copy_in(step).wait_recv()
        rest = self.vectors_in[0, 8:16, :]
        for at in range(1, self.dps):
            rest = rest + self.vectors_in[at, 8:16, :]
        for at in range(self.dps):
            self.vectors[0:8, at * 128 : (at + 1) * 128] = self.vectors_in[at, 0:8, :]
        for row, first in ((QB, 0), (VB, 2)):
            self.vectors[row : row + 1, 0:128] = rest[first : first + 1]
            self.vectors[row : row + 1, 128:256] = rest[first + 1 : first + 2]

    def give_vectors(self):
        if not self.own_vectors:
            self.vector_g[...] = self.sums[...]
            return
        for at in range(self.dps):
            half = (at * 32 // 128) * 128
            self.shares[at, 0:7, :] = self.sums[0:7, at * 128 : (at + 1) * 128]
            self.shares[at, 7:9, :] = self.sums[7:9, half : half + 128]
            self.shares[at, 9:16, :] = self.sums[9:16, 0:128]
        for step in range(1, self.dps):
            self.share_copy(step).start()

    def end_vectors(self):
        if not self.own_vectors:
            return
        total = self.shares[self.dp_at]
        most = total[PEAK : PEAK + 1]
        for step in range(1, self.dps):
            self.share_copy(step).wait_recv()
            came = self.shares_in[step - 1]
            total = total + came
            most = jnp.maximum(most, came[PEAK : PEAK + 1])
        self.group[0] = total
        for step in range(1, 4):
            self.group_copy(step).start()
        whole = total[0:6]
        for step in range(1, 4):
            self.group_copy(step).wait_recv()
            whole = whole + self.group[step, 0:6, :]
        narrow = jnp.concatenate([total[7:9], self.clip(most), jnp.zeros((5, 128), F32)], axis=0)
        shift = lax.rem(128 - lax.rem(self.dp_at * 32, 128), 128)
        narrow = pltpu.roll(narrow, shift, 1)
        self.vector_g[0:6, :] = whole
        self.vector_g[6:7, :] = total[6:7]
        self.vector_g[7:9, :] = narrow[0:2]
        self.vector_g[9:10, :] = most
        self.vector_g[10:11, :] = narrow[2:3]
        self.vector_g[11:16, :] = jnp.zeros((5, 128), F32)

    def vector(self, row, start=0, size=None):
        size = self.width if size is None else size
        return self.vectors[row : row + 1, pl.ds(start, size)]

    def add_sum(self, row, value, start=0):
        cols = pl.ds(start, value.shape[1])
        self.sums[row : row + 1, cols] = self.sums[row : row + 1, cols] + value

    def mask(self, micro):
        row = self.mp_at * self.part + lax.broadcasted_iota(jnp.int32, (self.part, 1), 0)
        live = jnp.where(self.counts[micro] > 0, 1.0, 0.0).astype(F32)
        return jnp.where(row < IMG_LEN, live, 0.0)

    def put_rows(self, ref, micro, rows):
        filler = jnp.zeros((self.pad - self.part, self.width), F32)
        ref[self.own_block(micro), :] = jnp.concatenate([rows, filler], axis=0).astype(BF16)

    def first_norm(self, micro):
        scaled, _ = standardize(self.images[micro, 0].astype(F32))
        self.put_rows(self.normed_one, micro, scaled * self.vector(G1) + self.vector(S1))
        self.spread(0, micro, self.normed_one)

    def out_rows(self, micro):
        return self.out_grad[micro, 0].astype(F32) * self.mask(micro)

    def project_back(self, micro):
        rows = self.out_rows(micro)
        self.put_rows(self.proj_back, micro, rows)
        self.add_sum(DDB, sum_rows(rows.astype(BF16).astype(F32)))
        self.spread(2, micro, self.proj_back)

    def second_norm(self, micro):
        rows = self.images[micro, 0].astype(F32) + self.collected(0, micro) + self.vector(OB)
        self.after_attn[micro] = rows
        scaled, _ = standardize(rows)
        self.put_rows(self.normed_two, micro, scaled * self.vector(G2) + self.vector(S2))
        self.spread(1, micro, self.normed_two)

    def give_result(self, micro):
        rows = self.after_attn[micro] + self.collected(1, micro) + self.vector(DB)
        self.rows_g[0, micro, 0] = (self.mask(micro) * rows).astype(BF16)

    def second_norm_back(self, micro):
        incoming = self.collected(2, micro)
        scaled, inverse = standardize(self.after_attn[micro])
        rows = self.out_rows(micro) + norm_back(incoming, scaled, inverse, self.vector(G2))
        self.attn_back[micro] = rows
        self.add_sum(DOB, sum_rows(rows.astype(BF16).astype(F32)))
        self.add_sum(DG2, sum_rows(incoming * scaled))
        self.add_sum(DS2, sum_rows(incoming))
        self.put_rows(self.attended_back, micro, rows)
        self.spread(3, micro, self.attended_back)

    def first_norm_back(self, micro):
        incoming = self.collected(3, micro)
        scaled, inverse = standardize(self.images[micro, 0].astype(F32))
        self.add_sum(DG1, sum_rows(incoming * scaled))
        self.add_sum(DS1, sum_rows(incoming))
        rows = self.attn_back[micro] + norm_back(incoming, scaled, inverse, self.vector(G1))
        self.rows_g[1, micro, 0] = rows.astype(BF16)

    def image_rows(self, micro):
        return pl.ds(micro * self.rows, self.rows)

    def counted(self, axis):
        shape = (self.rows, 1) if axis == 0 else (1, self.rows)
        row = lax.broadcasted_iota(jnp.int32, shape, axis)
        block = row // self.pad
        inside = row - block * self.pad
        return (inside < self.part) & (block * self.part + inside < IMG_LEN)

    def head_columns(self, head):
        column = lax.broadcasted_iota(jnp.int32, (self.rows, TILE), 1)
        return column // HD == head

    def project_heads(self, micro):
        rows = self.image_rows(micro)
        normed = self.normed_one[rows, :]
        scale = 1.0 / math.sqrt(HD)
        query = dot_nn(normed, self.weights[PQ]) + self.vector(QB, 0, TILE)
        self.queries[rows, :] = (query.astype(BF16).astype(F32) * scale).astype(BF16)
        self.keys[rows, :] = dot_nn(normed, self.weights[PK]).astype(BF16)
        value = dot_nn(normed, self.weights[PV]) + self.vector(VB, 0, TILE)
        self.values[rows, :] = value.astype(BF16)

    def attend(self, micro):
        rows = self.image_rows(micro)
        self.turned[...] = self.values[rows, :].T
        live = jnp.where(self.counts[micro] > 0, 0.0, -1e30).astype(F32)

        def one_head(head, carry):
            query = jnp.where(self.head_columns(head), self.queries[rows, :], jnp.zeros((), BF16))
            scores = dot_nt(self.keys[rows, :], query)
            scores = jnp.where(self.counted(0), scores, -1e30)
            top = jnp.max(scores, axis=0, keepdims=True)
            expo = jnp.exp(scores - top)
            total = jnp.sum(expo, axis=0, keepdims=True)
            self.log_total[micro, head] = top + jnp.log(total)
            cols = pl.ds(pl.multiple_of(head * HD, HD), HD)
            mixed = dot_nn(self.turned[cols, :], expo.astype(BF16))
            self.mixed_turned[micro, cols, :] = mixed * (1.0 / total)
            peak = jnp.max(jnp.where(self.counted(1), top, -1e30), axis=1, keepdims=True)
            peak = jnp.where(live < 0.0, -1e30, peak)
            lane = lax.broadcasted_iota(jnp.int32, (1, 128), 1)
            seen = self.sums[PEAK : PEAK + 1, 0:128]
            self.sums[PEAK : PEAK + 1, 0:128] = jnp.where(
                lane == head, jnp.maximum(seen, peak), seen
            )
            return carry

        lax.fori_loop(0, self.heads, one_head, 0)
        self.mixed[rows, :] = self.mixed_turned[micro].T.astype(BF16)

    def attend_back(self, micro):
        rows = self.image_rows(micro)
        self.mixed_back[...] = dot_nn(self.attended_back[rows, :], self.weights[PO]).astype(BF16)
        self.turned[...] = self.keys[rows, :].T
        self.mixed_back_turned[...] = self.mixed_back[...].T
        self.key_sum[...] = jnp.zeros_like(self.key_sum)
        self.value_sum[...] = jnp.zeros_like(self.value_sum)
        chunk = self.rows // 2

        def one_head(head, carry):
            columns = self.head_columns(head)
            none = jnp.zeros((), BF16)
            query = jnp.where(columns, self.queries[rows, :], none)
            outward = jnp.where(columns, self.mixed_back[...], none)
            cols = pl.ds(pl.multiple_of(head * HD, HD), HD)
            dots = self.mixed_back_turned[cols, :].astype(F32) * self.mixed_turned[micro, cols, :]
            delta = jnp.sum(dots, axis=0, keepdims=True)
            log_total = self.log_total[micro, head]
            for at in range(2):
                part = pl.ds(micro * self.rows + at * chunk, chunk)
                here = pl.ds(at * chunk, chunk)
                scores = dot_nt(self.keys[part, :], query)
                counted = self.counted(0)[at * chunk : (at + 1) * chunk]
                probs = jnp.where(counted, jnp.exp(scores - log_total), 0.0)
                prob_back = dot_nt(self.values[part, :], outward)
                self.probs[here, :] = probs.astype(BF16)
                self.score_back[here, :] = (probs * (prob_back - delta)).astype(BF16)
            self.value_sum[...] += dot_nn(self.probs[...], outward)
            self.key_sum[...] += dot_nn(self.score_back[...], query)
            self.query_turned[cols, :] = dot_nn(self.turned[cols, :], self.score_back[...])
            return carry

        lax.fori_loop(0, self.heads, one_head, 0)
        scale = 1.0 / math.sqrt(HD)
        query_back = (self.query_turned[...] * scale).T.astype(BF16)
        value_back = self.value_sum[...].astype(BF16)
        self.queries[rows, :] = query_back
        self.keys[rows, :] = self.key_sum[...].astype(BF16)
        self.values[rows, :] = value_back
        self.add_sum(DQB, sum_rows(query_back.astype(F32)))
        self.add_sum(DVB, sum_rows(value_back.astype(F32)))

    def feed(self, micro, chunk):
        cols = pl.ds(chunk * TILE, TILE)
        up, down = self.weights.at[4 + 2 * chunk], self.weights.at[5 + 2 * chunk]
        part = self.rows // 2
        total = jnp.zeros((1, TILE), F32)
        for at in range(2):
            rows = pl.ds(micro * self.rows + at * part, part)
            hidden = dot_nn(self.normed_two[rows, :], up[...])
            hidden = hidden + self.vector(UB, chunk * TILE, TILE)
            gate = jax.nn.sigmoid(1.702 * hidden)
            self.activated[rows, cols] = (hidden * gate).astype(BF16)
            back = dot_nn(self.proj_back[rows, :], down[...])
            back = back * (gate + 1.702 * hidden * gate * (1.0 - gate))
            back = back.astype(BF16)
            self.pre_back[rows, cols] = back
            total = total + sum_rows(back.astype(F32))
        self.add_sum(DUB, total, chunk * TILE)

    def out_terms(self, rows, cols):
        return dot_nt(self.mixed[rows, :], self.weights[PO, cols, :])

    def wide_terms(self, ref, first):
        def terms(rows, cols):
            total = None
            for chunk in range(self.chunks):
                one = dot_nt(
                    ref[rows, chunk * TILE : (chunk + 1) * TILE],
                    self.weights[first + 2 * chunk, cols, :],
                )
                total = one if total is None else total + one
            return total

        return terms

    def input_terms(self, rows, cols):
        total = dot_nt(self.queries[rows, :], self.weights[PQ, cols, :])
        total = total + dot_nt(self.keys[rows, :], self.weights[PK, cols, :])
        return total + dot_nt(self.values[rows, :], self.weights[PV, cols, :])

    def enter(self):
        barrier = pltpu.get_barrier_semaphore()
        peers = [self.sib, self.across]
        if self.own_vectors:
            peers.append((self.dp_at, (1 - self.chip_at) * 2 + 1 - self.core_at))
        for peer in peers:
            pl.semaphore_signal(barrier, inc=1, device_id=peer, device_id_type=MESH)
        if self.own_vectors:

            def hail(step):
                peer = (lax.rem(self.dp_at + step, self.dps), self.mp_at)
                pl.semaphore_signal(barrier, inc=1, device_id=peer, device_id_type=MESH)

            each(1, self.dps, hail)
            pl.semaphore_wait(barrier, 3 + self.dps - 1)
        else:
            pl.semaphore_signal(barrier, inc=1, device_id=self.pair, device_id_type=MESH)

            def hail(step):
                peer = self.line_peer(step)
                pl.semaphore_signal(barrier, inc=1, device_id=peer, device_id_type=MESH)

            each(1, self.lines, hail)
            pl.semaphore_wait(barrier, 2 + self.lines)

    def run(self):
        pieces = 4 + 2 * self.chunks
        self.enter()
        if self.own_vectors:
            for step in range(1, self.dps):
                self.vector_copy(step).start()
        for piece in range(4):
            self.send_weight(piece)
        self.sums[...] = jnp.zeros_like(self.sums)
        self.sums[PEAK : PEAK + 1, :] = jnp.full((1, self.width), -1e30, F32)
        self.take_vectors()
        for micro in (0, 1):
            self.first_norm(micro)
        self.pass_weight(PQ)
        self.project_back(0)
        self.project_back(1)
        self.spread_on(0, 0, self.normed_one)
        self.pass_weight(PK)
        self.spread_on(0, 1, self.normed_one)
        self.pass_weight(PV)
        for piece in range(4, pieces):
            self.send_weight(piece)
        for piece in range(3):
            self.await_weight(piece)
        self.spread_end(0, 0, self.normed_one)
        self.project_heads(0)
        self.attend(0)
        self.pass_weight(PO)
        self.spread_end(0, 1, self.normed_one)
        self.project_heads(1)
        self.attend(1)
        self.pass_weight(4)
        self.await_weight(PO)
        self.collect(0, 0, self.out_terms)
        self.collect(0, 1, self.out_terms)
        self.pass_weight(5)
        self.spread_on(2, 0, self.proj_back)
        self.spread_on(2, 1, self.proj_back)
        self.second_norm(0)
        self.pass_weight(6)
        self.second_norm(1)
        self.pass_weight(7)
        self.spread_on(1, 0, self.normed_two)
        self.pass_weight(8)
        self.spread_on(1, 1, self.normed_two)
        waiting = list(range(9, pieces))
        for micro in (0, 1):
            self.spread_end(1, micro, self.normed_two)
            self.spread_end(2, micro, self.proj_back)
        for chunk in range(self.chunks):
            up, down = 4 + 2 * chunk, 5 + 2 * chunk
            self.await_weight(up)
            self.await_weight(down)
            self.feed(0, chunk)
            if waiting:
                self.pass_weight(waiting.pop(0))
            self.feed(1, chunk)
            if waiting:
                self.pass_weight(waiting.pop(0))
            cols = slice(chunk * TILE, (chunk + 1) * TILE)
            self.grad_make(up, self.normed_two, self.pre_back[:, cols], False)
        self.spread_sent(1)
        self.collect(2, 0, self.wide_terms(self.pre_back, 4))
        for chunk in range(self.chunks):
            self.grad_send(4 + 2 * chunk)
        self.collect(2, 1, self.wide_terms(self.pre_back, 4))

        def down_grad(chunk):
            cols = slice(chunk * TILE, (chunk + 1) * TILE)
            self.grad_make(5 + 2 * chunk, self.proj_back, self.activated[:, cols])

        down_grad(0)
        self.second_norm_back(0)
        self.grad_pass(4)
        down_grad(1)
        down_grad(2)
        self.second_norm_back(1)
        self.grad_pass(6)
        down_grad(3)
        self.grad_pass(8)
        self.spread_on(3, 0, self.attended_back)
        self.spread_end(3, 0, self.attended_back)
        self.attend_back(0)
        self.spread_on(3, 1, self.attended_back)
        self.collect(3, 0, self.input_terms)
        self.grad_pass(10)
        self.grad_pass(5)
        self.spread_end(3, 1, self.attended_back)
        self.spread_sent(2)
        self.grad_make(PO, self.attended_back, self.mixed[...])
        self.attend_back(1)
        self.grad_make(PQ, self.normed_one, self.queries[...])
        self.grad_make(PK, self.normed_one, self.keys[...])
        self.grad_make(PV, self.normed_one, self.values[...])
        self.grad_pass(7)
        self.collect(3, 1, self.input_terms)
        self.grad_pass(9)
        self.grad_pass(11)
        self.collect(1, 0, self.wide_terms(self.activated, 5))
        self.grad_pass(PO)
        self.first_norm_back(0)
        self.collect(1, 1, self.wide_terms(self.activated, 5))
        self.first_norm_back(1)
        self.give_vectors()
        self.grad_pass(PQ)
        self.give_result(0)
        self.grad_pass(PK)
        self.give_result(1)
        self.grad_pass(PV)
        for piece in range(4, pieces):
            self.grad_end(piece)
        self.end_vectors()
        for piece in (PO, PQ, PK, PV):
            self.grad_end(piece)
        for kind in (0, 3):
            self.spread_sent(kind)
        for one in self.late + self.stage_sends[0] + self.stage_sends[1]:
            one.wait_send()
        for piece in range(pieces):
            self.weight_pair(piece, 0, True).wait_send()
            each(1, self.lines, lambda step: self.weight_line(piece, step).wait_send())
            each(1, self.lines, lambda step: self.weight_pair(piece, step, False).wait_send())
            each(0, self.lines, lambda line: self.grad_pair(piece, line).wait_send())
            each(1, self.lines, lambda step: self.grad_line(piece, step).wait_send())
        if self.own_vectors:
            for step in range(1, self.dps):
                self.vector_copy(step).wait_send()
                self.share_copy(step).wait_send()
            for step in range(1, 4):
                self.group_copy(step).wait_send()


def layer_kernel(size, names, *refs):
    named = dict(zip(names, refs))
    named["attended_back"] = named["normed_two"]
    Layer(size, named).run()


def fused_layer(size, counts, tau, images, out_grad, packed, weights):
    width, shard, part, rows, pad = (size[key] for key in ("width", "shard", "part", "rows", "pad"))
    lines, dps, pieces = size["lines"], size["dps"], 4 + 2 * size["chunks"]
    units = size["chunks"] * TILE
    vmem = pl.BlockSpec(memory_space=pltpu.VMEM)
    anywhere = pl.BlockSpec(memory_space=pl.ANY)
    vector_shape = (16, 128) if size["own_vectors"] else (16, width)
    outputs = {
        "rows_g": ((2,) + images.shape, BF16),
        "weight_g": ((shard, pieces * TILE + 2 * TILE), F32),
        "vector_g": (vector_shape, F32),
    }
    dma = pltpu.SemaphoreType.DMA
    vm = pltpu.VMEM
    scratch = {
        "weights": vm((pieces, width, TILE), BF16),
        "normed_one": vm((2 * rows, width), BF16),
        "normed_two": vm((2 * rows, width), BF16),
        "proj_back": vm((2 * rows, width), BF16),
        "queries": vm((2 * rows, TILE), BF16),
        "keys": vm((2 * rows, TILE), BF16),
        "values": vm((2 * rows, TILE), BF16),
        "mixed": vm((2 * rows, TILE), BF16),
        "mixed_turned": vm((2, TILE, rows), F32),
        "log_total": vm((2, size["heads"], 1, rows), F32),
        "activated": vm((2 * rows, units), BF16),
        "pre_back": vm((2 * rows, units), BF16),
        "turned": vm((TILE, rows), BF16),
        "mixed_back": vm((rows, TILE), BF16),
        "mixed_back_turned": vm((TILE, rows), BF16),
        "query_turned": vm((TILE, rows), F32),
        "key_sum": vm((rows, TILE), F32),
        "value_sum": vm((rows, TILE), F32),
        "probs": vm((rows, rows), BF16),
        "score_back": vm((rows, rows), BF16),
        "stage": vm((2, 2, pad, width), BF16),
        "keep_far": vm((pad, width), F32),
        "keep_own": vm((2, 2, pad, width), F32),
        "sib_in": vm((4, 2, 2, pad, width), BF16),
        "far_in": vm((4, 2, pad, width), BF16),
        "after_attn": vm((2, part, width), F32),
        "attn_back": vm((2, part, width), F32),
        "wide_sums": vm((pieces - 4, width, TILE), BF16),
        "pair_in": vm((pieces, lines, shard, TILE), BF16),
        "line_in": vm((pieces, lines - 1, shard, TILE), BF16),
        "vectors": vm((16, width), F32),
        "sums": vm((16, width), F32),
        "wz_send": dma((pieces, lines - 1)),
        "wz_recv": dma((pieces, lines - 1)),
        "wx_send": dma((pieces, lines)),
        "wx_recv": dma((pieces, lines)),
        "wl_sem": dma((pieces,)),
        "ag_send": dma((4, 2, 3)),
        "ag_recv": dma((4, 2, 3)),
        "rs_send": dma((4, 2, 3)),
        "rs_recv": dma((4, 2, 3)),
        "gx_send": dma((pieces, lines)),
        "gx_recv": dma((pieces, lines)),
        "gz_send": dma((pieces, lines - 1)),
        "gz_recv": dma((pieces, lines - 1)),
    }
    if size["own_vectors"]:
        scratch |= {
            "vectors_in": vm((dps, 16, 128), F32),
            "shares": vm((dps, 16, 128), F32),
            "shares_in": vm((dps - 1, 16, 128), F32),
            "group": vm((4, 16, 128), F32),
            "v_send": dma((2, dps - 1)),
            "v_recv": dma((2, dps - 1)),
            "m_send": dma((3,)),
            "m_recv": dma((3,)),
        }
    inputs = ["counts", "tau", "images", "out_grad", "packed"]
    inputs += ["query_w", "key_w", "value_w", "out_w", "up_w", "down_w"]
    names = inputs + list(outputs) + list(scratch)
    return pl.pallas_call(
        functools.partial(layer_kernel, size, names),
        out_shape=[jax.ShapeDtypeStruct(*spec) for spec in outputs.values()],
        in_specs=[pl.BlockSpec(memory_space=pltpu.SMEM)] * 2 + [vmem] * 3 + [anywhere] * 6,
        out_specs=[vmem] * len(outputs),
        scratch_shapes=list(scratch.values()),
        compiler_params=pltpu.CompilerParams(
            collective_id=0, has_side_effects=True, vmem_limit_bytes=63 * 2**20
        ),
    )(counts, tau, images, out_grad, packed, *weights)


def on_device(
    images,
    counts,
    first_gain,
    first_shift,
    query_weight,
    query_bias,
    key_weight,
    value_weight,
    value_bias,
    out_weight,
    out_bias,
    second_gain,
    second_shift,
    up_weight,
    up_bias,
    down_weight,
    down_bias,
    clip_tau,
    out_grad,
):
    part, width = images.shape[2:]
    dps = lax.axis_size("dp")
    dp_at = lax.axis_index("dp")
    shard = query_weight.shape[0]
    pad = (part + 15) // 16 * 16
    size = {
        "width": width,
        "shard": shard,
        "part": part,
        "pad": pad,
        "rows": pad * lax.axis_size("mp"),
        "dps": dps,
        "lines": dps // 2,
        "heads": query_weight.shape[1] // HD,
        "chunks": up_weight.shape[1] // TILE,
        "own_vectors": shard == 128,
    }
    bias_cols = query_bias.shape[1]
    parts = [first_gain, first_shift, out_bias, second_gain, second_shift, down_bias, up_bias[0]]
    if size["own_vectors"]:
        place = jnp.zeros((2, TILE), F32)
        biases = jnp.concatenate([query_bias, value_bias]).astype(F32)
        place = lax.dynamic_update_slice(place, biases, (0, dp_at * bias_cols))
        packed = jnp.concatenate(
            [
                jnp.stack(parts).astype(F32),
                jnp.zeros((1, 128), F32),
                place.reshape(4, 128),
                jnp.zeros((4, 128), F32),
            ]
        )
    else:
        whole = [lax.all_gather(one, "dp", axis=0, tiled=True) for one in parts]
        rest = [
            jnp.pad(lax.all_gather(one[0], "dp", axis=0, tiled=True), (0, width - TILE))
            for one in (query_bias, value_bias)
        ]
        filler = jnp.zeros((width,), BF16)
        packed = jnp.stack(whole + [filler] + rest + [filler] * 6).astype(F32)
    weights = (query_weight, key_weight, value_weight, out_weight, up_weight, down_weight)
    rows_g, weight_g, vector_g = fused_layer(
        size, counts.reshape(-1), clip_tau.reshape(1, 1), images, out_grad, packed, weights
    )
    columns, units = query_weight.shape[1], up_weight.shape[1]
    edges = [0, columns, 2 * columns, 3 * columns, 4 * columns]
    edges += [edges[-1] + units, edges[-1] + 2 * units]
    query_g, key_g, value_g, out_g, up_g, down_g = (
        weight_g[:, low:high] for low, high in zip(edges[:-1], edges[1:])
    )
    if size["own_vectors"]:
        vectors = [vector_g[row] for row in range(7)]
        query_bias_g = vector_g[DQB : DQB + 1, :bias_cols]
        value_bias_g = vector_g[DVB : DVB + 1, :bias_cols]
        peaks = vector_g[PEAK, : size["heads"]]
        clipped_query = weight_g[:, edges[-1] : edges[-1] + columns]
        clipped_key = weight_g[:, edges[-1] + columns :]
        clipped_bias = vector_g[PEAK + 1 : PEAK + 2, :bias_cols]
    else:
        mine = vector_g[:DUB]
        mine = lax.psum(mine, "mp")
        mine = lax.psum_scatter(mine, "dp", scatter_dimension=1, tiled=True)
        up_bias_g = lax.psum_scatter(vector_g[DUB], "dp", scatter_dimension=0, tiled=True)
        vectors = [mine[row] for row in range(6)] + [up_bias_g]
        both = vector_g[DQB : DVB + 1, :TILE]
        both = lax.psum_scatter(both, "dp", scatter_dimension=1, tiled=True)
        query_bias_g, value_bias_g = both[0:1], both[1:2]
        peaks = lax.pmax(vector_g[PEAK, : size["heads"]], "dp")
        head_root = jnp.sqrt(clip_tau / jnp.maximum(peaks, clip_tau))
        column_root = jnp.repeat(head_root, HD)
        clipped_query = query_weight.astype(F32) * column_root[None, :]
        clipped_key = key_weight.astype(F32) * column_root[None, :]
        bias_root = lax.dynamic_slice(column_root, (dp_at * bias_cols,), (bias_cols,))
        clipped_bias = query_bias.astype(F32) * bias_root[None, :]
    return (
        rows_g[0],
        rows_g[1],
        vectors[DG1],
        vectors[DS1],
        query_g,
        query_bias_g,
        key_g,
        value_g,
        value_bias_g,
        out_g,
        vectors[DOB],
        vectors[DG2],
        vectors[DS2],
        up_g,
        vectors[DUB][None, :],
        down_g,
        vectors[DDB],
        peaks,
        clipped_query,
        clipped_key,
        clipped_bias,
    )


def solution(mesh):
    rows = P(None, "dp", "mp", None)
    wide, small, bias = P("dp", "mp"), P("dp"), P("mp", "dp")
    return jax.shard_map(
        on_device,
        mesh=mesh,
        in_specs=(
            rows,
            P(None, "dp"),
            small,
            small,
            wide,
            bias,
            wide,
            wide,
            bias,
            wide,
            small,
            small,
            small,
            wide,
            bias,
            wide,
            small,
            P(),
            rows,
        ),
        out_specs=(
            rows,
            rows,
            small,
            small,
            wide,
            bias,
            wide,
            wide,
            bias,
            wide,
            small,
            small,
            small,
            wide,
            bias,
            wide,
            small,
            P("mp"),
            wide,
            wide,
            bias,
        ),
        check_vma=False,
    )
```

```python
import functools
import math

import jax
import jax.numpy as jnp
from jax import lax
from jax.experimental import pallas as pl
from jax.experimental.pallas import tpu as pltpu
from jax.sharding import PartitionSpec as P

HD = 64
IMG_LEN = 577
F32 = jnp.float32
BF16 = jnp.bfloat16
MESH = pl.DeviceIdType.MESH
TILE = 256
PQ, PK, PV, PO = 0, 1, 2, 3
PAIR_FIRST = (2, 8)
LINE_FIRST = (4, 5)
DIRECT = (0, 1, 2)
G1, S1, OB, G2, S2, DB, UB, QB, VB = 0, 1, 2, 3, 4, 5, 6, 8, 9
DG1, DS1, DOB, DG2, DS2, DDB, DUB, DQB, DVB, PEAK = 0, 1, 2, 3, 4, 5, 6, 7, 8, 9


def dot_nn(left, right):
    return lax.dot_general(left, right, (((1,), (0,)), ((), ())), preferred_element_type=F32)


def dot_nt(left, right):
    return lax.dot_general(left, right, (((1,), (1,)), ((), ())), preferred_element_type=F32)


def dot_tn(left, right):
    return lax.dot_general(left, right, (((0,), (0,)), ((), ())), preferred_element_type=F32)


def standardize(rows):
    center = rows - jnp.mean(rows, axis=-1, keepdims=True)
    inverse = lax.rsqrt(jnp.mean(center * center, axis=-1, keepdims=True) + 1e-05)
    return center * inverse, inverse


def norm_back(incoming, scaled, inverse, gain):
    upward = incoming * gain
    return inverse * (
        upward
        - jnp.mean(upward, axis=-1, keepdims=True)
        - scaled * jnp.mean(upward * scaled, axis=-1, keepdims=True)
    )


def each(low, high, body):
    if high - low <= 8:
        for at in range(low, high):
            body(at)
    else:

        def step(at, carry):
            body(at)
            return carry

        lax.fori_loop(low, high, step, 0)


def sum_rows(rows):
    return jnp.sum(rows, axis=0, keepdims=True)


class Layer:
    def __init__(self, size, refs):
        self.__dict__.update(size)
        self.__dict__.update(refs)
        self.dp_at = lax.axis_index("dp")
        self.mp_at = lax.axis_index("mp")
        self.line_at = self.dp_at // 2
        self.pair_at = lax.rem(self.dp_at, 2)
        self.chip_at = self.mp_at // 2
        self.core_at = lax.rem(self.mp_at, 2)
        self.sib = (self.dp_at, self.chip_at * 2 + 1 - self.core_at)
        self.across = (self.dp_at, (1 - self.chip_at) * 2 + self.core_at)
        self.pair = (self.line_at * 2 + 1 - self.pair_at, self.mp_at)
        self.middle = (self.line_at == 1) | (self.line_at == 2)
        self.pieces = 4 + 2 * self.chunks
        self.pair_first = PAIR_FIRST if self.lines == 4 else ()
        self.line_first = LINE_FIRST if self.lines == 4 else ()
        self.pair_slots = (self.pieces - len(self.line_first)) * self.lines
        self.rest = None
        self.stage_sends = [[], []]
        self.spread_sends = [[], [], [], []]
        self.late = []

    def line_of(self, step):
        return lax.rem(self.line_at + step + self.lines, self.lines)

    def line_peer(self, step):
        return (self.line_of(step) * 2 + self.pair_at, self.mp_at)

    def slot(self, line, pair):
        return pl.ds(pl.multiple_of((line * 2 + pair) * self.shard, self.shard), self.shard)

    def block(self, micro, chip, core):
        start = micro * self.rows + (chip * 2 + core) * self.pad
        return pl.ds(pl.multiple_of(start, 16), self.pad)

    def own_block(self, micro):
        return self.block(micro, self.chip_at, self.core_at)

    def source(self, piece):
        if piece < 4:
            return (self.query_w, self.key_w, self.value_w, self.out_w)[piece]
        which, chunk = (piece - 4) % 2, (piece - 4) // 2
        return (self.up_w, self.down_w)[which].at[:, pl.ds(chunk * TILE, TILE)]

    def copy(self, src, dst, send_sem, recv_sem, device):
        return pltpu.make_async_remote_copy(
            src_ref=src,
            dst_ref=dst,
            send_sem=send_sem,
            recv_sem=recv_sem,
            device_id=device,
            device_id_type=MESH,
        )

    def channels(self, piece):
        if piece in self.pair_first:
            return ((piece, False), (self.pieces + self.pair_first.index(piece), True))
        return ((piece, False),)

    def shard_place(self, piece, line, other):
        pair = 1 - self.pair_at if other else self.pair_at
        return self.weights.at[piece, self.slot(line, pair)]

    def broad(self, piece, channel, other, step):
        place = self.shard_place(piece, self.line_at, other)
        return self.copy(
            place if other else self.source(piece),
            place,
            self.wz_send.at[channel, step - 1],
            self.wz_recv.at[channel, step - 1],
            self.line_peer(step),
        )

    def broad_in(self, piece, channel, other, step):
        place = self.shard_place(piece, self.line_of(-step), other)
        return self.copy(
            place,
            place,
            self.wz_send.at[channel, step - 1],
            self.wz_recv.at[channel, step - 1],
            self.line_peer(-step),
        )

    def broad_each(self, piece, channel, other, act):
        def one(step):
            if self.lines == 4 and step != 2:
                @pl.when(self.line_at != (3 if step == 1 else 0))
                def _():
                    act(self.broad(piece, channel, other, step))
            else:
                act(self.broad(piece, channel, other, step))

        each(1, self.lines, one)

    def relay(self, piece, channel, other, act):
        if self.lines != 4:
            return

        @pl.when(self.middle)
        def _():
            place = self.shard_place(piece, 3 * (2 - self.line_at), other)
            end = (3 * (self.line_at - 1) * 2 + self.pair_at, self.mp_at)
            act(
                self.copy(
                    place,
                    place,
                    self.wz_send.at[channel, 3],
                    self.wz_recv.at[channel, 2 * (self.line_at - 1)],
                    end,
                )
            )

    def weight_pair(self, piece, step, own):
        place = self.shard_place(piece, self.line_of(-step), False)
        return self.copy(
            self.source(piece) if own else place,
            place,
            self.wx_send.at[piece, step],
            self.wx_recv.at[piece, step],
            self.pair,
        )

    def weight_pair_in(self, piece, step):
        place = self.shard_place(piece, self.line_of(-step), True)
        return self.copy(
            place, place, self.wx_send.at[piece, step], self.wx_recv.at[piece, step], self.pair
        )

    def weight_local(self, piece):
        return pltpu.make_async_copy(
            self.source(piece),
            self.shard_place(piece, self.line_at, False),
            self.wl_sem.at[piece],
        )

    def send_weight(self, piece):
        self.weight_pair(piece, 0, True).start()
        self.broad_each(piece, piece, False, lambda one: one.start())
        self.weight_local(piece).start()

    def pass_weight(self, piece):
        self.flush()
        if piece in self.pair_first:
            self.weight_pair_in(piece, 0).wait_recv()
            channel, other = self.channels(piece)[1]
            self.broad_each(piece, channel, other, lambda one: one.start())
            return

        def one(step, last=False):
            self.broad_in(piece, piece, False, step).wait_recv()
            if last:
                self.relay(piece, piece, False, lambda one: one.start())
            self.weight_pair(piece, step, False).start()

        if self.lines == 4:
            second = jnp.where(self.line_at < 2, 3, 1)
            one(2, True)
            one(second)
            self.rest = lambda: one(4 - second)
        else:
            each(1, self.lines, one)

    def flush(self):
        if self.rest is not None:
            self.rest()
        self.rest = None

    def relay_weight(self, piece):
        for channel, other in self.channels(piece):
            if piece in self.pair_first:
                self.broad_in(piece, channel, other, 2).wait_recv()
                self.relay(piece, channel, other, lambda one: one.start())

    def await_weight(self, piece):
        self.weight_local(piece).wait()
        if piece in self.pair_first:
            for channel, other in self.channels(piece):
                for step in (1, 3):
                    self.broad_in(piece, channel, other, step).wait_recv()
        else:
            each(0, self.lines, lambda step: self.weight_pair_in(piece, step).wait_recv())

    def weight_sent(self, piece):
        self.weight_pair(piece, 0, True).wait_send()
        for channel, other in self.channels(piece):
            self.broad_each(piece, channel, other, lambda one: one.wait_send())
            self.relay(piece, channel, other, lambda one: one.wait_send())
        if piece not in self.pair_first:
            each(1, self.lines, lambda step: self.weight_pair(piece, step, False).wait_send())

    def spread_copy(self, kind, micro, ref, which):
        place = ref.at[self.own_block(micro)]
        if which == 2:
            place = ref.at[self.block(micro, 1 - self.chip_at, self.core_at)]
        return self.copy(
            place,
            place,
            self.ag_send.at[kind, micro, which],
            self.ag_recv.at[kind, micro, which],
            self.across if which == 0 else self.sib,
        )

    def spread_in(self, kind, micro, ref, which):
        chip = self.chip_at if which == 1 else 1 - self.chip_at
        core = self.core_at if which == 0 else 1 - self.core_at
        place = ref.at[self.block(micro, chip, core)]
        return self.copy(
            place,
            place,
            self.ag_send.at[kind, micro, which],
            self.ag_recv.at[kind, micro, which],
            self.across if which == 0 else self.sib,
        )

    def spread(self, kind, micro, ref):
        for which in (0, 1):
            one = self.spread_copy(kind, micro, ref, which)
            one.start()
            self.spread_sends[kind].append(one)

    def spread_on(self, kind, micro, ref):
        self.spread_in(kind, micro, ref, 0).wait_recv()
        one = self.spread_copy(kind, micro, ref, 2)
        one.start()
        self.spread_sends[kind].append(one)

    def spread_sent(self, kind):
        for one in self.spread_sends[kind]:
            one.wait_send()
        self.spread_sends[kind] = []

    def spread_end(self, kind, micro, ref):
        self.spread_in(kind, micro, ref, 1).wait_recv()
        self.spread_in(kind, micro, ref, 2).wait_recv()

    def collect(self, kind, micro, terms):
        for one in self.stage_sends[micro]:
            one.wait_send()
        self.stage_sends[micro] = []
        held = 1 if kind == 1 else 0
        for half, chip in ((0, 1 - self.chip_at), (1, self.chip_at)):
            start = pl.multiple_of(micro * self.rows + chip * 2 * self.pad, 16)
            stage, keep = self.stage.at[micro, half], self.keep.at[held, micro, half]

            for tile in range(self.width // TILE):
                cols = pl.ds(tile * TILE, TILE)
                product = terms(pl.ds(start, 2 * self.pad), cols)
                low, high = product[: self.pad], product[self.pad :]
                keep[:, cols] = jnp.where(self.core_at == 0, low, high)
                stage[:, cols] = jnp.where(self.core_at == 0, high, low).astype(BF16)
            one = self.copy(
                stage,
                self.sib_in.at[kind, micro, half],
                self.rs_send.at[kind, micro, half],
                self.rs_recv.at[kind, micro, half],
                self.sib,
            )
            one.start()
            self.stage_sends[micro].append(one)

    def collect_far(self, kind, micro):
        incoming = self.sib_in.at[kind, micro, 0]
        self.copy(
            incoming,
            incoming,
            self.rs_send.at[kind, micro, 0],
            self.rs_recv.at[kind, micro, 0],
            self.sib,
        ).wait_recv()
        held = self.keep[1 if kind == 1 else 0, micro, 0]
        incoming[...] = (held + incoming[...].astype(F32)).astype(BF16)
        one = self.copy(
            incoming,
            self.far_in.at[kind, micro],
            self.rs_send.at[kind, micro, 2],
            self.rs_recv.at[kind, micro, 2],
            self.across,
        )
        one.start()
        self.late.append(one)

    def collected(self, kind, micro):
        near, far = self.sib_in.at[kind, micro, 1], self.far_in.at[kind, micro]
        self.copy(
            near, near, self.rs_send.at[kind, micro, 1], self.rs_recv.at[kind, micro, 1], self.sib
        ).wait_recv()
        self.copy(
            far, far, self.rs_send.at[kind, micro, 2], self.rs_recv.at[kind, micro, 2], self.across
        ).wait_recv()
        total = self.keep[1 if kind == 1 else 0, micro, 1] + near[...].astype(F32)
        return (total + far[...].astype(F32))[: self.part]

    def summed(self, piece):
        if piece < 4:
            return self.proj_back.at[: self.width, piece * TILE : (piece + 1) * TILE]
        return self.wide_sums.at[piece - 4]

    def sum_place(self, piece, line, other):
        pair = 1 - self.pair_at if other else self.pair_at
        return self.summed(piece).at[self.slot(line, pair)]

    def sum_channels(self, piece):
        if piece in self.line_first:
            return ((piece, False), (self.pieces + self.line_first.index(piece), True))
        return ((piece, False),)

    def relayed(self, piece):
        return self.lines == 4 and piece not in DIRECT

    def out_columns(self, piece):
        at = piece if piece < 4 else 4 + self.chunks * ((piece - 4) % 2) + (piece - 4) // 2
        return self.weight_g.at[:, pl.ds(at * TILE, TILE)]

    def pair_place(self, piece, line):
        if piece in self.line_first:
            return self.pair_in.at[self.pair_slots + self.line_first.index(piece)]
        before = sum(1 for other in self.line_first if other < piece)
        return self.pair_in.at[(piece - before) * self.lines + line]

    def grad_pair(self, piece, line):
        at = 0 if piece in self.line_first else line
        return self.copy(
            self.sum_place(piece, line, True),
            self.pair_place(piece, line),
            self.gx_send.at[piece, at],
            self.gx_recv.at[piece, at],
            self.pair,
        )

    def line_source(self, piece, line, other):
        if piece in self.line_first:
            return self.sum_place(piece, line, other)
        return self.pair_place(piece, line)

    def grad_line(self, piece, channel, other, step):
        line = self.line_of(step)
        target, at = line, step - 1
        if self.relayed(piece) and step != 2:
            far = self.line_at == (3 if step == 1 else 0)
            target = jnp.where(far, 2 if step == 1 else 1, line)
            at = jnp.where(far, 3, step - 1)
        return self.copy(
            self.line_source(piece, line, other),
            self.line_in.at[channel, at],
            self.gz_send.at[channel, step - 1],
            self.gz_recv.at[channel, at],
            (target * 2 + self.pair_at, self.mp_at),
        )

    def grad_line_in(self, channel, at):
        place = self.line_in.at[channel, at]
        return self.copy(
            place, place, self.gz_send.at[channel, 0], self.gz_recv.at[channel, at], self.pair
        )

    def grad_make(self, piece, left, right):
        out = self.summed(piece)
        for tile in range(self.width // TILE):
            cols = pl.ds(tile * TILE, TILE)
            out[cols, :] = dot_tn(left[:, cols], right).astype(BF16)
        self.grad_send(piece)

    def grad_send(self, piece):
        if piece in self.line_first:
            for channel, other in self.sum_channels(piece):
                for step in (1, 3):
                    self.grad_line(piece, channel, other, step).start()

                @pl.when(jnp.logical_not(self.middle))
                def _():
                    self.grad_line(piece, channel, other, 2).start()
        else:
            each(0, self.lines, lambda line: self.grad_pair(piece, line).start())

    def grad_pass(self, piece):
        def one(step, wait=True):
            line = self.line_of(step)
            if wait:
                self.grad_pair(piece, line).wait_recv()
            ref = self.pair_place(piece, line)
            total = self.sum_place(piece, line, False)[...].astype(F32) + ref[...].astype(F32)
            ref[...] = total.astype(BF16)
            self.grad_line(piece, piece, False, step).start()

        if piece in self.line_first:
            return
        if self.relayed(piece):
            one(1)
            one(3)
            self.grad_pair(piece, self.line_of(2)).wait_recv()
            pl.when(jnp.logical_not(self.middle))(lambda: one(2, False))
        else:
            each(1, self.lines, one)

    def grad_relay(self, piece):
        if not self.relayed(piece):
            return

        @pl.when(self.middle)
        def _():
            for channel, other in self.sum_channels(piece):
                line = self.line_of(2)
                self.grad_line_in(channel, 3).wait_recv()
                ref = self.line_source(piece, line, other)
                total = ref[...].astype(F32) + self.line_in[channel, 3].astype(F32)
                if piece not in self.line_first:
                    total = total + self.sum_place(piece, line, False)[...].astype(F32)
                ref[...] = total.astype(BF16)
                self.grad_line(piece, channel, other, 2).start()

    def line_total(self, piece, channel, ref):
        for step in range(1, self.lines):

            def one():
                self.grad_line_in(channel, step - 1).wait_recv()
                ref[...] += self.line_in[channel, step - 1].astype(F32)

            if self.relayed(piece) and step != 2:
                pl.when(self.line_at != (0 if step == 1 else 3))(one)
            else:
                one()

    def grad_cross(self, piece):
        if piece not in self.line_first:
            return
        ref = self.sum_place(piece, self.line_at, True)
        total = self.out_columns(piece)
        total[...] = ref[...].astype(F32)
        self.line_total(piece, self.sum_channels(piece)[1][0], total)
        ref[...] = total[...].astype(BF16)
        self.grad_pair(piece, self.line_at).start()

    def grad_end(self, piece):
        ref = self.out_columns(piece)
        self.grad_pair(piece, self.line_at).wait_recv()
        came = self.pair_place(piece, self.line_at)[...].astype(F32)
        ref[...] = self.sum_place(piece, self.line_at, False)[...].astype(F32) + came
        self.line_total(piece, piece, ref)

    def grad_sent(self, piece):
        if piece in self.line_first:
            self.grad_pair(piece, self.line_at).wait_send()
        else:
            each(0, self.lines, lambda line: self.grad_pair(piece, line).wait_send())
        for channel, other in self.sum_channels(piece):
            each(
                1,
                self.lines,
                lambda step: self.grad_line(piece, channel, other, step).wait_send(),
            )

    def clip(self, peaks):
        root = jnp.sqrt(self.tau[0, 0] / jnp.maximum(peaks, self.tau[0, 0]))
        head = lax.broadcasted_iota(jnp.int32, (1, TILE), 1) // HD
        roots = jnp.zeros((1, TILE), F32)
        for at in range(self.heads):
            roots = jnp.where(head == at, root[:, at : at + 1], roots)
        first = (4 + 2 * self.chunks) * TILE
        mine = self.slot(self.line_at, self.pair_at)
        for at, piece in enumerate((PQ, PK)):
            cols = slice(first + at * TILE, first + (at + 1) * TILE)
            self.weight_g[:, cols] = self.weights[piece, mine, :].astype(F32) * roots
        bias = self.packed[8:9, :] * roots[:, 0:128] + self.packed[9:10, :] * roots[:, 128:256]
        return bias

    def vector_copy(self, step):
        return self.copy(
            self.packed,
            self.vectors_in.at[self.dp_at],
            self.v_send.at[0, step - 1],
            self.v_recv.at[0, step - 1],
            (lax.rem(self.dp_at + step, self.dps), self.mp_at),
        )

    def vector_copy_in(self, step):
        origin = lax.rem(self.dp_at - step + self.dps, self.dps)
        place = self.vectors_in.at[origin]
        return self.copy(
            place,
            place,
            self.v_send.at[0, step - 1],
            self.v_recv.at[0, step - 1],
            (origin, self.mp_at),
        )

    def share_copy(self, step):
        target = lax.rem(self.dp_at + step, self.dps)
        return self.copy(
            self.shares.at[target],
            self.shares_in.at[step - 1],
            self.v_send.at[1, step - 1],
            self.v_recv.at[1, step - 1],
            (target, self.mp_at),
        )

    def group_copy(self, step):
        return self.copy(
            self.group.at[0],
            self.group.at[step],
            self.m_send.at[step - 1],
            self.m_recv.at[step - 1],
            (self.dp_at, lax.rem(self.mp_at + step, 4)),
        )

    def take_vectors(self):
        if not self.own_vectors:
            self.vectors[...] = self.packed[...]
            return
        self.vectors_in[self.dp_at] = self.packed[...]
        for step in range(1, self.dps):
            self.vector_copy_in(step).wait_recv()
        rest = self.vectors_in[0, 8:16, :]
        for at in range(1, self.dps):
            rest = rest + self.vectors_in[at, 8:16, :]
        for at in range(self.dps):
            self.vectors[0:8, at * 128 : (at + 1) * 128] = self.vectors_in[at, 0:8, :]
        for row, first in ((QB, 0), (VB, 2)):
            self.vectors[row : row + 1, 0:128] = rest[first : first + 1]
            self.vectors[row : row + 1, 128:256] = rest[first + 1 : first + 2]

    def give_vectors(self):
        if not self.own_vectors:
            self.vector_g[...] = self.sums[...]
            return
        for at in range(self.dps):
            half = (at * 32 // 128) * 128
            self.shares[at, 0:7, :] = self.sums[0:7, at * 128 : (at + 1) * 128]
            self.shares[at, 7:9, :] = self.sums[7:9, half : half + 128]
            self.shares[at, 9:16, :] = self.sums[9:16, 0:128]
        for step in range(1, self.dps):
            self.share_copy(step).start()

    def end_vectors(self):
        if not self.own_vectors:
            return
        total = self.shares[self.dp_at]
        most = total[PEAK : PEAK + 1]
        for step in range(1, self.dps):
            self.share_copy(step).wait_recv()
            came = self.shares_in[step - 1]
            total = total + came
            most = jnp.maximum(most, came[PEAK : PEAK + 1])
        self.group[0] = total
        for step in range(1, 4):
            self.group_copy(step).start()
        whole = total[0:6]
        for step in range(1, 4):
            self.group_copy(step).wait_recv()
            whole = whole + self.group[step, 0:6, :]
        narrow = jnp.concatenate([total[7:9], self.clip(most), jnp.zeros((5, 128), F32)], axis=0)
        shift = lax.rem(128 - lax.rem(self.dp_at * 32, 128), 128)
        narrow = pltpu.roll(narrow, shift, 1)
        self.vector_g[0:6, :] = whole
        self.vector_g[6:7, :] = total[6:7]
        self.vector_g[7:9, :] = narrow[0:2]
        self.vector_g[9:10, :] = most
        self.vector_g[10:11, :] = narrow[2:3]
        self.vector_g[11:16, :] = jnp.zeros((5, 128), F32)

    def vector(self, row, start=0, size=None):
        size = self.width if size is None else size
        return self.vectors[row : row + 1, pl.ds(start, size)]

    def add_sum(self, row, value, start=0):
        cols = pl.ds(start, value.shape[1])
        self.sums[row : row + 1, cols] = self.sums[row : row + 1, cols] + value

    def mask(self, micro):
        row = self.mp_at * self.part + lax.broadcasted_iota(jnp.int32, (self.part, 1), 0)
        live = jnp.where(self.counts[micro] > 0, 1.0, 0.0).astype(F32)
        return jnp.where(row < IMG_LEN, live, 0.0)

    def put_rows(self, ref, micro, rows):
        filler = jnp.zeros((self.pad - self.part, self.width), F32)
        ref[self.own_block(micro), :] = jnp.concatenate([rows, filler], axis=0).astype(BF16)

    def first_norm(self, micro):
        scaled, _ = standardize(self.images[micro, 0].astype(F32))
        self.put_rows(self.normed_one, micro, scaled * self.vector(G1) + self.vector(S1))
        self.spread(0, micro, self.normed_one)

    def out_rows(self, micro):
        return self.out_grad[micro, 0].astype(F32) * self.mask(micro)

    def project_back(self, micro):
        rows = self.out_rows(micro)
        self.put_rows(self.proj_back, micro, rows)
        self.add_sum(DDB, sum_rows(rows.astype(BF16).astype(F32)))
        self.spread(2, micro, self.proj_back)

    def second_norm(self, micro):
        rows = self.images[micro, 0].astype(F32) + self.collected(0, micro) + self.vector(OB)
        self.after_attn[micro] = rows
        scaled, _ = standardize(rows)
        self.put_rows(self.normed_two, micro, scaled * self.vector(G2) + self.vector(S2))
        self.spread(1, micro, self.normed_two)

    def give_result(self, micro):
        rows = self.after_attn[micro] + self.collected(1, micro) + self.vector(DB)
        self.rows_g[0, micro, 0] = (self.mask(micro) * rows).astype(BF16)

    def second_norm_back(self, micro):
        incoming = self.collected(2, micro)
        scaled, inverse = standardize(self.after_attn[micro])
        rows = self.out_rows(micro) + norm_back(incoming, scaled, inverse, self.vector(G2))
        self.attn_back[micro] = rows
        self.add_sum(DOB, sum_rows(rows.astype(BF16).astype(F32)))
        self.add_sum(DG2, sum_rows(incoming * scaled))
        self.add_sum(DS2, sum_rows(incoming))
        self.put_rows(self.attended_back, micro, rows)
        self.spread(3, micro, self.attended_back)

    def first_norm_back(self, micro):
        incoming = self.collected(3, micro)
        scaled, inverse = standardize(self.images[micro, 0].astype(F32))
        self.add_sum(DG1, sum_rows(incoming * scaled))
        self.add_sum(DS1, sum_rows(incoming))
        rows = self.attn_back[micro] + norm_back(incoming, scaled, inverse, self.vector(G1))
        self.rows_g[1, micro, 0] = rows.astype(BF16)

    def image_rows(self, micro):
        return pl.ds(micro * self.rows, self.rows)

    def counted(self, axis):
        shape = (self.rows, 1) if axis == 0 else (1, self.rows)
        row = lax.broadcasted_iota(jnp.int32, shape, axis)
        block = row // self.pad
        inside = row - block * self.pad
        return (inside < self.part) & (block * self.part + inside < IMG_LEN)

    def head_columns(self, head):
        column = lax.broadcasted_iota(jnp.int32, (self.rows, TILE), 1)
        return column // HD == head

    def project_heads(self, micro):
        rows = self.image_rows(micro)
        normed = self.normed_one[rows, :]
        scale = 1.0 / math.sqrt(HD)
        query = dot_nn(normed, self.weights[PQ]) + self.vector(QB, 0, TILE)
        self.queries[rows, :] = (query.astype(BF16).astype(F32) * scale).astype(BF16)
        self.keys[rows, :] = dot_nn(normed, self.weights[PK]).astype(BF16)
        value = dot_nn(normed, self.weights[PV]) + self.vector(VB, 0, TILE)
        self.values[rows, :] = value.astype(BF16)

    def attend(self, micro, between):
        rows = self.image_rows(micro)
        values = self.turned.at[:, : self.rows]
        values[...] = self.values[rows, :].T
        live = jnp.where(self.counts[micro] > 0, 0.0, -1e30).astype(F32)
        split = (self.rows // 2 + 127) // 128 * 128

        def one_head(head):
            query = jnp.where(self.head_columns(head), self.queries[rows, :], jnp.zeros((), BF16))
            cols = pl.ds(head * HD, HD)
            top = total = mixed = None
            for low, high in ((0, split), (split, self.rows)):
                part = pl.ds(micro * self.rows + low, high - low)
                scores = dot_nt(self.keys[part, :], query)
                scores = jnp.where(self.counted(0)[low:high], scores, -1e30)
                most = jnp.max(scores, axis=0, keepdims=True)
                if top is None:
                    expo = jnp.exp(scores - most)
                    total = jnp.sum(expo, axis=0, keepdims=True)
                    mixed = dot_nn(values[cols, low:high], expo.astype(BF16))
                    top = most
                else:
                    most = jnp.maximum(top, most)
                    again = jnp.exp(top - most)
                    expo = jnp.exp(scores - most)
                    total = total * again + jnp.sum(expo, axis=0, keepdims=True)
                    added = dot_nn(values[cols, low:high], expo.astype(BF16))
                    mixed = mixed * again + added
                    top = most
            self.log_total[micro, pl.ds(head, 1), :] = top + jnp.log(total)
            self.mixed_turned[micro, cols, :] = mixed * (1.0 / total)
            peak = jnp.max(jnp.where(self.counted(1), top, -1e30), axis=1, keepdims=True)
            peak = jnp.where(live < 0.0, -1e30, peak)
            lane = lax.broadcasted_iota(jnp.int32, (1, 128), 1)
            seen = self.sums[PEAK : PEAK + 1, 0:128]
            self.sums[PEAK : PEAK + 1, 0:128] = jnp.where(
                lane == head, jnp.maximum(seen, peak), seen
            )

        for head in range(self.heads):
            if head == self.heads // 2:
                between()
            one_head(head)
        self.mixed[rows, :] = self.mixed_turned[micro].T.astype(BF16)

    def attend_back(self, micro, between):
        rows = self.image_rows(micro)
        self.mixed_back[...] = dot_nn(self.attended_back[rows, :], self.weights[PO]).astype(BF16)
        keys = self.turned.at[:, : self.rows]
        outwards = self.turned.at[:, self.rows :]
        keys[...] = self.keys[rows, :].T
        outwards[...] = self.mixed_back[...].T
        self.key_sum[...] = jnp.zeros_like(self.key_sum)
        self.value_sum[...] = jnp.zeros_like(self.value_sum)
        chunk = self.rows // 2

        def one_head(head):
            columns = self.head_columns(head)
            none = jnp.zeros((), BF16)
            query = jnp.where(columns, self.queries[rows, :], none)
            outward = jnp.where(columns, self.mixed_back[...], none)
            cols = pl.ds(head * HD, HD)
            dots = outwards[cols, :].astype(F32) * self.mixed_turned[micro, cols, :]
            delta = jnp.sum(dots, axis=0, keepdims=True)
            log_total = self.log_total[micro, pl.ds(head, 1), :]
            for at in range(2):
                part = pl.ds(micro * self.rows + at * chunk, chunk)
                here = pl.ds(at * chunk, chunk)
                scores = dot_nt(self.keys[part, :], query)
                counted = self.counted(0)[at * chunk : (at + 1) * chunk]
                probs = jnp.where(counted, jnp.exp(scores - log_total), 0.0)
                prob_back = dot_nt(self.values[part, :], outward)
                self.probs[here, :] = probs.astype(BF16)
                self.score_back[here, :] = (probs * (prob_back - delta)).astype(BF16)
            self.value_sum[...] += dot_nn(self.probs[...], outward)
            self.key_sum[...] += dot_nn(self.score_back[...], query)
            self.mixed_turned[micro, cols, :] = dot_nn(keys[cols, :], self.score_back[...])

        for head in range(self.heads):
            if head == self.heads // 2:
                between()
            one_head(head)
        scale = 1.0 / math.sqrt(HD)
        query_back = (self.mixed_turned[micro] * scale).T.astype(BF16)
        value_back = self.value_sum[...].astype(BF16)
        self.queries[rows, :] = query_back
        self.keys[rows, :] = self.key_sum[...].astype(BF16)
        self.values[rows, :] = value_back
        self.add_sum(DQB, sum_rows(query_back.astype(F32)))
        self.add_sum(DVB, sum_rows(value_back.astype(F32)))

    def feed(self, micro, chunk):
        cols = pl.ds(chunk * TILE, TILE)
        up, down = self.weights.at[4 + 2 * chunk], self.weights.at[5 + 2 * chunk]
        part = self.rows // 2
        total = jnp.zeros((1, TILE), F32)
        for at in range(2):
            rows = pl.ds(micro * self.rows + at * part, part)
            hidden = dot_nn(self.normed_two[rows, :], up[...])
            hidden = hidden + self.vector(UB, chunk * TILE, TILE)
            gate = jax.nn.sigmoid(1.702 * hidden)
            self.activated[rows, cols] = (hidden * gate).astype(BF16)
            back = dot_nn(self.proj_back[rows, :], down[...])
            back = back * (gate + 1.702 * hidden * gate * (1.0 - gate))
            back = back.astype(BF16)
            self.pre_back[rows, cols] = back
            total = total + sum_rows(back.astype(F32))
        self.add_sum(DUB, total, chunk * TILE)

    def out_terms(self, rows, cols):
        return dot_nt(self.mixed[rows, :], self.weights[PO, cols, :])

    def wide_terms(self, ref, first):
        def terms(rows, cols):
            total = None
            for chunk in range(self.chunks):
                one = dot_nt(
                    ref[rows, chunk * TILE : (chunk + 1) * TILE],
                    self.weights[first + 2 * chunk, cols, :],
                )
                total = one if total is None else total + one
            return total

        return terms

    def input_terms(self, rows, cols):
        total = dot_nt(self.queries[rows, :], self.weights[PQ, cols, :])
        total = total + dot_nt(self.keys[rows, :], self.weights[PK, cols, :])
        return total + dot_nt(self.values[rows, :], self.weights[PV, cols, :])

    def enter(self):
        barrier = pltpu.get_barrier_semaphore()
        peers = [self.sib, self.across]
        if self.own_vectors:
            peers.append((self.dp_at, (1 - self.chip_at) * 2 + 1 - self.core_at))
        for peer in peers:
            pl.semaphore_signal(barrier, inc=1, device_id=peer, device_id_type=MESH)
        if self.own_vectors:

            def hail(step):
                peer = (lax.rem(self.dp_at + step, self.dps), self.mp_at)
                pl.semaphore_signal(barrier, inc=1, device_id=peer, device_id_type=MESH)

            each(1, self.dps, hail)
            pl.semaphore_wait(barrier, 3 + self.dps - 1)
        else:
            pl.semaphore_signal(barrier, inc=1, device_id=self.pair, device_id_type=MESH)

            def hail(step):
                peer = self.line_peer(step)
                pl.semaphore_signal(barrier, inc=1, device_id=peer, device_id_type=MESH)

            each(1, self.lines, hail)
            pl.semaphore_wait(barrier, 2 + self.lines)

    def run(self):
        pieces = self.pieces
        last = self.chunks - 1
        self.enter()
        if self.own_vectors:
            for step in range(1, self.dps):
                self.vector_copy(step).start()
        for piece in (PQ, PV, PK):
            self.send_weight(piece)
        self.sums[...] = jnp.zeros_like(self.sums)
        self.sums[PEAK : PEAK + 1, :] = jnp.full((1, self.width), -1e30, F32)
        self.take_vectors()
        self.pass_weight(PV)
        for micro in (0, 1):
            self.first_norm(micro)
        self.pass_weight(PQ)
        self.pass_weight(PK)
        self.send_weight(PO)
        self.spread_on(0, 0, self.normed_one)
        self.relay_weight(PV)
        self.flush()
        self.send_weight(4)
        self.await_weight(PQ)
        self.await_weight(PK)
        self.spread_on(0, 1, self.normed_one)
        self.project_back(0)
        self.await_weight(PV)
        self.spread_end(0, 0, self.normed_one)
        self.project_heads(0)
        self.pass_weight(PO)
        self.send_weight(5)
        self.attend(0, lambda: None)
        self.flush()
        self.await_weight(PO)
        self.collect(0, 0, self.out_terms)
        self.collect_far(0, 0)
        self.pass_weight(4)
        self.send_weight(6)
        self.spread_end(0, 1, self.normed_one)
        self.project_heads(1)

        def between():
            self.spread_on(2, 0, self.proj_back)
            self.pass_weight(5)
            self.send_weight(7)

        self.attend(1, between)
        self.collect(0, 1, self.out_terms)
        self.collect_far(0, 1)
        self.pass_weight(6)
        self.send_weight(8)
        self.second_norm(0)
        self.pass_weight(8)
        self.send_weight(9)
        self.pass_weight(7)
        self.second_norm(1)
        self.project_back(1)
        self.send_weight(10)
        self.spread_on(1, 0, self.normed_two)
        self.pass_weight(9)
        self.send_weight(11)
        self.relay_weight(8)
        self.spread_end(1, 0, self.normed_two)
        self.spread_end(2, 0, self.proj_back)
        self.await_weight(4)
        self.await_weight(5)
        self.feed(0, 0)
        self.await_weight(6)
        self.await_weight(7)
        self.feed(0, 1)
        self.spread_on(1, 1, self.normed_two)
        self.pass_weight(10)
        self.await_weight(8)
        self.await_weight(9)
        self.feed(0, 2)
        self.pass_weight(11)
        self.spread_on(2, 1, self.proj_back)
        self.flush()
        self.await_weight(10)
        self.await_weight(11)
        self.feed(0, last)
        self.collect(2, 0, self.wide_terms(self.pre_back, 4))
        self.collect_far(2, 0)
        self.spread_end(1, 1, self.normed_two)
        self.spread_end(2, 1, self.proj_back)
        for chunk in range(self.chunks):
            self.feed(1, chunk)
        self.collect(2, 1, self.wide_terms(self.pre_back, 4))
        self.collect_far(2, 1)

        def up_grad(chunk):
            cols = slice(chunk * TILE, (chunk + 1) * TILE)
            self.grad_make(4 + 2 * chunk, self.normed_two, self.pre_back[:, cols])

        def down_grad(chunk):
            cols = slice(chunk * TILE, (chunk + 1) * TILE)
            self.grad_make(5 + 2 * chunk, self.proj_back, self.activated[:, cols])

        up_grad(1)
        self.second_norm_back(0)
        up_grad(0)
        down_grad(0)
        down_grad(1)
        self.second_norm_back(1)
        up_grad(2)
        self.spread_on(3, 0, self.attended_back)
        self.grad_pass(6)
        down_grad(2)
        self.collect(1, 0, self.wide_terms(self.activated, 5))
        self.grad_pass(7)
        self.spread_end(3, 0, self.attended_back)

        def between_first():
            self.grad_pass(8)
            self.grad_relay(4)
            self.grad_relay(5)

        self.attend_back(0, between_first)
        self.spread_on(3, 1, self.attended_back)
        self.collect(3, 0, self.input_terms)
        self.collect_far(3, 0)
        self.collect_far(1, 0)
        up_grad(3)
        self.grad_pass(9)
        self.grad_relay(6)
        self.grad_cross(4)
        self.grad_cross(5)
        down_grad(3)
        self.spread_sent(2)
        self.spread_end(3, 1, self.attended_back)
        self.grad_make(PO, self.attended_back, self.mixed[...])
        self.collect(1, 1, self.wide_terms(self.activated, 5))

        def between_second():
            self.grad_pass(10)
            self.grad_relay(7)
            self.grad_relay(8)

        self.attend_back(1, between_second)
        self.grad_make(PQ, self.normed_one, self.queries[...])
        self.grad_make(PK, self.normed_one, self.keys[...])
        self.grad_make(PV, self.normed_one, self.values[...])
        self.collect(3, 1, self.input_terms)
        self.collect_far(3, 1)
        self.collect_far(1, 1)
        self.grad_pass(11)
        self.grad_relay(9)
        self.first_norm_back(0)
        self.grad_pass(PO)
        self.grad_relay(10)
        self.first_norm_back(1)
        self.give_vectors()
        self.grad_pass(PQ)
        self.grad_relay(11)
        for piece in range(4, 10):
            self.grad_end(piece)
        self.grad_pass(PK)
        self.grad_relay(PO)
        self.give_result(0)
        self.give_result(1)
        self.grad_pass(PV)
        for piece in range(10, pieces):
            self.grad_end(piece)
        self.end_vectors()
        for piece in (PO, PQ, PK, PV):
            self.grad_end(piece)
        for kind in (0, 1, 3):
            self.spread_sent(kind)
        for one in self.late + self.stage_sends[0] + self.stage_sends[1]:
            one.wait_send()
        for piece in range(pieces):
            self.weight_sent(piece)
            self.grad_sent(piece)
        if self.own_vectors:
            for step in range(1, self.dps):
                self.vector_copy(step).wait_send()
                self.share_copy(step).wait_send()
            for step in range(1, 4):
                self.group_copy(step).wait_send()


def layer_kernel(size, names, *refs):
    named = dict(zip(names, refs))
    Layer(size, named).run()


def fused_layer(size, counts, tau, images, out_grad, packed, weights):
    width, shard, part, rows, pad = (size[key] for key in ("width", "shard", "part", "rows", "pad"))
    lines, dps, pieces = size["lines"], size["dps"], 4 + 2 * size["chunks"]
    units = size["chunks"] * TILE
    vmem = pl.BlockSpec(memory_space=pltpu.VMEM)
    anywhere = pl.BlockSpec(memory_space=pl.ANY)
    vector_shape = (16, 128) if size["own_vectors"] else (16, width)
    outputs = {
        "rows_g": ((2,) + images.shape, BF16),
        "weight_g": ((shard, pieces * TILE + 2 * TILE), F32),
        "vector_g": (vector_shape, F32),
    }
    four = lines == 4
    channels = pieces + (len(PAIR_FIRST) if four else 0)
    pair_slots = pieces * lines - (len(LINE_FIRST) * (lines - 1) if four else 0)
    sum_channels = pieces + (len(LINE_FIRST) if four else 0)
    lines_in = 4 if four else lines - 1
    dma = pltpu.SemaphoreType.DMA
    vm = pltpu.VMEM
    scratch = {
        "weights": vm((pieces, width, TILE), BF16),
        "normed_one": vm((2 * rows, width), BF16),
        "normed_two": vm((2 * rows, width), BF16),
        "proj_back": vm((2 * rows, width), BF16),
        "attended_back": vm((2 * rows, width), BF16),
        "queries": vm((2 * rows, TILE), BF16),
        "keys": vm((2 * rows, TILE), BF16),
        "values": vm((2 * rows, TILE), BF16),
        "mixed": vm((2 * rows, TILE), BF16),
        "mixed_turned": vm((2, TILE, rows), F32),
        "log_total": vm((2, size["heads"], rows), F32),
        "activated": vm((2 * rows, units), BF16),
        "pre_back": vm((2 * rows, units), BF16),
        "turned": vm((TILE, 2 * rows), BF16),
        "mixed_back": vm((rows, TILE), BF16),
        "key_sum": vm((rows, TILE), F32),
        "value_sum": vm((rows, TILE), F32),
        "probs": vm((rows, rows), BF16),
        "score_back": vm((rows, rows), BF16),
        "stage": vm((2, 2, pad, width), BF16),
        "keep": vm((2, 2, 2, pad, width), F32),
        "sib_in": vm((4, 2, 2, pad, width), BF16),
        "far_in": vm((4, 2, pad, width), BF16),
        "after_attn": vm((2, part, width), F32),
        "attn_back": vm((2, part, width), F32),
        "wide_sums": vm((pieces - 4, width, TILE), BF16),
        "pair_in": vm((pair_slots, shard, TILE), BF16),
        "line_in": vm((sum_channels, lines_in, shard, TILE), BF16),
        "vectors": vm((16, width), F32),
        "sums": vm((16, width), F32),
        "wz_send": dma((channels, lines_in)),
        "wz_recv": dma((channels, lines - 1)),
        "wx_send": dma((pieces, lines)),
        "wx_recv": dma((pieces, lines)),
        "wl_sem": dma((pieces,)),
        "ag_send": dma((4, 2, 3)),
        "ag_recv": dma((4, 2, 3)),
        "rs_send": dma((4, 2, 3)),
        "rs_recv": dma((4, 2, 3)),
        "gx_send": dma((pieces, lines)),
        "gx_recv": dma((pieces, lines)),
        "gz_send": dma((sum_channels, lines - 1)),
        "gz_recv": dma((sum_channels, lines_in)),
    }
    if size["own_vectors"]:
        scratch |= {
            "vectors_in": vm((dps, 16, 128), F32),
            "shares": vm((dps, 16, 128), F32),
            "shares_in": vm((dps - 1, 16, 128), F32),
            "group": vm((4, 16, 128), F32),
            "v_send": dma((2, dps - 1)),
            "v_recv": dma((2, dps - 1)),
            "m_send": dma((3,)),
            "m_recv": dma((3,)),
        }
    inputs = ["counts", "tau", "images", "out_grad", "packed"]
    inputs += ["query_w", "key_w", "value_w", "out_w", "up_w", "down_w"]
    names = inputs + list(outputs) + list(scratch)
    return pl.pallas_call(
        functools.partial(layer_kernel, size, names),
        out_shape=[jax.ShapeDtypeStruct(*spec) for spec in outputs.values()],
        in_specs=[pl.BlockSpec(memory_space=pltpu.SMEM)] * 2 + [vmem] * 3 + [anywhere] * 6,
        out_specs=[vmem] * len(outputs),
        scratch_shapes=list(scratch.values()),
        compiler_params=pltpu.CompilerParams(
            collective_id=0, has_side_effects=True, vmem_limit_bytes=65024 * 2**10
        ),
    )(counts, tau, images, out_grad, packed, *weights)


def on_device(
    images,
    counts,
    first_gain,
    first_shift,
    query_weight,
    query_bias,
    key_weight,
    value_weight,
    value_bias,
    out_weight,
    out_bias,
    second_gain,
    second_shift,
    up_weight,
    up_bias,
    down_weight,
    down_bias,
    clip_tau,
    out_grad,
):
    part, width = images.shape[2:]
    dps = lax.axis_size("dp")
    dp_at = lax.axis_index("dp")
    shard = query_weight.shape[0]
    pad = (part + 15) // 16 * 16
    size = {
        "width": width,
        "shard": shard,
        "part": part,
        "pad": pad,
        "rows": pad * lax.axis_size("mp"),
        "dps": dps,
        "lines": dps // 2,
        "heads": query_weight.shape[1] // HD,
        "chunks": up_weight.shape[1] // TILE,
        "own_vectors": shard == 128,
    }
    bias_cols = query_bias.shape[1]
    parts = [first_gain, first_shift, out_bias, second_gain, second_shift, down_bias, up_bias[0]]
    if size["own_vectors"]:
        place = jnp.zeros((2, TILE), F32)
        biases = jnp.concatenate([query_bias, value_bias]).astype(F32)
        place = lax.dynamic_update_slice(place, biases, (0, dp_at * bias_cols))
        packed = jnp.concatenate(
            [
                jnp.stack(parts).astype(F32),
                jnp.zeros((1, 128), F32),
                place.reshape(4, 128),
                jnp.zeros((4, 128), F32),
            ]
        )
    else:
        whole = [lax.all_gather(one, "dp", axis=0, tiled=True) for one in parts]
        rest = [
            jnp.pad(lax.all_gather(one[0], "dp", axis=0, tiled=True), (0, width - TILE))
            for one in (query_bias, value_bias)
        ]
        filler = jnp.zeros((width,), BF16)
        packed = jnp.stack(whole + [filler] + rest + [filler] * 6).astype(F32)
    weights = (query_weight, key_weight, value_weight, out_weight, up_weight, down_weight)
    rows_g, weight_g, vector_g = fused_layer(
        size, counts.reshape(-1), clip_tau.reshape(1, 1), images, out_grad, packed, weights
    )
    columns, units = query_weight.shape[1], up_weight.shape[1]
    edges = [0, columns, 2 * columns, 3 * columns, 4 * columns]
    edges += [edges[-1] + units, edges[-1] + 2 * units]
    query_g, key_g, value_g, out_g, up_g, down_g = (
        weight_g[:, low:high] for low, high in zip(edges[:-1], edges[1:])
    )
    if size["own_vectors"]:
        vectors = [vector_g[row] for row in range(7)]
        query_bias_g = vector_g[DQB : DQB + 1, :bias_cols]
        value_bias_g = vector_g[DVB : DVB + 1, :bias_cols]
        peaks = vector_g[PEAK, : size["heads"]]
        clipped_query = weight_g[:, edges[-1] : edges[-1] + columns]
        clipped_key = weight_g[:, edges[-1] + columns :]
        clipped_bias = vector_g[PEAK + 1 : PEAK + 2, :bias_cols]
    else:
        mine = vector_g[:DUB]
        mine = lax.psum(mine, "mp")
        mine = lax.psum_scatter(mine, "dp", scatter_dimension=1, tiled=True)
        up_bias_g = lax.psum_scatter(vector_g[DUB], "dp", scatter_dimension=0, tiled=True)
        vectors = [mine[row] for row in range(6)] + [up_bias_g]
        both = vector_g[DQB : DVB + 1, :TILE]
        both = lax.psum_scatter(both, "dp", scatter_dimension=1, tiled=True)
        query_bias_g, value_bias_g = both[0:1], both[1:2]
        peaks = lax.pmax(vector_g[PEAK, : size["heads"]], "dp")
        head_root = jnp.sqrt(clip_tau / jnp.maximum(peaks, clip_tau))
        column_root = jnp.repeat(head_root, HD)
        clipped_query = query_weight.astype(F32) * column_root[None, :]
        clipped_key = key_weight.astype(F32) * column_root[None, :]
        bias_root = lax.dynamic_slice(column_root, (dp_at * bias_cols,), (bias_cols,))
        clipped_bias = query_bias.astype(F32) * bias_root[None, :]
    return (
        rows_g[0],
        rows_g[1],
        vectors[DG1],
        vectors[DS1],
        query_g,
        query_bias_g,
        key_g,
        value_g,
        value_bias_g,
        out_g,
        vectors[DOB],
        vectors[DG2],
        vectors[DS2],
        up_g,
        vectors[DUB][None, :],
        down_g,
        vectors[DDB],
        peaks,
        clipped_query,
        clipped_key,
        clipped_bias,
    )


def solution(mesh):
    rows = P(None, "dp", "mp", None)
    wide, small, bias = P("dp", "mp"), P("dp"), P("mp", "dp")
    return jax.shard_map(
        on_device,
        mesh=mesh,
        in_specs=(
            rows,
            P(None, "dp"),
            small,
            small,
            wide,
            bias,
            wide,
            wide,
            bias,
            wide,
            small,
            small,
            small,
            wide,
            bias,
            wide,
            small,
            P(),
            rows,
        ),
        out_specs=(
            rows,
            rows,
            small,
            small,
            wide,
            bias,
            wide,
            wide,
            bias,
            wide,
            small,
            small,
            small,
            wide,
            bias,
            wide,
            small,
            P("mp"),
            wide,
            wide,
            bias,
        ),
        check_vma=False,
    )
```

```python
import functools
import math

import jax
import jax.numpy as jnp
from jax import lax
from jax.experimental import pallas as pl
from jax.experimental.pallas import tpu as pltpu
from jax.sharding import PartitionSpec as P

HD = 64
IMG_LEN = 577
F32 = jnp.float32
BF16 = jnp.bfloat16
MESH = pl.DeviceIdType.MESH
TILE = 256
PQ, PK, PV, PO = 0, 1, 2, 3
PAIR_FIRST = (6, 9)
LINE_FIRST = (4, 5)
DIRECT = (0, 1, 2)
G1, S1, OB, G2, S2, DB, UB, QB, VB = 0, 1, 2, 3, 4, 5, 6, 8, 9
DG1, DS1, DOB, DG2, DS2, DDB, DUB, DQB, DVB, PEAK = 0, 1, 2, 3, 4, 5, 6, 7, 8, 9


def dot_nn(left, right):
    return lax.dot_general(left, right, (((1,), (0,)), ((), ())), preferred_element_type=F32)


def dot_nt(left, right):
    return lax.dot_general(left, right, (((1,), (1,)), ((), ())), preferred_element_type=F32)


def dot_tn(left, right):
    return lax.dot_general(left, right, (((0,), (0,)), ((), ())), preferred_element_type=F32)


def standardize(rows):
    center = rows - jnp.mean(rows, axis=-1, keepdims=True)
    inverse = lax.rsqrt(jnp.mean(center * center, axis=-1, keepdims=True) + 1e-05)
    return center * inverse, inverse


def norm_back(incoming, scaled, inverse, gain):
    upward = incoming * gain
    return inverse * (
        upward
        - jnp.mean(upward, axis=-1, keepdims=True)
        - scaled * jnp.mean(upward * scaled, axis=-1, keepdims=True)
    )


def each(low, high, body):
    if high - low <= 8:
        for at in range(low, high):
            body(at)
    else:

        def step(at, carry):
            body(at)
            return carry

        lax.fori_loop(low, high, step, 0)


def tiles(width, body):
    def step(at, carry):
        body(2 * at)
        body(2 * at + 1)
        return carry

    lax.fori_loop(0, width // (2 * TILE), step, 0)


def sum_rows(rows):
    return jnp.sum(rows, axis=0, keepdims=True)


class Layer:
    def __init__(self, size, refs):
        self.__dict__.update(size)
        self.__dict__.update(refs)
        self.dp_at = lax.axis_index("dp")
        self.mp_at = lax.axis_index("mp")
        self.line_at = self.dp_at // 2
        self.pair_at = lax.rem(self.dp_at, 2)
        self.chip_at = self.mp_at // 2
        self.core_at = lax.rem(self.mp_at, 2)
        self.sib = (self.dp_at, self.chip_at * 2 + 1 - self.core_at)
        self.across = (self.dp_at, (1 - self.chip_at) * 2 + self.core_at)
        self.pair = (self.line_at * 2 + 1 - self.pair_at, self.mp_at)
        self.middle = (self.line_at == 1) | (self.line_at == 2)
        self.pieces = 4 + 2 * self.chunks
        self.pair_first = PAIR_FIRST if self.lines == 4 else ()
        self.line_first = LINE_FIRST if self.lines == 4 else ()
        self.pair_slots = (self.pieces - len(self.line_first)) * self.lines
        self.rest = None
        self.stage_sends = [[], []]
        self.spread_sends = [[], [], [], []]
        self.late = []

    def line_of(self, step):
        return lax.rem(self.line_at + step + self.lines, self.lines)

    def line_peer(self, step):
        return (self.line_of(step) * 2 + self.pair_at, self.mp_at)

    def slot(self, line, pair):
        return pl.ds(pl.multiple_of((line * 2 + pair) * self.shard, self.shard), self.shard)

    def block(self, micro, chip, core):
        start = micro * self.rows + (chip * 2 + core) * self.pad
        return pl.ds(pl.multiple_of(start, 16), self.pad)

    def own_block(self, micro):
        return self.block(micro, self.chip_at, self.core_at)

    def source(self, piece):
        if piece < 4:
            return (self.query_w, self.key_w, self.value_w, self.out_w)[piece]
        which, chunk = (piece - 4) % 2, (piece - 4) // 2
        return (self.up_w, self.down_w)[which].at[:, pl.ds(chunk * TILE, TILE)]

    def copy(self, src, dst, send_sem, recv_sem, device):
        return pltpu.make_async_remote_copy(
            src_ref=src,
            dst_ref=dst,
            send_sem=send_sem,
            recv_sem=recv_sem,
            device_id=device,
            device_id_type=MESH,
        )

    def channels(self, piece):
        if piece in self.pair_first:
            return ((piece, False), (self.pieces + self.pair_first.index(piece), True))
        return ((piece, False),)

    def shard_place(self, piece, line, other):
        pair = 1 - self.pair_at if other else self.pair_at
        return self.weights.at[piece, self.slot(line, pair)]

    def broad(self, piece, channel, other, step):
        place = self.shard_place(piece, self.line_at, other)
        return self.copy(
            place if other else self.source(piece),
            place,
            self.wz_send.at[channel, step - 1],
            self.wz_recv.at[channel, step - 1],
            self.line_peer(step),
        )

    def broad_in(self, piece, channel, other, step):
        place = self.shard_place(piece, self.line_of(-step), other)
        return self.copy(
            place,
            place,
            self.wz_send.at[channel, step - 1],
            self.wz_recv.at[channel, step - 1],
            self.line_peer(-step),
        )

    def broad_each(self, piece, channel, other, act):
        def one(step):
            if self.lines == 4 and step != 2:
                @pl.when(self.line_at != (3 if step == 1 else 0))
                def _():
                    act(self.broad(piece, channel, other, step))
            else:
                act(self.broad(piece, channel, other, step))

        each(1, self.lines, one)

    def relay(self, piece, channel, other, act):
        if self.lines != 4:
            return

        @pl.when(self.middle)
        def _():
            place = self.shard_place(piece, 3 * (2 - self.line_at), other)
            end = (3 * (self.line_at - 1) * 2 + self.pair_at, self.mp_at)
            act(
                self.copy(
                    place,
                    place,
                    self.wz_send.at[channel, 3],
                    self.wz_recv.at[channel, 2 * (self.line_at - 1)],
                    end,
                )
            )

    def weight_pair(self, piece, step, own):
        place = self.shard_place(piece, self.line_of(-step), False)
        return self.copy(
            self.source(piece) if own else place,
            place,
            self.wx_send.at[piece, step],
            self.wx_recv.at[piece, step],
            self.pair,
        )

    def weight_pair_in(self, piece, step):
        place = self.shard_place(piece, self.line_of(-step), True)
        return self.copy(
            place, place, self.wx_send.at[piece, step], self.wx_recv.at[piece, step], self.pair
        )

    def weight_local(self, piece):
        return pltpu.make_async_copy(
            self.source(piece),
            self.shard_place(piece, self.line_at, False),
            self.wl_sem.at[piece],
        )

    def send_pair(self, piece):
        self.weight_pair(piece, 0, True).start()

    def send_weight(self, piece, pair=True):
        if pair:
            self.send_pair(piece)
        self.broad_each(piece, piece, False, lambda one: one.start())
        self.weight_local(piece).start()

    def pass_weight(self, piece):
        self.flush()
        if piece in self.pair_first:
            self.weight_pair_in(piece, 0).wait_recv()
            channel, other = self.channels(piece)[1]
            self.broad_each(piece, channel, other, lambda one: one.start())
            return

        def one(step, last=False):
            self.broad_in(piece, piece, False, step).wait_recv()
            if last:
                self.relay(piece, piece, False, lambda one: one.start())
            self.weight_pair(piece, step, False).start()

        if self.lines == 4:
            second = jnp.where(self.line_at < 2, 3, 1)
            one(2, True)
            one(second)
            self.rest = lambda: one(4 - second)
        else:
            each(1, self.lines, one)

    def flush(self):
        if self.rest is not None:
            self.rest()
        self.rest = None

    def relay_weight(self, piece):
        for channel, other in self.channels(piece):
            if piece in self.pair_first:
                self.broad_in(piece, channel, other, 2).wait_recv()
                self.relay(piece, channel, other, lambda one: one.start())

    def await_weight(self, piece):
        self.weight_local(piece).wait()
        if piece in self.pair_first:
            for channel, other in self.channels(piece):
                for step in (1, 3):
                    self.broad_in(piece, channel, other, step).wait_recv()
        else:
            each(0, self.lines, lambda step: self.weight_pair_in(piece, step).wait_recv())

    def weight_sent(self, piece):
        self.weight_pair(piece, 0, True).wait_send()
        for channel, other in self.channels(piece):
            self.broad_each(piece, channel, other, lambda one: one.wait_send())
            self.relay(piece, channel, other, lambda one: one.wait_send())
        if piece not in self.pair_first:
            each(1, self.lines, lambda step: self.weight_pair(piece, step, False).wait_send())

    def spread_copy(self, kind, micro, ref, which):
        place = ref.at[self.own_block(micro)]
        if which == 2:
            place = ref.at[self.block(micro, 1 - self.chip_at, self.core_at)]
        return self.copy(
            place,
            place,
            self.ag_send.at[kind, micro, which],
            self.ag_recv.at[kind, micro, which],
            self.across if which == 0 else self.sib,
        )

    def spread_in(self, kind, micro, ref, which):
        chip = self.chip_at if which == 1 else 1 - self.chip_at
        core = self.core_at if which == 0 else 1 - self.core_at
        place = ref.at[self.block(micro, chip, core)]
        return self.copy(
            place,
            place,
            self.ag_send.at[kind, micro, which],
            self.ag_recv.at[kind, micro, which],
            self.across if which == 0 else self.sib,
        )

    def spread(self, kind, micro, ref):
        for which in (0, 1):
            one = self.spread_copy(kind, micro, ref, which)
            one.start()
            self.spread_sends[kind].append(one)

    def spread_on(self, kind, micro, ref):
        self.spread_in(kind, micro, ref, 0).wait_recv()
        one = self.spread_copy(kind, micro, ref, 2)
        one.start()
        self.spread_sends[kind].append(one)

    def spread_sent(self, kind):
        for one in self.spread_sends[kind]:
            one.wait_send()
        self.spread_sends[kind] = []

    def spread_end(self, kind, micro, ref):
        self.spread_in(kind, micro, ref, 1).wait_recv()
        self.spread_in(kind, micro, ref, 2).wait_recv()

    def collect(self, kind, micro, terms):
        for one in self.stage_sends[micro]:
            one.wait_send()
        self.stage_sends[micro] = []
        held = 1 if kind == 1 else 0
        for half, chip in ((0, 1 - self.chip_at), (1, self.chip_at)):
            start = pl.multiple_of(micro * self.rows + chip * 2 * self.pad, 16)
            stage, keep = self.stage.at[micro, half], self.keep.at[held, micro, half]

            def tile_of(tile):
                cols = pl.ds(pl.multiple_of(tile * TILE, TILE), TILE)
                product = terms(pl.ds(start, 2 * self.pad), cols)
                low, high = product[: self.pad], product[self.pad :]
                keep[:, cols] = jnp.where(self.core_at == 0, low, high)
                stage[:, cols] = jnp.where(self.core_at == 0, high, low).astype(BF16)

            tiles(self.width, tile_of)
            one = self.copy(
                stage,
                self.sib_in.at[kind, micro, half],
                self.rs_send.at[kind, micro, half],
                self.rs_recv.at[kind, micro, half],
                self.sib,
            )
            one.start()
            self.stage_sends[micro].append(one)

    def collect_far(self, kind, micro):
        incoming = self.sib_in.at[kind, micro, 0]
        self.copy(
            incoming,
            incoming,
            self.rs_send.at[kind, micro, 0],
            self.rs_recv.at[kind, micro, 0],
            self.sib,
        ).wait_recv()
        held = self.keep[1 if kind == 1 else 0, micro, 0]
        incoming[...] = (held + incoming[...].astype(F32)).astype(BF16)
        one = self.copy(
            incoming,
            self.far_in.at[kind, micro],
            self.rs_send.at[kind, micro, 2],
            self.rs_recv.at[kind, micro, 2],
            self.across,
        )
        one.start()
        self.late.append(one)

    def collected(self, kind, micro):
        near, far = self.sib_in.at[kind, micro, 1], self.far_in.at[kind, micro]
        self.copy(
            near, near, self.rs_send.at[kind, micro, 1], self.rs_recv.at[kind, micro, 1], self.sib
        ).wait_recv()
        self.copy(
            far, far, self.rs_send.at[kind, micro, 2], self.rs_recv.at[kind, micro, 2], self.across
        ).wait_recv()
        total = self.keep[1 if kind == 1 else 0, micro, 1] + near[...].astype(F32)
        return (total + far[...].astype(F32))[: self.part]

    def summed(self, piece):
        if piece < 4:
            return self.proj_back.at[: self.width, piece * TILE : (piece + 1) * TILE]
        return self.wide_sums.at[piece - 4]

    def sum_place(self, piece, line, other):
        pair = 1 - self.pair_at if other else self.pair_at
        return self.summed(piece).at[self.slot(line, pair)]

    def sum_channels(self, piece):
        if piece in self.line_first:
            return ((piece, False), (self.pieces + self.line_first.index(piece), True))
        return ((piece, False),)

    def relayed(self, piece):
        return self.lines == 4 and piece not in DIRECT

    def out_columns(self, piece):
        at = piece if piece < 4 else 4 + self.chunks * ((piece - 4) % 2) + (piece - 4) // 2
        return self.weight_g.at[:, pl.ds(at * TILE, TILE)]

    def pair_place(self, piece, line):
        if piece in self.line_first:
            return self.pair_in.at[self.pair_slots + self.line_first.index(piece)]
        before = sum(1 for other in self.line_first if other < piece)
        return self.pair_in.at[(piece - before) * self.lines + line]

    def grad_pair(self, piece, line):
        at = 0 if piece in self.line_first else line
        return self.copy(
            self.sum_place(piece, line, True),
            self.pair_place(piece, line),
            self.gx_send.at[piece, at],
            self.gx_recv.at[piece, at],
            self.pair,
        )

    def line_source(self, piece, line, other):
        if piece in self.line_first:
            return self.sum_place(piece, line, other)
        return self.pair_place(piece, line)

    def grad_line(self, piece, channel, other, step):
        line = self.line_of(step)
        target, at = line, step - 1
        if self.relayed(piece) and step != 2:
            far = self.line_at == (3 if step == 1 else 0)
            target = jnp.where(far, 2 if step == 1 else 1, line)
            at = jnp.where(far, 3, step - 1)
        return self.copy(
            self.line_source(piece, line, other),
            self.line_in.at[channel, at],
            self.gz_send.at[channel, step - 1],
            self.gz_recv.at[channel, at],
            (target * 2 + self.pair_at, self.mp_at),
        )

    def grad_line_in(self, channel, at):
        place = self.line_in.at[channel, at]
        return self.copy(
            place, place, self.gz_send.at[channel, 0], self.gz_recv.at[channel, at], self.pair
        )

    def grad_make(self, piece, left, right):
        out = self.summed(piece)

        def one(tile):
            cols = pl.ds(pl.multiple_of(tile * TILE, TILE), TILE)
            out[cols, :] = dot_tn(left[:, cols], right).astype(BF16)

        tiles(self.width, one)
        self.grad_send(piece)

    def grad_send(self, piece):
        if piece in self.line_first:
            for channel, other in self.sum_channels(piece):
                for step in (1, 3):
                    self.grad_line(piece, channel, other, step).start()

                @pl.when(jnp.logical_not(self.middle))
                def _():
                    self.grad_line(piece, channel, other, 2).start()
        else:
            each(0, self.lines, lambda line: self.grad_pair(piece, line).start())

    def grad_pass(self, piece):
        def one(step, wait=True):
            line = self.line_of(step)
            if wait:
                self.grad_pair(piece, line).wait_recv()
            ref = self.pair_place(piece, line)
            total = self.sum_place(piece, line, False)[...].astype(F32) + ref[...].astype(F32)
            ref[...] = total.astype(BF16)
            self.grad_line(piece, piece, False, step).start()

        if piece in self.line_first:
            return
        if self.relayed(piece):
            one(1)
            one(3)
            self.grad_pair(piece, self.line_of(2)).wait_recv()
            pl.when(jnp.logical_not(self.middle))(lambda: one(2, False))
        else:
            each(1, self.lines, one)

    def grad_relay(self, piece):
        if not self.relayed(piece):
            return

        @pl.when(self.middle)
        def _():
            for channel, other in self.sum_channels(piece):
                line = self.line_of(2)
                self.grad_line_in(channel, 3).wait_recv()
                ref = self.line_source(piece, line, other)
                total = ref[...].astype(F32) + self.line_in[channel, 3].astype(F32)
                if piece not in self.line_first:
                    total = total + self.sum_place(piece, line, False)[...].astype(F32)
                ref[...] = total.astype(BF16)
                self.grad_line(piece, channel, other, 2).start()

    def line_total(self, piece, channel, ref):
        for step in range(1, self.lines):

            def one():
                self.grad_line_in(channel, step - 1).wait_recv()
                ref[...] += self.line_in[channel, step - 1].astype(F32)

            if self.relayed(piece) and step != 2:
                pl.when(self.line_at != (0 if step == 1 else 3))(one)
            else:
                one()

    def grad_cross(self, piece):
        if piece not in self.line_first:
            return
        ref = self.sum_place(piece, self.line_at, True)
        total = self.out_columns(piece)
        total[...] = ref[...].astype(F32)
        self.line_total(piece, self.sum_channels(piece)[1][0], total)
        ref[...] = total[...].astype(BF16)
        self.grad_pair(piece, self.line_at).start()

    def grad_end(self, piece):
        ref = self.out_columns(piece)
        self.grad_pair(piece, self.line_at).wait_recv()
        came = self.pair_place(piece, self.line_at)[...].astype(F32)
        ref[...] = self.sum_place(piece, self.line_at, False)[...].astype(F32) + came
        self.line_total(piece, piece, ref)

    def grad_sent(self, piece):
        if piece in self.line_first:
            self.grad_pair(piece, self.line_at).wait_send()
        else:
            each(0, self.lines, lambda line: self.grad_pair(piece, line).wait_send())
        for channel, other in self.sum_channels(piece):
            each(
                1,
                self.lines,
                lambda step: self.grad_line(piece, channel, other, step).wait_send(),
            )

    def clip(self, peaks):
        root = jnp.sqrt(self.tau[0, 0] / jnp.maximum(peaks, self.tau[0, 0]))
        head = lax.broadcasted_iota(jnp.int32, (1, TILE), 1) // HD
        roots = jnp.zeros((1, TILE), F32)
        for at in range(self.heads):
            roots = jnp.where(head == at, root[:, at : at + 1], roots)
        first = (4 + 2 * self.chunks) * TILE
        mine = self.slot(self.line_at, self.pair_at)
        for at, piece in enumerate((PQ, PK)):
            cols = slice(first + at * TILE, first + (at + 1) * TILE)
            self.weight_g[:, cols] = self.weights[piece, mine, :].astype(F32) * roots
        low, high = self.own_packed[8:9, :], self.own_packed[9:10, :]
        bias = low * roots[:, 0:128] + high * roots[:, 128:256]
        return bias

    def vector_copy(self, step):
        return self.copy(
            self.own_packed,
            self.vectors_in.at[self.dp_at],
            self.v_send.at[0, step - 1],
            self.v_recv.at[0, step - 1],
            (lax.rem(self.dp_at + step, self.dps), self.mp_at),
        )

    def vector_copy_in(self, step):
        origin = lax.rem(self.dp_at - step + self.dps, self.dps)
        place = self.vectors_in.at[origin]
        return self.copy(
            place,
            place,
            self.v_send.at[0, step - 1],
            self.v_recv.at[0, step - 1],
            (origin, self.mp_at),
        )

    def share_copy(self, step):
        target = lax.rem(self.dp_at + step, self.dps)
        return self.copy(
            self.shares.at[target],
            self.shares_in.at[step - 1],
            self.v_send.at[1, step - 1],
            self.v_recv.at[1, step - 1],
            (target, self.mp_at),
        )

    def group_copy(self, step):
        return self.copy(
            self.group.at[0],
            self.group.at[step],
            self.m_send.at[step - 1],
            self.m_recv.at[step - 1],
            (self.dp_at, lax.rem(self.mp_at + step, 4)),
        )

    def pack_vectors(self):
        if not self.own_vectors:
            return
        rows = [ref[...].astype(F32) for ref in self.small[:7]] + [jnp.zeros((1, 128), F32)]
        shift = lax.rem(self.dp_at * 32, 128)
        for ref in self.small[7:]:
            wide = jnp.concatenate([ref[...].astype(F32), jnp.zeros((1, 96), F32)], axis=1)
            wide = pltpu.roll(wide, shift, 1)
            rows.append(jnp.where(self.dp_at < 4, wide, 0.0))
            rows.append(jnp.where(self.dp_at < 4, 0.0, wide))
        self.own_packed[...] = jnp.concatenate(rows + [jnp.zeros((4, 128), F32)], axis=0)

    def take_vectors(self):
        if not self.own_vectors:
            self.vectors[...] = self.small[0][...]
            return
        self.vectors_in[self.dp_at] = self.own_packed[...]
        for step in range(1, self.dps):
            self.vector_copy_in(step).wait_recv()
        rest = self.vectors_in[0, 8:16, :]
        for at in range(1, self.dps):
            rest = rest + self.vectors_in[at, 8:16, :]
        for at in range(self.dps):
            self.vectors[0:8, at * 128 : (at + 1) * 128] = self.vectors_in[at, 0:8, :]
        for row, first in ((QB, 0), (VB, 2)):
            self.vectors[row : row + 1, 0:128] = rest[first : first + 1]
            self.vectors[row : row + 1, 128:256] = rest[first + 1 : first + 2]

    def give_vectors(self):
        if not self.own_vectors:
            self.vector_g[...] = self.sums[...]
            return
        for at in range(self.dps):
            half = (at * 32 // 128) * 128
            self.shares[at, 0:7, :] = self.sums[0:7, at * 128 : (at + 1) * 128]
            self.shares[at, 7:9, :] = self.sums[7:9, half : half + 128]
            self.shares[at, 9:16, :] = self.sums[9:16, 0:128]
        for step in range(1, self.dps):
            self.share_copy(step).start()

    def end_vectors(self):
        if not self.own_vectors:
            return
        total = self.shares[self.dp_at]
        most = total[PEAK : PEAK + 1]
        for step in range(1, self.dps):
            self.share_copy(step).wait_recv()
            came = self.shares_in[step - 1]
            total = total + came
            most = jnp.maximum(most, came[PEAK : PEAK + 1])
        self.group[0] = jnp.concatenate([total[:PEAK], most, total[PEAK + 1 :]], axis=0)
        for step in range(1, 4):
            self.group_copy(step).start()

    def last_vectors(self):
        if not self.own_vectors:
            return
        total = self.group[0]
        most = total[PEAK : PEAK + 1]
        whole = total[0:6]
        for step in range(1, 4):
            self.group_copy(step).wait_recv()
            whole = whole + self.group[step, 0:6, :]
        narrow = jnp.concatenate([total[7:9], self.clip(most), jnp.zeros((5, 128), F32)], axis=0)
        shift = lax.rem(128 - lax.rem(self.dp_at * 32, 128), 128)
        narrow = pltpu.roll(narrow, shift, 1)
        self.vector_g[0:6, :] = whole
        self.vector_g[6:7, :] = total[6:7]
        self.vector_g[7:9, :] = narrow[0:2]
        self.vector_g[9:10, :] = most
        self.vector_g[10:11, :] = narrow[2:3]
        self.vector_g[11:16, :] = jnp.zeros((5, 128), F32)

    def vector(self, row, start=0, size=None):
        size = self.width if size is None else size
        return self.vectors[row : row + 1, pl.ds(start, size)]

    def add_sum(self, row, value, start=0):
        cols = pl.ds(start, value.shape[1])
        self.sums[row : row + 1, cols] = self.sums[row : row + 1, cols] + value

    def mask(self, micro):
        row = self.mp_at * self.part + lax.broadcasted_iota(jnp.int32, (self.part, 1), 0)
        live = jnp.where(self.counts[micro] > 0, 1.0, 0.0).astype(F32)
        return jnp.where(row < IMG_LEN, live, 0.0)

    def put_rows(self, ref, micro, rows):
        filler = jnp.zeros((self.pad - self.part, self.width), F32)
        ref[self.own_block(micro), :] = jnp.concatenate([rows, filler], axis=0).astype(BF16)

    def first_norm(self, micro):
        scaled, _ = standardize(self.images[micro, 0].astype(F32))
        self.put_rows(self.normed_one, micro, scaled * self.vector(G1) + self.vector(S1))
        self.spread(0, micro, self.normed_one)

    def out_rows(self, micro):
        return self.out_grad[micro, 0].astype(F32) * self.mask(micro)

    def project_back(self, micro):
        rows = self.out_rows(micro)
        self.put_rows(self.proj_back, micro, rows)
        self.add_sum(DDB, sum_rows(rows.astype(BF16).astype(F32)))
        self.spread(2, micro, self.proj_back)

    def second_norm(self, micro):
        rows = self.images[micro, 0].astype(F32) + self.collected(0, micro) + self.vector(OB)
        self.after_attn[micro] = rows
        scaled, _ = standardize(rows)
        self.put_rows(self.normed_two, micro, scaled * self.vector(G2) + self.vector(S2))
        self.spread(1, micro, self.normed_two)

    def give_result(self, micro):
        rows = self.after_attn[micro] + self.collected(1, micro) + self.vector(DB)
        self.rows_g[0, micro, 0] = (self.mask(micro) * rows).astype(BF16)

    def second_norm_back(self, micro):
        incoming = self.collected(2, micro)
        scaled, inverse = standardize(self.after_attn[micro])
        rows = self.out_rows(micro) + norm_back(incoming, scaled, inverse, self.vector(G2))
        self.attn_back[micro] = rows
        self.add_sum(DOB, sum_rows(rows.astype(BF16).astype(F32)))
        self.add_sum(DG2, sum_rows(incoming * scaled))
        self.add_sum(DS2, sum_rows(incoming))
        self.put_rows(self.attended_back, micro, rows)
        self.spread(3, micro, self.attended_back)

    def first_norm_back(self, micro):
        incoming = self.collected(3, micro)
        scaled, inverse = standardize(self.images[micro, 0].astype(F32))
        self.add_sum(DG1, sum_rows(incoming * scaled))
        self.add_sum(DS1, sum_rows(incoming))
        rows = self.attn_back[micro] + norm_back(incoming, scaled, inverse, self.vector(G1))
        self.rows_g[1, micro, 0] = rows.astype(BF16)

    def image_rows(self, micro):
        return pl.ds(micro * self.rows, self.rows)

    def counted(self, axis):
        shape = (self.rows, 1) if axis == 0 else (1, self.rows)
        row = lax.broadcasted_iota(jnp.int32, shape, axis)
        block = row // self.pad
        inside = row - block * self.pad
        return (inside < self.part) & (block * self.part + inside < IMG_LEN)

    def head_columns(self, head):
        column = lax.broadcasted_iota(jnp.int32, (self.rows, TILE), 1)
        return column // HD == head

    def project_heads(self, micro):
        rows = self.image_rows(micro)
        normed = self.normed_one[rows, :]
        scale = 1.0 / math.sqrt(HD)
        query = dot_nn(normed, self.weights[PQ]) + self.vector(QB, 0, TILE)
        self.queries[rows, :] = (query.astype(BF16).astype(F32) * scale).astype(BF16)
        self.keys[rows, :] = dot_nn(normed, self.weights[PK]).astype(BF16)
        value = dot_nn(normed, self.weights[PV]) + self.vector(VB, 0, TILE)
        self.values[rows, :] = value.astype(BF16)

    def attend(self, micro, between):
        rows = self.image_rows(micro)
        values = self.turned.at[:, : self.rows]
        values[...] = self.values[rows, :].T
        live = jnp.where(self.counts[micro] > 0, 0.0, -1e30).astype(F32)
        split = (self.rows // 2 + 127) // 128 * 128

        def one_head(head, carry):
            pl.when(head == self.heads // 2)(between)
            query = jnp.where(self.head_columns(head), self.queries[rows, :], jnp.zeros((), BF16))
            cols = pl.ds(pl.multiple_of(head * HD, HD), HD)
            top = total = mixed = None
            for low, high in ((0, split), (split, self.rows)):
                part = pl.ds(micro * self.rows + low, high - low)
                scores = dot_nt(self.keys[part, :], query)
                scores = jnp.where(self.counted(0)[low:high], scores, -1e30)
                most = jnp.max(scores, axis=0, keepdims=True)
                if top is None:
                    expo = jnp.exp(scores - most)
                    total = jnp.sum(expo, axis=0, keepdims=True)
                    mixed = dot_nn(values[cols, low:high], expo.astype(BF16))
                    top = most
                else:
                    most = jnp.maximum(top, most)
                    again = jnp.exp(top - most)
                    expo = jnp.exp(scores - most)
                    total = total * again + jnp.sum(expo, axis=0, keepdims=True)
                    added = dot_nn(values[cols, low:high], expo.astype(BF16))
                    mixed = mixed * again + added
                    top = most
            self.log_total[micro, pl.ds(head, 1), :] = top + jnp.log(total)
            self.mixed_turned[micro, cols, :] = mixed * (1.0 / total)
            peak = jnp.max(jnp.where(self.counted(1), top, -1e30), axis=1, keepdims=True)
            peak = jnp.where(live < 0.0, -1e30, peak)
            lane = lax.broadcasted_iota(jnp.int32, (1, 128), 1)
            seen = self.sums[PEAK : PEAK + 1, 0:128]
            self.sums[PEAK : PEAK + 1, 0:128] = jnp.where(
                lane == head, jnp.maximum(seen, peak), seen
            )
            return carry

        lax.fori_loop(0, self.heads, one_head, 0)
        self.mixed[rows, :] = self.mixed_turned[micro].T.astype(BF16)

    def attend_back(self, micro, between):
        rows = self.image_rows(micro)
        self.mixed_back[...] = dot_nn(self.attended_back[rows, :], self.weights[PO]).astype(BF16)
        keys = self.turned.at[:, : self.rows]
        outwards = self.turned.at[:, self.rows :]
        keys[...] = self.keys[rows, :].T
        outwards[...] = self.mixed_back[...].T
        self.key_sum[...] = jnp.zeros_like(self.key_sum)
        self.value_sum[...] = jnp.zeros_like(self.value_sum)
        chunk = self.rows // 2

        def one_head(head, carry):
            pl.when(head == self.heads // 2)(between)
            columns = self.head_columns(head)
            none = jnp.zeros((), BF16)
            query = jnp.where(columns, self.queries[rows, :], none)
            outward = jnp.where(columns, self.mixed_back[...], none)
            cols = pl.ds(pl.multiple_of(head * HD, HD), HD)
            dots = outwards[cols, :].astype(F32) * self.mixed_turned[micro, cols, :]
            delta = jnp.sum(dots, axis=0, keepdims=True)
            log_total = self.log_total[micro, pl.ds(head, 1), :]
            for at in range(2):
                part = pl.ds(micro * self.rows + at * chunk, chunk)
                here = pl.ds(at * chunk, chunk)
                scores = dot_nt(self.keys[part, :], query)
                counted = self.counted(0)[at * chunk : (at + 1) * chunk]
                probs = jnp.where(counted, jnp.exp(scores - log_total), 0.0)
                prob_back = dot_nt(self.values[part, :], outward)
                self.probs[here, :] = probs.astype(BF16)
                self.score_back[here, :] = (probs * (prob_back - delta)).astype(BF16)
            self.value_sum[...] += dot_nn(self.probs[...], outward)
            self.key_sum[...] += dot_nn(self.score_back[...], query)
            self.mixed_turned[micro, cols, :] = dot_nn(keys[cols, :], self.score_back[...])
            return carry

        lax.fori_loop(0, self.heads, one_head, 0)
        scale = 1.0 / math.sqrt(HD)
        query_back = (self.mixed_turned[micro] * scale).T.astype(BF16)
        value_back = self.value_sum[...].astype(BF16)
        self.queries[rows, :] = query_back
        self.keys[rows, :] = self.key_sum[...].astype(BF16)
        self.values[rows, :] = value_back
        self.add_sum(DQB, sum_rows(query_back.astype(F32)))
        self.add_sum(DVB, sum_rows(value_back.astype(F32)))

    def feed(self, micro, chunk):
        cols = pl.ds(chunk * TILE, TILE)
        up, down = self.weights.at[4 + 2 * chunk], self.weights.at[5 + 2 * chunk]
        part = self.rows // 2
        total = jnp.zeros((1, TILE), F32)
        for at in range(2):
            rows = pl.ds(micro * self.rows + at * part, part)
            hidden = dot_nn(self.normed_two[rows, :], up[...])
            hidden = hidden + self.vector(UB, chunk * TILE, TILE)
            gate = jax.nn.sigmoid(1.702 * hidden)
            self.activated[rows, cols] = (hidden * gate).astype(BF16)
            back = dot_nn(self.proj_back[rows, :], down[...])
            back = back * (gate + 1.702 * hidden * gate * (1.0 - gate))
            back = back.astype(BF16)
            self.pre_back[rows, cols] = back
            total = total + sum_rows(back.astype(F32))
        self.add_sum(DUB, total, chunk * TILE)

    def out_terms(self, rows, cols):
        return dot_nt(self.mixed[rows, :], self.weights[PO, cols, :])

    def wide_terms(self, ref, first):
        def terms(rows, cols):
            total = None
            for chunk in range(self.chunks):
                one = dot_nt(
                    ref[rows, chunk * TILE : (chunk + 1) * TILE],
                    self.weights[first + 2 * chunk, cols, :],
                )
                total = one if total is None else total + one
            return total

        return terms

    def input_terms(self, rows, cols):
        total = dot_nt(self.queries[rows, :], self.weights[PQ, cols, :])
        total = total + dot_nt(self.keys[rows, :], self.weights[PK, cols, :])
        return total + dot_nt(self.values[rows, :], self.weights[PV, cols, :])

    def enter(self):
        barrier = pltpu.get_barrier_semaphore()
        peers = [self.sib, self.across]
        if self.own_vectors:
            peers.append((self.dp_at, (1 - self.chip_at) * 2 + 1 - self.core_at))
        for peer in peers:
            pl.semaphore_signal(barrier, inc=1, device_id=peer, device_id_type=MESH)
        if self.own_vectors:

            def hail(step):
                peer = (lax.rem(self.dp_at + step, self.dps), self.mp_at)
                pl.semaphore_signal(barrier, inc=1, device_id=peer, device_id_type=MESH)

            each(1, self.dps, hail)
            pl.semaphore_wait(barrier, 3 + self.dps - 1)
        else:
            pl.semaphore_signal(barrier, inc=1, device_id=self.pair, device_id_type=MESH)

            def hail(step):
                peer = self.line_peer(step)
                pl.semaphore_signal(barrier, inc=1, device_id=peer, device_id_type=MESH)

            each(1, self.lines, hail)
            pl.semaphore_wait(barrier, 2 + self.lines)

    def run(self):
        pieces = self.pieces
        last = self.chunks - 1
        self.pack_vectors()
        self.enter()
        if self.own_vectors:
            for step in range(1, self.dps):
                self.vector_copy(step).start()
        for piece in (PQ, PK, PV):
            self.send_weight(piece)
        self.sums[...] = jnp.zeros_like(self.sums)
        self.sums[PEAK : PEAK + 1, :] = jnp.full((1, self.width), -1e30, F32)
        self.take_vectors()
        for micro in (0, 1):
            self.first_norm(micro)
        self.pass_weight(PQ)
        self.send_weight(PO)
        self.pass_weight(PK)
        self.send_weight(4)
        self.spread_on(0, 0, self.normed_one)
        self.pass_weight(PV)
        self.send_weight(5)
        self.send_pair(6)
        self.send_pair(9)
        self.await_weight(PQ)
        self.spread_on(0, 1, self.normed_one)
        self.project_back(0)
        self.flush()
        self.await_weight(PK)
        self.await_weight(PV)
        self.spread_end(0, 0, self.normed_one)
        self.project_heads(0)
        self.pass_weight(PO)
        self.send_weight(6, False)
        self.attend(0, self.flush)
        self.await_weight(PO)
        self.collect(0, 0, self.out_terms)
        self.collect_far(0, 0)
        self.pass_weight(4)
        self.send_weight(7)
        self.spread_end(0, 1, self.normed_one)
        self.project_heads(1)
        self.spread_on(2, 0, self.proj_back)
        self.pass_weight(5)
        self.send_weight(8)
        self.attend(1, self.flush)
        self.pass_weight(6)
        self.collect(0, 1, self.out_terms)
        self.collect_far(0, 1)
        self.send_weight(9, False)
        self.second_norm(0)
        self.pass_weight(7)
        self.send_weight(10)
        self.relay_weight(6)
        self.pass_weight(8)
        self.send_weight(11)
        self.second_norm(1)
        self.project_back(1)
        self.pass_weight(9)
        self.spread_on(1, 0, self.normed_two)
        self.pass_weight(10)
        self.spread_end(1, 0, self.normed_two)
        self.spread_end(2, 0, self.proj_back)
        self.await_weight(4)
        self.await_weight(5)
        self.feed(0, 0)
        self.await_weight(6)
        self.await_weight(7)
        self.feed(0, 1)
        self.spread_on(1, 1, self.normed_two)
        self.pass_weight(11)
        self.relay_weight(9)
        self.await_weight(8)
        self.await_weight(9)
        self.feed(0, 2)
        self.flush()
        self.spread_on(2, 1, self.proj_back)
        self.await_weight(10)
        self.await_weight(11)
        self.feed(0, last)
        self.collect(2, 0, self.wide_terms(self.pre_back, 4))
        self.collect_far(2, 0)
        self.spread_end(1, 1, self.normed_two)
        self.spread_end(2, 1, self.proj_back)
        for chunk in range(self.chunks):
            self.feed(1, chunk)
        self.collect(2, 1, self.wide_terms(self.pre_back, 4))
        self.collect_far(2, 1)

        def up_grad(chunk):
            cols = slice(chunk * TILE, (chunk + 1) * TILE)
            self.grad_make(4 + 2 * chunk, self.normed_two, self.pre_back[:, cols])

        def down_grad(chunk):
            cols = slice(chunk * TILE, (chunk + 1) * TILE)
            self.grad_make(5 + 2 * chunk, self.proj_back, self.activated[:, cols])

        up_grad(1)
        self.second_norm_back(0)
        up_grad(0)
        down_grad(0)
        down_grad(1)
        up_grad(2)
        self.second_norm_back(1)
        self.grad_pass(6)
        down_grad(2)
        self.spread_on(3, 0, self.attended_back)
        up_grad(3)
        self.grad_pass(7)
        down_grad(3)
        self.spread_end(3, 0, self.attended_back)

        def between_first():
            self.grad_pass(8)
            self.grad_relay(4)

        self.attend_back(0, between_first)
        self.spread_on(3, 1, self.attended_back)
        self.collect(3, 0, self.input_terms)
        self.collect_far(3, 0)
        self.grad_pass(9)
        self.grad_relay(6)
        self.grad_relay(5)
        self.spread_sent(2)
        self.spread_end(3, 1, self.attended_back)
        self.grad_make(PO, self.attended_back, self.mixed[...])

        def between_second():
            self.grad_pass(10)
            self.grad_relay(7)
            self.grad_relay(8)

        self.attend_back(1, between_second)
        self.grad_make(PV, self.normed_one, self.values[...])
        self.grad_make(PQ, self.normed_one, self.queries[...])
        self.grad_make(PK, self.normed_one, self.keys[...])
        self.collect(3, 1, self.input_terms)
        self.collect_far(3, 1)
        self.grad_pass(11)
        self.grad_cross(4)
        self.grad_cross(5)
        self.grad_relay(9)
        self.grad_relay(10)
        self.collect(1, 0, self.wide_terms(self.activated, 5))
        self.collect_far(1, 0)
        self.grad_pass(PO)
        self.first_norm_back(0)
        self.collect(1, 1, self.wide_terms(self.activated, 5))
        self.collect_far(1, 1)
        self.grad_pass(PV)
        self.first_norm_back(1)
        self.give_vectors()
        self.grad_relay(11)
        self.grad_relay(PO)
        for piece in range(4, 10):
            self.grad_end(piece)
        self.grad_pass(PQ)
        self.end_vectors()
        self.grad_pass(PK)
        self.give_result(0)
        self.give_result(1)
        for piece in range(10, pieces):
            self.grad_end(piece)
        self.last_vectors()
        for piece in (PO, PV, PQ, PK):
            self.grad_end(piece)
        for kind in (0, 1, 3):
            self.spread_sent(kind)
        for one in self.late + self.stage_sends[0] + self.stage_sends[1]:
            one.wait_send()
        for piece in range(pieces):
            self.weight_sent(piece)
            self.grad_sent(piece)
        if self.own_vectors:
            for step in range(1, self.dps):
                self.vector_copy(step).wait_send()
                self.share_copy(step).wait_send()
            for step in range(1, 4):
                self.group_copy(step).wait_send()


def layer_kernel(size, names, *refs):
    named = dict(zip(names, refs))
    named["small"] = [named[name] for name in names if name.startswith("small_")]
    Layer(size, named).run()


def fused_layer(size, counts, tau, images, out_grad, small, weights):
    width, shard, part, rows, pad = (size[key] for key in ("width", "shard", "part", "rows", "pad"))
    lines, dps, pieces = size["lines"], size["dps"], 4 + 2 * size["chunks"]
    units = size["chunks"] * TILE
    vmem = pl.BlockSpec(memory_space=pltpu.VMEM)
    anywhere = pl.BlockSpec(memory_space=pl.ANY)
    vector_shape = (16, 128) if size["own_vectors"] else (16, width)
    outputs = {
        "rows_g": ((2,) + images.shape, BF16),
        "weight_g": ((shard, pieces * TILE + 2 * TILE), F32),
        "vector_g": (vector_shape, F32),
    }
    four = lines == 4
    channels = pieces + (len(PAIR_FIRST) if four else 0)
    pair_slots = pieces * lines - (len(LINE_FIRST) * (lines - 1) if four else 0)
    sum_channels = pieces + (len(LINE_FIRST) if four else 0)
    lines_in = 4 if four else lines - 1
    dma = pltpu.SemaphoreType.DMA
    vm = pltpu.VMEM
    scratch = {
        "weights": vm((pieces, width, TILE), BF16),
        "normed_one": vm((2 * rows, width), BF16),
        "normed_two": vm((2 * rows, width), BF16),
        "proj_back": vm((2 * rows, width), BF16),
        "attended_back": vm((2 * rows, width), BF16),
        "queries": vm((2 * rows, TILE), BF16),
        "keys": vm((2 * rows, TILE), BF16),
        "values": vm((2 * rows, TILE), BF16),
        "mixed": vm((2 * rows, TILE), BF16),
        "mixed_turned": vm((2, TILE, rows), F32),
        "log_total": vm((2, size["heads"], rows), F32),
        "activated": vm((2 * rows, units), BF16),
        "pre_back": vm((2 * rows, units), BF16),
        "turned": vm((TILE, 2 * rows), BF16),
        "mixed_back": vm((rows, TILE), BF16),
        "key_sum": vm((rows, TILE), F32),
        "value_sum": vm((rows, TILE), F32),
        "probs": vm((rows, rows), BF16),
        "score_back": vm((rows, rows), BF16),
        "stage": vm((2, 2, pad, width), BF16),
        "keep": vm((2, 2, 2, pad, width), F32),
        "sib_in": vm((4, 2, 2, pad, width), BF16),
        "far_in": vm((4, 2, pad, width), BF16),
        "after_attn": vm((2, part, width), F32),
        "attn_back": vm((2, part, width), F32),
        "wide_sums": vm((pieces - 4, width, TILE), BF16),
        "pair_in": vm((pair_slots, shard, TILE), BF16),
        "line_in": vm((sum_channels, lines_in, shard, TILE), BF16),
        "vectors": vm((16, width), F32),
        "sums": vm((16, width), F32),
        "wz_send": dma((channels, lines_in)),
        "wz_recv": dma((channels, lines - 1)),
        "wx_send": dma((pieces, lines)),
        "wx_recv": dma((pieces, lines)),
        "wl_sem": dma((pieces,)),
        "ag_send": dma((4, 2, 3)),
        "ag_recv": dma((4, 2, 3)),
        "rs_send": dma((4, 2, 3)),
        "rs_recv": dma((4, 2, 3)),
        "gx_send": dma((pieces, lines)),
        "gx_recv": dma((pieces, lines)),
        "gz_send": dma((sum_channels, lines - 1)),
        "gz_recv": dma((sum_channels, lines_in)),
    }
    if size["own_vectors"]:
        scratch |= {
            "own_packed": vm((16, 128), F32),
            "vectors_in": vm((dps, 16, 128), F32),
            "shares": vm((dps, 16, 128), F32),
            "shares_in": vm((dps - 1, 16, 128), F32),
            "group": vm((4, 16, 128), F32),
            "v_send": dma((2, dps - 1)),
            "v_recv": dma((2, dps - 1)),
            "m_send": dma((3,)),
            "m_recv": dma((3,)),
        }
    inputs = ["counts", "tau", "images", "out_grad"] + [f"small_{at}" for at in range(len(small))]
    inputs += ["query_w", "key_w", "value_w", "out_w", "up_w", "down_w"]
    names = inputs + list(outputs) + list(scratch)
    return pl.pallas_call(
        functools.partial(layer_kernel, size, names),
        out_shape=[jax.ShapeDtypeStruct(*spec) for spec in outputs.values()],
        in_specs=[pl.BlockSpec(memory_space=pltpu.SMEM)] * 2
        + [vmem] * (2 + len(small))
        + [anywhere] * 6,
        out_specs=[vmem] * len(outputs),
        scratch_shapes=list(scratch.values()),
        compiler_params=pltpu.CompilerParams(
            collective_id=0, has_side_effects=True, vmem_limit_bytes=65024 * 2**10
        ),
    )(counts, tau, images, out_grad, *small, *weights)


def on_device(
    images,
    counts,
    first_gain,
    first_shift,
    query_weight,
    query_bias,
    key_weight,
    value_weight,
    value_bias,
    out_weight,
    out_bias,
    second_gain,
    second_shift,
    up_weight,
    up_bias,
    down_weight,
    down_bias,
    clip_tau,
    out_grad,
):
    part, width = images.shape[2:]
    dps = lax.axis_size("dp")
    dp_at = lax.axis_index("dp")
    shard = query_weight.shape[0]
    pad = (part + 15) // 16 * 16
    size = {
        "width": width,
        "shard": shard,
        "part": part,
        "pad": pad,
        "rows": pad * lax.axis_size("mp"),
        "dps": dps,
        "lines": dps // 2,
        "heads": query_weight.shape[1] // HD,
        "chunks": up_weight.shape[1] // TILE,
        "own_vectors": shard == 128,
    }
    bias_cols = query_bias.shape[1]
    parts = [first_gain, first_shift, out_bias, second_gain, second_shift, down_bias, up_bias[0]]
    if size["own_vectors"]:
        small = [one.reshape(1, -1) for one in parts] + [query_bias, value_bias]
    else:
        whole = [lax.all_gather(one, "dp", axis=0, tiled=True) for one in parts]
        rest = [
            jnp.pad(lax.all_gather(one[0], "dp", axis=0, tiled=True), (0, width - TILE))
            for one in (query_bias, value_bias)
        ]
        filler = jnp.zeros((width,), BF16)
        small = [jnp.stack(whole + [filler] + rest + [filler] * 6).astype(F32)]
    weights = (query_weight, key_weight, value_weight, out_weight, up_weight, down_weight)
    rows_g, weight_g, vector_g = fused_layer(
        size, counts.reshape(-1), clip_tau.reshape(1, 1), images, out_grad, small, weights
    )
    columns, units = query_weight.shape[1], up_weight.shape[1]
    edges = [0, columns, 2 * columns, 3 * columns, 4 * columns]
    edges += [edges[-1] + units, edges[-1] + 2 * units]
    query_g, key_g, value_g, out_g, up_g, down_g = (
        weight_g[:, low:high] for low, high in zip(edges[:-1], edges[1:])
    )
    if size["own_vectors"]:
        vectors = [vector_g[row] for row in range(7)]
        query_bias_g = vector_g[DQB : DQB + 1, :bias_cols]
        value_bias_g = vector_g[DVB : DVB + 1, :bias_cols]
        peaks = vector_g[PEAK, : size["heads"]]
        clipped_query = weight_g[:, edges[-1] : edges[-1] + columns]
        clipped_key = weight_g[:, edges[-1] + columns :]
        clipped_bias = vector_g[PEAK + 1 : PEAK + 2, :bias_cols]
    else:
        mine = vector_g[:DUB]
        mine = lax.psum(mine, "mp")
        mine = lax.psum_scatter(mine, "dp", scatter_dimension=1, tiled=True)
        up_bias_g = lax.psum_scatter(vector_g[DUB], "dp", scatter_dimension=0, tiled=True)
        vectors = [mine[row] for row in range(6)] + [up_bias_g]
        both = vector_g[DQB : DVB + 1, :TILE]
        both = lax.psum_scatter(both, "dp", scatter_dimension=1, tiled=True)
        query_bias_g, value_bias_g = both[0:1], both[1:2]
        peaks = lax.pmax(vector_g[PEAK, : size["heads"]], "dp")
        head_root = jnp.sqrt(clip_tau / jnp.maximum(peaks, clip_tau))
        column_root = jnp.repeat(head_root, HD)
        clipped_query = query_weight.astype(F32) * column_root[None, :]
        clipped_key = key_weight.astype(F32) * column_root[None, :]
        bias_root = lax.dynamic_slice(column_root, (dp_at * bias_cols,), (bias_cols,))
        clipped_bias = query_bias.astype(F32) * bias_root[None, :]
    return (
        rows_g[0],
        rows_g[1],
        vectors[DG1],
        vectors[DS1],
        query_g,
        query_bias_g,
        key_g,
        value_g,
        value_bias_g,
        out_g,
        vectors[DOB],
        vectors[DG2],
        vectors[DS2],
        up_g,
        vectors[DUB][None, :],
        down_g,
        vectors[DDB],
        peaks,
        clipped_query,
        clipped_key,
        clipped_bias,
    )


def solution(mesh):
    rows = P(None, "dp", "mp", None)
    wide, small, bias = P("dp", "mp"), P("dp"), P("mp", "dp")
    return jax.shard_map(
        on_device,
        mesh=mesh,
        in_specs=(
            rows,
            P(None, "dp"),
            small,
            small,
            wide,
            bias,
            wide,
            wide,
            bias,
            wide,
            small,
            small,
            small,
            wide,
            bias,
            wide,
            small,
            P(),
            rows,
        ),
        out_specs=(
            rows,
            rows,
            small,
            small,
            wide,
            bias,
            wide,
            wide,
            bias,
            wide,
            small,
            small,
            small,
            wide,
            bias,
            wide,
            small,
            P("mp"),
            wide,
            wide,
            bias,
        ),
        check_vma=False,
    )
```

```python
import functools
import math

import jax
import jax.numpy as jnp
from jax import lax
from jax.experimental import pallas as pl
from jax.experimental.pallas import tpu as pltpu
from jax.sharding import PartitionSpec as P

HD = 64
IMG_LEN = 577
F32 = jnp.float32
BF16 = jnp.bfloat16
MESH = pl.DeviceIdType.MESH
TILE = 256
PQ, PK, PV, PO = 0, 1, 2, 3
PAIR_FIRST = (6, 9)
LINE_FIRST = (4, 5)
DIRECT = (0, 1)
G1, S1, OB, G2, S2, DB, UB, QB, VB = 0, 1, 2, 3, 4, 5, 6, 8, 9
DG1, DS1, DOB, DG2, DS2, DDB, DUB, DQB, DVB, PEAK = 0, 1, 2, 3, 4, 5, 6, 7, 8, 9


def dot_nn(left, right):
    return lax.dot_general(left, right, (((1,), (0,)), ((), ())), preferred_element_type=F32)


def dot_nt(left, right):
    return lax.dot_general(left, right, (((1,), (1,)), ((), ())), preferred_element_type=F32)


def dot_tn(left, right):
    return lax.dot_general(left, right, (((0,), (0,)), ((), ())), preferred_element_type=F32)


def standardize(rows):
    center = rows - jnp.mean(rows, axis=-1, keepdims=True)
    inverse = lax.rsqrt(jnp.mean(center * center, axis=-1, keepdims=True) + 1e-05)
    return center * inverse, inverse


def norm_back(incoming, scaled, inverse, gain):
    upward = incoming * gain
    return inverse * (
        upward
        - jnp.mean(upward, axis=-1, keepdims=True)
        - scaled * jnp.mean(upward * scaled, axis=-1, keepdims=True)
    )


def each(low, high, body):
    if high - low <= 8:
        for at in range(low, high):
            body(at)
    else:

        def step(at, carry):
            body(at)
            return carry

        lax.fori_loop(low, high, step, 0)


def tiles(width, body, at_once=2):
    def step(at, carry):
        for more in range(at_once):
            body(at_once * at + more)
        return carry

    lax.fori_loop(0, width // (at_once * TILE), step, 0)


def sum_rows(rows):
    return jnp.sum(rows, axis=0, keepdims=True)


class Layer:
    def __init__(self, size, refs):
        self.__dict__.update(size)
        self.__dict__.update(refs)
        self.dp_at = lax.axis_index("dp")
        self.mp_at = lax.axis_index("mp")
        self.line_at = self.dp_at // 2
        self.pair_at = lax.rem(self.dp_at, 2)
        self.chip_at = self.mp_at // 2
        self.core_at = lax.rem(self.mp_at, 2)
        self.sib = (self.dp_at, self.chip_at * 2 + 1 - self.core_at)
        self.across = (self.dp_at, (1 - self.chip_at) * 2 + self.core_at)
        self.pair = (self.line_at * 2 + 1 - self.pair_at, self.mp_at)
        self.middle = (self.line_at == 1) | (self.line_at == 2)
        self.pieces = 4 + 2 * self.chunks
        self.pair_first = PAIR_FIRST if self.lines == 4 else ()
        self.line_first = LINE_FIRST if self.lines == 4 else ()
        self.pair_slots = (self.pieces - len(self.line_first)) * self.lines
        self.rest = None
        self.stage_sends = [[], []]
        self.spread_sends = [[], [], [], []]
        self.late = []

    def line_of(self, step):
        return lax.rem(self.line_at + step + self.lines, self.lines)

    def line_peer(self, step):
        return (self.line_of(step) * 2 + self.pair_at, self.mp_at)

    def slot(self, line, pair):
        return pl.ds(pl.multiple_of((line * 2 + pair) * self.shard, self.shard), self.shard)

    def block(self, micro, chip, core):
        start = micro * self.rows + (chip * 2 + core) * self.pad
        return pl.ds(pl.multiple_of(start, 16), self.pad)

    def own_block(self, micro):
        return self.block(micro, self.chip_at, self.core_at)

    def source(self, piece):
        if piece < 4:
            return (self.query_w, self.key_w, self.value_w, self.out_w)[piece]
        which, chunk = (piece - 4) % 2, (piece - 4) // 2
        return (self.up_w, self.down_w)[which].at[:, pl.ds(chunk * TILE, TILE)]

    def copy(self, src, dst, send_sem, recv_sem, device):
        return pltpu.make_async_remote_copy(
            src_ref=src,
            dst_ref=dst,
            send_sem=send_sem,
            recv_sem=recv_sem,
            device_id=device,
            device_id_type=MESH,
        )

    def channels(self, piece):
        if piece in self.pair_first:
            return ((piece, False), (self.pieces + self.pair_first.index(piece), True))
        return ((piece, False),)

    def shard_place(self, piece, line, other):
        pair = 1 - self.pair_at if other else self.pair_at
        return self.weights.at[piece, self.slot(line, pair)]

    def broad(self, piece, channel, other, step):
        place = self.shard_place(piece, self.line_at, other)
        return self.copy(
            place if other else self.source(piece),
            place,
            self.wz_send.at[channel, step - 1],
            self.wz_recv.at[channel, step - 1],
            self.line_peer(step),
        )

    def broad_in(self, piece, channel, other, step):
        place = self.shard_place(piece, self.line_of(-step), other)
        return self.copy(
            place,
            place,
            self.wz_send.at[channel, step - 1],
            self.wz_recv.at[channel, step - 1],
            self.line_peer(-step),
        )

    def broad_each(self, piece, channel, other, act):
        def one(step):
            if self.lines == 4 and step != 2:
                @pl.when(self.line_at != (3 if step == 1 else 0))
                def _():
                    act(self.broad(piece, channel, other, step))
            else:
                act(self.broad(piece, channel, other, step))

        each(1, self.lines, one)

    def relay(self, piece, channel, other, act):
        if self.lines != 4:
            return

        @pl.when(self.middle)
        def _():
            place = self.shard_place(piece, 3 * (2 - self.line_at), other)
            end = (3 * (self.line_at - 1) * 2 + self.pair_at, self.mp_at)
            act(
                self.copy(
                    place,
                    place,
                    self.wz_send.at[channel, 3],
                    self.wz_recv.at[channel, 2 * (self.line_at - 1)],
                    end,
                )
            )

    def weight_pair(self, piece, step, own):
        place = self.shard_place(piece, self.line_of(-step), False)
        return self.copy(
            self.source(piece) if own else place,
            place,
            self.wx_send.at[piece, step],
            self.wx_recv.at[piece, step],
            self.pair,
        )

    def weight_pair_in(self, piece, step):
        place = self.shard_place(piece, self.line_of(-step), True)
        return self.copy(
            place, place, self.wx_send.at[piece, step], self.wx_recv.at[piece, step], self.pair
        )

    def weight_local(self, piece):
        return pltpu.make_async_copy(
            self.source(piece),
            self.shard_place(piece, self.line_at, False),
            self.wl_sem.at[piece],
        )

    def send_pair(self, piece):
        self.weight_pair(piece, 0, True).start()

    def send_weight(self, piece, pair=True):
        if pair:
            self.send_pair(piece)
        self.broad_each(piece, piece, False, lambda one: one.start())
        self.weight_local(piece).start()

    def pass_weight(self, piece):
        self.flush()
        if piece in self.pair_first:
            self.weight_pair_in(piece, 0).wait_recv()
            channel, other = self.channels(piece)[1]
            self.broad_each(piece, channel, other, lambda one: one.start())
            return

        def one(step, last=False):
            self.broad_in(piece, piece, False, step).wait_recv()
            if last:
                self.relay(piece, piece, False, lambda one: one.start())
            self.weight_pair(piece, step, False).start()

        if self.lines == 4:
            second = jnp.where(self.line_at < 2, 3, 1)
            one(2, True)
            one(second)
            self.rest = lambda: one(4 - second)
        else:
            each(1, self.lines, one)

    def flush(self):
        if self.rest is not None:
            self.rest()
        self.rest = None

    def relay_weight(self, piece):
        for channel, other in self.channels(piece):
            if piece in self.pair_first:
                self.broad_in(piece, channel, other, 2).wait_recv()
                self.relay(piece, channel, other, lambda one: one.start())

    def await_weight(self, piece):
        self.weight_local(piece).wait()
        if piece in self.pair_first:
            for channel, other in self.channels(piece):
                for step in (1, 3):
                    self.broad_in(piece, channel, other, step).wait_recv()
        else:
            each(0, self.lines, lambda step: self.weight_pair_in(piece, step).wait_recv())

    def weight_sent(self, piece):
        self.weight_pair(piece, 0, True).wait_send()
        for channel, other in self.channels(piece):
            self.broad_each(piece, channel, other, lambda one: one.wait_send())
            self.relay(piece, channel, other, lambda one: one.wait_send())
        if piece not in self.pair_first:
            each(1, self.lines, lambda step: self.weight_pair(piece, step, False).wait_send())

    def spread_copy(self, kind, micro, ref, which):
        place = ref.at[self.own_block(micro)]
        if which == 2:
            place = ref.at[self.block(micro, 1 - self.chip_at, self.core_at)]
        return self.copy(
            place,
            place,
            self.ag_send.at[kind, micro, which],
            self.ag_recv.at[kind, micro, which],
            self.across if which == 0 else self.sib,
        )

    def spread_in(self, kind, micro, ref, which):
        chip = self.chip_at if which == 1 else 1 - self.chip_at
        core = self.core_at if which == 0 else 1 - self.core_at
        place = ref.at[self.block(micro, chip, core)]
        return self.copy(
            place,
            place,
            self.ag_send.at[kind, micro, which],
            self.ag_recv.at[kind, micro, which],
            self.across if which == 0 else self.sib,
        )

    def spread(self, kind, micro, ref):
        for which in (0, 1):
            self.spread_copy(kind, micro, ref, which).start()
            self.spread_sends[kind].append((micro, ref, which))

    def spread_on(self, kind, micro, ref):
        self.spread_in(kind, micro, ref, 0).wait_recv()
        self.spread_copy(kind, micro, ref, 2).start()
        self.spread_sends[kind].append((micro, ref, 2))

    def spread_sent(self, kind):
        for micro, ref, which in self.spread_sends[kind]:
            self.spread_copy(kind, micro, ref, which).wait_send()
        self.spread_sends[kind] = []

    def spread_end(self, kind, micro, ref):
        self.spread_in(kind, micro, ref, 1).wait_recv()
        self.spread_in(kind, micro, ref, 2).wait_recv()

    def collect(self, kind, micro, terms):
        for one in self.stage_sends[micro]:
            one.wait_send()
        self.stage_sends[micro] = []
        held = 1 if kind == 1 else 0
        for half, chip in ((0, 1 - self.chip_at), (1, self.chip_at)):
            start = pl.multiple_of(micro * self.rows + chip * 2 * self.pad, 16)
            stage, keep = self.stage.at[micro, half], self.keep.at[held, micro, half]

            def tile_of(tile):
                cols = pl.ds(pl.multiple_of(tile * TILE, TILE), TILE)
                product = terms(pl.ds(start, 2 * self.pad), cols)
                low, high = product[: self.pad], product[self.pad :]
                keep[:, cols] = jnp.where(self.core_at == 0, low, high)
                stage[:, cols] = jnp.where(self.core_at == 0, high, low).astype(BF16)

            tiles(self.width, tile_of, 1 if kind == 1 else 4)
            one = self.copy(
                stage,
                self.sib_in.at[kind, micro, half],
                self.rs_send.at[kind, micro, half],
                self.rs_recv.at[kind, micro, half],
                self.sib,
            )
            one.start()
            self.stage_sends[micro].append(one)

    def collect_far(self, kind, micro):
        incoming = self.sib_in.at[kind, micro, 0]
        self.copy(
            incoming,
            incoming,
            self.rs_send.at[kind, micro, 0],
            self.rs_recv.at[kind, micro, 0],
            self.sib,
        ).wait_recv()
        held = self.keep[1 if kind == 1 else 0, micro, 0]
        incoming[...] = (held + incoming[...].astype(F32)).astype(BF16)
        one = self.copy(
            incoming,
            self.far_in.at[kind, micro],
            self.rs_send.at[kind, micro, 2],
            self.rs_recv.at[kind, micro, 2],
            self.across,
        )
        one.start()
        self.late.append(one)

    def collected(self, kind, micro):
        near, far = self.sib_in.at[kind, micro, 1], self.far_in.at[kind, micro]
        self.copy(
            near, near, self.rs_send.at[kind, micro, 1], self.rs_recv.at[kind, micro, 1], self.sib
        ).wait_recv()
        self.copy(
            far, far, self.rs_send.at[kind, micro, 2], self.rs_recv.at[kind, micro, 2], self.across
        ).wait_recv()
        total = self.keep[1 if kind == 1 else 0, micro, 1] + near[...].astype(F32)
        return (total + far[...].astype(F32))[: self.part]

    def summed(self, piece):
        if piece < 4:
            return self.proj_back.at[: self.width, piece * TILE : (piece + 1) * TILE]
        return self.wide_sums.at[piece - 4]

    def sum_place(self, piece, line, other):
        pair = 1 - self.pair_at if other else self.pair_at
        return self.summed(piece).at[self.slot(line, pair)]

    def sum_channels(self, piece):
        if piece in self.line_first:
            return ((piece, False), (self.pieces + self.line_first.index(piece), True))
        return ((piece, False),)

    def relayed(self, piece):
        return self.lines == 4 and piece not in DIRECT

    def out_columns(self, piece):
        at = piece if piece < 4 else 4 + self.chunks * ((piece - 4) % 2) + (piece - 4) // 2
        return self.weight_g.at[:, pl.ds(at * TILE, TILE)]

    def pair_place(self, piece, line):
        if piece in self.line_first:
            return self.pair_in.at[self.pair_slots + self.line_first.index(piece)]
        before = sum(1 for other in self.line_first if other < piece)
        return self.pair_in.at[(piece - before) * self.lines + line]

    def grad_pair(self, piece, line):
        at = 0 if piece in self.line_first else line
        return self.copy(
            self.sum_place(piece, line, True),
            self.pair_place(piece, line),
            self.gx_send.at[piece, at],
            self.gx_recv.at[piece, at],
            self.pair,
        )

    def line_source(self, piece, line, other):
        if piece in self.line_first:
            return self.sum_place(piece, line, other)
        return self.pair_place(piece, line)

    def grad_line(self, piece, channel, other, step):
        line = self.line_of(step)
        target, at = line, step - 1
        if self.relayed(piece) and step != 2:
            far = self.line_at == (3 if step == 1 else 0)
            target = jnp.where(far, 2 if step == 1 else 1, line)
            at = jnp.where(far, 3, step - 1)
        return self.copy(
            self.line_source(piece, line, other),
            self.line_in.at[channel, at],
            self.gz_send.at[channel, step - 1],
            self.gz_recv.at[channel, at],
            (target * 2 + self.pair_at, self.mp_at),
        )

    def grad_line_in(self, channel, at):
        place = self.line_in.at[channel, at]
        return self.copy(
            place, place, self.gz_send.at[channel, 0], self.gz_recv.at[channel, at], self.pair
        )

    def grad_make(self, piece, left, right, send=True):
        out = self.summed(piece)

        def one(tile):
            cols = pl.ds(pl.multiple_of(tile * TILE, TILE), TILE)
            out[cols, :] = dot_tn(left[:, cols], right).astype(BF16)

        tiles(self.width, one)
        if send:
            self.grad_send(piece)

    def grad_send(self, piece):
        if piece in self.line_first:
            for channel, other in self.sum_channels(piece):
                for step in (1, 3):
                    self.grad_line(piece, channel, other, step).start()

                @pl.when(jnp.logical_not(self.middle))
                def _():
                    self.grad_line(piece, channel, other, 2).start()
        else:
            each(0, self.lines, lambda line: self.grad_pair(piece, line).start())

    def grad_pass(self, piece):
        def one(step, wait=True):
            line = self.line_of(step)
            if wait:
                self.grad_pair(piece, line).wait_recv()
            ref = self.pair_place(piece, line)
            total = self.sum_place(piece, line, False)[...].astype(F32) + ref[...].astype(F32)
            ref[...] = total.astype(BF16)
            self.grad_line(piece, piece, False, step).start()

        if piece in self.line_first:
            return
        if self.relayed(piece):
            one(1)
            one(3)
            self.grad_pair(piece, self.line_of(2)).wait_recv()
            pl.when(jnp.logical_not(self.middle))(lambda: one(2, False))
        else:
            each(1, self.lines, one)

    def grad_relay(self, piece):
        if not self.relayed(piece):
            return

        @pl.when(self.middle)
        def _():
            for channel, other in self.sum_channels(piece):
                line = self.line_of(2)
                self.grad_line_in(channel, 3).wait_recv()
                ref = self.line_source(piece, line, other)
                total = ref[...].astype(F32) + self.line_in[channel, 3].astype(F32)
                if piece not in self.line_first:
                    total = total + self.sum_place(piece, line, False)[...].astype(F32)
                ref[...] = total.astype(BF16)
                self.grad_line(piece, channel, other, 2).start()

    def line_total(self, piece, channel, ref):
        for step in range(1, self.lines):

            def one():
                self.grad_line_in(channel, step - 1).wait_recv()
                ref[...] += self.line_in[channel, step - 1].astype(F32)

            if self.relayed(piece) and step != 2:
                pl.when(self.line_at != (0 if step == 1 else 3))(one)
            else:
                one()

    def grad_cross(self, piece):
        if piece not in self.line_first:
            return
        ref = self.sum_place(piece, self.line_at, True)
        total = self.out_columns(piece)
        total[...] = ref[...].astype(F32)
        self.line_total(piece, self.sum_channels(piece)[1][0], total)
        ref[...] = total[...].astype(BF16)
        self.grad_pair(piece, self.line_at).start()

    def grad_end(self, piece):
        ref = self.out_columns(piece)
        self.grad_pair(piece, self.line_at).wait_recv()
        came = self.pair_place(piece, self.line_at)[...].astype(F32)
        ref[...] = self.sum_place(piece, self.line_at, False)[...].astype(F32) + came
        self.line_total(piece, piece, ref)

    def grad_sent(self, piece):
        if piece in self.line_first:
            self.grad_pair(piece, self.line_at).wait_send()
        else:
            each(0, self.lines, lambda line: self.grad_pair(piece, line).wait_send())
        for channel, other in self.sum_channels(piece):
            each(
                1,
                self.lines,
                lambda step: self.grad_line(piece, channel, other, step).wait_send(),
            )

    def clip(self, peaks):
        root = jnp.sqrt(self.tau[0, 0] / jnp.maximum(peaks, self.tau[0, 0]))
        head = lax.broadcasted_iota(jnp.int32, (1, TILE), 1) // HD
        roots = jnp.zeros((1, TILE), F32)
        for at in range(self.heads):
            roots = jnp.where(head == at, root[:, at : at + 1], roots)
        first = (4 + 2 * self.chunks) * TILE
        mine = self.slot(self.line_at, self.pair_at)
        for at, piece in enumerate((PQ, PK)):
            cols = slice(first + at * TILE, first + (at + 1) * TILE)
            self.weight_g[:, cols] = self.weights[piece, mine, :].astype(F32) * roots
        low, high = self.own_packed[8:9, :], self.own_packed[9:10, :]
        bias = low * roots[:, 0:128] + high * roots[:, 128:256]
        return bias

    def vector_copy(self, step):
        return self.copy(
            self.own_packed,
            self.vectors_in.at[self.dp_at],
            self.v_send.at[0, step - 1],
            self.v_recv.at[0, step - 1],
            (lax.rem(self.dp_at + step, self.dps), self.mp_at),
        )

    def vector_copy_in(self, step):
        origin = lax.rem(self.dp_at - step + self.dps, self.dps)
        place = self.vectors_in.at[origin]
        return self.copy(
            place,
            place,
            self.v_send.at[0, step - 1],
            self.v_recv.at[0, step - 1],
            (origin, self.mp_at),
        )

    def share_copy(self, step):
        target = lax.rem(self.dp_at + step, self.dps)
        return self.copy(
            self.shares.at[target],
            self.shares_in.at[step - 1],
            self.v_send.at[1, step - 1],
            self.v_recv.at[1, step - 1],
            (target, self.mp_at),
        )

    def group_copy(self, step):
        return self.copy(
            self.group.at[0],
            self.group.at[step],
            self.m_send.at[step - 1],
            self.m_recv.at[step - 1],
            (self.dp_at, lax.rem(self.mp_at + step, 4)),
        )

    def pack_vectors(self):
        if not self.own_vectors:
            return
        rows = [ref[...].astype(F32) for ref in self.small[:7]] + [jnp.zeros((1, 128), F32)]
        shift = lax.rem(self.dp_at * 32, 128)
        for ref in self.small[7:]:
            wide = jnp.concatenate([ref[...].astype(F32), jnp.zeros((1, 96), F32)], axis=1)
            wide = pltpu.roll(wide, shift, 1)
            rows.append(jnp.where(self.dp_at < 4, wide, 0.0))
            rows.append(jnp.where(self.dp_at < 4, 0.0, wide))
        self.own_packed[...] = jnp.concatenate(rows + [jnp.zeros((4, 128), F32)], axis=0)

    def take_vectors(self):
        if not self.own_vectors:
            self.vectors[...] = self.small[0][...]
            return
        self.vectors_in[self.dp_at] = self.own_packed[...]
        for step in range(1, self.dps):
            self.vector_copy_in(step).wait_recv()
        rest = self.vectors_in[0, 8:16, :]
        for at in range(1, self.dps):
            rest = rest + self.vectors_in[at, 8:16, :]
        for at in range(self.dps):
            self.vectors[0:8, at * 128 : (at + 1) * 128] = self.vectors_in[at, 0:8, :]
        for row, first in ((QB, 0), (VB, 2)):
            self.vectors[row : row + 1, 0:128] = rest[first : first + 1]
            self.vectors[row : row + 1, 128:256] = rest[first + 1 : first + 2]

    def give_vectors(self):
        if not self.own_vectors:
            self.vector_g[...] = self.sums[...]
            return
        for at in range(self.dps):
            half = (at * 32 // 128) * 128
            self.shares[at, 0:7, :] = self.sums[0:7, at * 128 : (at + 1) * 128]
            self.shares[at, 7:9, :] = self.sums[7:9, half : half + 128]
            self.shares[at, 9:16, :] = self.sums[9:16, 0:128]
        for step in range(1, self.dps):
            self.share_copy(step).start()

    def end_vectors(self):
        if not self.own_vectors:
            return
        total = self.shares[self.dp_at]
        most = total[PEAK : PEAK + 1]
        for step in range(1, self.dps):
            self.share_copy(step).wait_recv()
            came = self.shares_in[step - 1]
            total = total + came
            most = jnp.maximum(most, came[PEAK : PEAK + 1])
        self.group[0] = jnp.concatenate([total[:PEAK], most, total[PEAK + 1 :]], axis=0)
        for step in range(1, 4):
            self.group_copy(step).start()

    def last_vectors(self):
        if not self.own_vectors:
            return
        total = self.group[0]
        most = total[PEAK : PEAK + 1]
        whole = total[0:6]
        for step in range(1, 4):
            self.group_copy(step).wait_recv()
            whole = whole + self.group[step, 0:6, :]
        narrow = jnp.concatenate([total[7:9], self.clip(most), jnp.zeros((5, 128), F32)], axis=0)
        shift = lax.rem(128 - lax.rem(self.dp_at * 32, 128), 128)
        narrow = pltpu.roll(narrow, shift, 1)
        self.vector_g[0:6, :] = whole
        self.vector_g[6:7, :] = total[6:7]
        self.vector_g[7:9, :] = narrow[0:2]
        self.vector_g[9:10, :] = most
        self.vector_g[10:11, :] = narrow[2:3]
        self.vector_g[11:16, :] = jnp.zeros((5, 128), F32)

    def vector(self, row, start=0, size=None):
        size = self.width if size is None else size
        return self.vectors[row : row + 1, pl.ds(start, size)]

    def add_sum(self, row, value, start=0):
        cols = pl.ds(start, value.shape[1])
        self.sums[row : row + 1, cols] = self.sums[row : row + 1, cols] + value

    def mask(self, micro):
        row = self.mp_at * self.part + lax.broadcasted_iota(jnp.int32, (self.part, 1), 0)
        live = jnp.where(self.counts[micro] > 0, 1.0, 0.0).astype(F32)
        return jnp.where(row < IMG_LEN, live, 0.0)

    def put_rows(self, ref, micro, rows):
        filler = jnp.zeros((self.pad - self.part, self.width), F32)
        ref[self.own_block(micro), :] = jnp.concatenate([rows, filler], axis=0).astype(BF16)

    def first_norm(self, micro):
        scaled, _ = standardize(self.images[micro, 0].astype(F32))
        self.put_rows(self.normed_one, micro, scaled * self.vector(G1) + self.vector(S1))
        self.spread(0, micro, self.normed_one)

    def out_rows(self, micro):
        return self.out_grad[micro, 0].astype(F32) * self.mask(micro)

    def project_back(self, micro):
        rows = self.out_rows(micro)
        self.put_rows(self.proj_back, micro, rows)
        self.add_sum(DDB, sum_rows(rows.astype(BF16).astype(F32)))
        self.spread(2, micro, self.proj_back)

    def second_norm(self, micro):
        rows = self.images[micro, 0].astype(F32) + self.collected(0, micro) + self.vector(OB)
        self.after_attn[micro] = rows
        scaled, _ = standardize(rows)
        self.put_rows(self.normed_two, micro, scaled * self.vector(G2) + self.vector(S2))
        self.spread(1, micro, self.normed_two)

    def give_result(self, micro):
        rows = self.after_attn[micro] + self.collected(1, micro) + self.vector(DB)
        self.rows_g[0, micro, 0] = (self.mask(micro) * rows).astype(BF16)

    def second_norm_back(self, micro):
        incoming = self.collected(2, micro)
        scaled, inverse = standardize(self.after_attn[micro])
        rows = self.out_rows(micro) + norm_back(incoming, scaled, inverse, self.vector(G2))
        self.attn_back[micro] = rows
        self.add_sum(DOB, sum_rows(rows.astype(BF16).astype(F32)))
        self.add_sum(DG2, sum_rows(incoming * scaled))
        self.add_sum(DS2, sum_rows(incoming))
        self.put_rows(self.attended_back, micro, rows)
        self.spread(3, micro, self.attended_back)

    def first_norm_back(self, micro):
        incoming = self.collected(3, micro)
        scaled, inverse = standardize(self.images[micro, 0].astype(F32))
        self.add_sum(DG1, sum_rows(incoming * scaled))
        self.add_sum(DS1, sum_rows(incoming))
        rows = self.attn_back[micro] + norm_back(incoming, scaled, inverse, self.vector(G1))
        self.rows_g[1, micro, 0] = rows.astype(BF16)

    def image_rows(self, micro):
        return pl.ds(micro * self.rows, self.rows)

    def counted(self, axis):
        shape = (self.rows, 1) if axis == 0 else (1, self.rows)
        row = lax.broadcasted_iota(jnp.int32, shape, axis)
        block = row // self.pad
        inside = row - block * self.pad
        return (inside < self.part) & (block * self.part + inside < IMG_LEN)

    def head_columns(self, head):
        column = lax.broadcasted_iota(jnp.int32, (self.rows, TILE), 1)
        return column // HD == head

    def project_heads(self, micro):
        rows = self.image_rows(micro)
        normed = self.normed_one[rows, :]
        scale = 1.0 / math.sqrt(HD)
        query = dot_nn(normed, self.weights[PQ]) + self.vector(QB, 0, TILE)
        self.queries[rows, :] = (query.astype(BF16).astype(F32) * scale).astype(BF16)
        self.keys[rows, :] = dot_nn(normed, self.weights[PK]).astype(BF16)
        value = dot_nn(normed, self.weights[PV]) + self.vector(VB, 0, TILE)
        self.values[rows, :] = value.astype(BF16)

    def attend(self, micro, between):
        rows = self.image_rows(micro)
        values = self.turned.at[:, : self.rows]
        values[...] = self.values[rows, :].T
        live = jnp.where(self.counts[micro] > 0, 0.0, -1e30).astype(F32)
        split = (self.rows // 2 + 127) // 128 * 128

        def one_head(head):
            query = jnp.where(self.head_columns(head), self.queries[rows, :], jnp.zeros((), BF16))
            cols = pl.ds(pl.multiple_of(head * HD, HD), HD)
            top = total = mixed = None
            for low, high in ((0, split), (split, self.rows)):
                part = pl.ds(micro * self.rows + low, high - low)
                scores = dot_nt(self.keys[part, :], query)
                scores = jnp.where(self.counted(0)[low:high], scores, -1e30)
                most = jnp.max(scores, axis=0, keepdims=True)
                if top is None:
                    expo = jnp.exp(scores - most)
                    total = jnp.sum(expo, axis=0, keepdims=True)
                    mixed = dot_nn(values[cols, low:high], expo.astype(BF16))
                    top = most
                else:
                    most = jnp.maximum(top, most)
                    again = jnp.exp(top - most)
                    expo = jnp.exp(scores - most)
                    total = total * again + jnp.sum(expo, axis=0, keepdims=True)
                    added = dot_nn(values[cols, low:high], expo.astype(BF16))
                    mixed = mixed * again + added
                    top = most
            self.log_total[micro, pl.ds(head, 1), :] = top + jnp.log(total)
            self.mixed_turned[micro, cols, :] = mixed * (1.0 / total)
            peak = jnp.max(jnp.where(self.counted(1), top, -1e30), axis=1, keepdims=True)
            peak = jnp.where(live < 0.0, -1e30, peak)
            lane = lax.broadcasted_iota(jnp.int32, (1, 128), 1)
            seen = self.sums[PEAK : PEAK + 1, 0:128]
            self.sums[PEAK : PEAK + 1, 0:128] = jnp.where(
                lane == head, jnp.maximum(seen, peak), seen
            )

        def two_heads(at, carry):
            pl.when(at == 1)(between)
            one_head(2 * at)
            one_head(2 * at + 1)
            return carry

        lax.fori_loop(0, self.heads // 2, two_heads, 0)
        self.mixed[rows, :] = self.mixed_turned[micro].T.astype(BF16)

    def attend_back(self, micro, between):
        rows = self.image_rows(micro)
        self.mixed_back[...] = dot_nn(self.attended_back[rows, :], self.weights[PO]).astype(BF16)
        keys = self.turned.at[:, : self.rows]
        outwards = self.turned.at[:, self.rows :]
        keys[...] = self.keys[rows, :].T
        outwards[...] = self.mixed_back[...].T
        self.key_sum[...] = jnp.zeros_like(self.key_sum)
        self.value_sum[...] = jnp.zeros_like(self.value_sum)
        chunk = self.rows // 2

        def one_head(head, carry):
            columns = self.head_columns(head)
            none = jnp.zeros((), BF16)
            query = jnp.where(columns, self.queries[rows, :], none)
            outward = jnp.where(columns, self.mixed_back[...], none)
            cols = pl.ds(pl.multiple_of(head * HD, HD), HD)
            dots = outwards[cols, :].astype(F32) * self.mixed_turned[micro, cols, :]
            delta = jnp.sum(dots, axis=0, keepdims=True)
            log_total = self.log_total[micro, pl.ds(head, 1), :]
            for at in range(2):
                part = pl.ds(micro * self.rows + at * chunk, chunk)
                here = pl.ds(at * chunk, chunk)
                scores = dot_nt(self.keys[part, :], query)
                counted = self.counted(0)[at * chunk : (at + 1) * chunk]
                probs = jnp.where(counted, jnp.exp(scores - log_total), 0.0)
                prob_back = dot_nt(self.values[part, :], outward)
                self.probs[here, :] = probs.astype(BF16)
                self.score_back[here, :] = (probs * (prob_back - delta)).astype(BF16)
            self.value_sum[...] += dot_nn(self.probs[...], outward)
            self.key_sum[...] += dot_nn(self.score_back[...], query)
            self.mixed_turned[micro, cols, :] = dot_nn(keys[cols, :], self.score_back[...])
            return carry

        def with_between(head, carry):
            pl.when(head == self.heads // 2)(between)
            return one_head(head, carry)

        if micro == 0:
            lax.fori_loop(0, self.heads // 2, one_head, 0)
            between()
            lax.fori_loop(self.heads // 2, self.heads, one_head, 0)
        else:
            lax.fori_loop(0, self.heads, with_between, 0)
        scale = 1.0 / math.sqrt(HD)
        query_back = (self.mixed_turned[micro] * scale).T.astype(BF16)
        value_back = self.value_sum[...].astype(BF16)
        self.queries[rows, :] = query_back
        self.keys[rows, :] = self.key_sum[...].astype(BF16)
        self.values[rows, :] = value_back
        self.add_sum(DQB, sum_rows(query_back.astype(F32)))
        self.add_sum(DVB, sum_rows(value_back.astype(F32)))

    def feed(self, micro, chunk):
        cols = pl.ds(chunk * TILE, TILE)
        up, down = self.weights.at[4 + 2 * chunk], self.weights.at[5 + 2 * chunk]
        part = self.rows // 2
        total = jnp.zeros((1, TILE), F32)
        for at in range(2):
            rows = pl.ds(micro * self.rows + at * part, part)
            hidden = dot_nn(self.normed_two[rows, :], up[...])
            hidden = hidden + self.vector(UB, chunk * TILE, TILE)
            gate = jax.nn.sigmoid(1.702 * hidden)
            self.activated[rows, cols] = (hidden * gate).astype(BF16)
            back = dot_nn(self.proj_back[rows, :], down[...])
            back = back * (gate + 1.702 * hidden * gate * (1.0 - gate))
            back = back.astype(BF16)
            self.pre_back[rows, cols] = back
            total = total + sum_rows(back.astype(F32))
        self.add_sum(DUB, total, chunk * TILE)

    def out_terms(self, rows, cols):
        return dot_nt(self.mixed[rows, :], self.weights[PO, cols, :])

    def wide_terms(self, ref, first):
        def terms(rows, cols):
            total = None
            for chunk in range(self.chunks):
                one = dot_nt(
                    ref[rows, chunk * TILE : (chunk + 1) * TILE],
                    self.weights[first + 2 * chunk, cols, :],
                )
                total = one if total is None else total + one
            return total

        return terms

    def input_terms(self, rows, cols):
        total = dot_nt(self.queries[rows, :], self.weights[PQ, cols, :])
        total = total + dot_nt(self.keys[rows, :], self.weights[PK, cols, :])
        return total + dot_nt(self.values[rows, :], self.weights[PV, cols, :])

    def enter(self):
        barrier = pltpu.get_barrier_semaphore()
        peers = [self.sib, self.across]
        if self.own_vectors:
            peers.append((self.dp_at, (1 - self.chip_at) * 2 + 1 - self.core_at))
        for peer in peers:
            pl.semaphore_signal(barrier, inc=1, device_id=peer, device_id_type=MESH)
        if self.own_vectors:

            def hail(step):
                peer = (lax.rem(self.dp_at + step, self.dps), self.mp_at)
                pl.semaphore_signal(barrier, inc=1, device_id=peer, device_id_type=MESH)

            each(1, self.dps, hail)
            pl.semaphore_wait(barrier, 3 + self.dps - 1)
        else:
            pl.semaphore_signal(barrier, inc=1, device_id=self.pair, device_id_type=MESH)

            def hail(step):
                peer = self.line_peer(step)
                pl.semaphore_signal(barrier, inc=1, device_id=peer, device_id_type=MESH)

            each(1, self.lines, hail)
            pl.semaphore_wait(barrier, 2 + self.lines)

    def run(self):
        pieces = self.pieces
        last = self.chunks - 1
        self.pack_vectors()
        self.enter()
        if self.own_vectors:
            for step in range(1, self.dps):
                self.vector_copy(step).start()
        for piece in (PQ, PK, PV):
            self.send_weight(piece)
        self.sums[...] = jnp.zeros_like(self.sums)
        self.sums[PEAK : PEAK + 1, :] = jnp.full((1, self.width), -1e30, F32)
        self.take_vectors()
        for micro in (0, 1):
            self.first_norm(micro)
        self.pass_weight(PQ)
        self.pass_weight(PK)
        self.send_weight(PO)
        self.spread_on(0, 0, self.normed_one)
        self.pass_weight(PV)
        self.await_weight(PQ)
        self.spread_on(0, 1, self.normed_one)
        self.project_back(0)
        self.project_back(1)
        self.flush()
        self.send_weight(4)
        self.await_weight(PK)
        self.await_weight(PV)
        self.spread_end(0, 0, self.normed_one)
        self.project_heads(0)
        self.pass_weight(PO)
        self.send_weight(5)
        self.send_weight(6)
        self.spread_end(0, 1, self.normed_one)
        self.project_heads(1)
        self.flush()
        self.attend(0, lambda: None)
        self.await_weight(PO)
        self.collect(0, 0, self.out_terms)
        self.collect_far(0, 0)
        self.pass_weight(4)
        self.send_weight(7)
        self.spread_on(2, 0, self.proj_back)
        self.pass_weight(5)
        self.send_weight(8)
        self.send_pair(9)
        self.attend(1, self.flush)
        self.pass_weight(6)
        self.collect(0, 1, self.out_terms)
        self.collect_far(0, 1)
        self.spread_on(2, 1, self.proj_back)
        self.send_weight(9, False)
        self.second_norm(0)
        self.pass_weight(7)
        self.send_weight(10)
        self.pass_weight(8)
        self.send_weight(11)
        self.second_norm(1)
        self.relay_weight(6)
        self.pass_weight(9)
        self.spread_on(1, 0, self.normed_two)
        self.pass_weight(10)
        self.spread_end(1, 0, self.normed_two)
        self.spread_end(2, 0, self.proj_back)
        self.await_weight(4)
        self.await_weight(5)
        self.feed(0, 0)
        self.await_weight(6)
        self.await_weight(7)
        self.feed(0, 1)
        self.spread_on(1, 1, self.normed_two)
        self.pass_weight(11)
        self.relay_weight(9)

        def up_grad(chunk, send=True):
            cols = slice(chunk * TILE, (chunk + 1) * TILE)
            self.grad_make(4 + 2 * chunk, self.normed_two, self.pre_back[:, cols], send)

        def down_grad(chunk, send=True):
            cols = slice(chunk * TILE, (chunk + 1) * TILE)
            self.grad_make(5 + 2 * chunk, self.proj_back, self.activated[:, cols], send)

        self.await_weight(8)
        self.await_weight(9)
        self.feed(0, 2)
        self.flush()
        self.spread_end(1, 1, self.normed_two)
        self.spread_end(2, 1, self.proj_back)
        self.feed(1, 0)
        self.await_weight(10)
        self.await_weight(11)
        self.feed(0, last)
        self.collect(2, 0, self.wide_terms(self.pre_back, 4))
        self.collect_far(2, 0)
        self.feed(1, 1)
        up_grad(1)
        down_grad(1)
        self.feed(1, 2)
        self.feed(1, last)
        self.collect(2, 1, self.wide_terms(self.pre_back, 4))
        self.second_norm_back(0)
        up_grad(0)
        down_grad(0)
        self.collect_far(2, 1)
        up_grad(2)
        self.collect(1, 0, self.wide_terms(self.activated, 5))
        self.grad_pass(6)
        down_grad(2)
        self.spread_on(3, 0, self.attended_back)
        up_grad(3)
        self.spread_end(3, 0, self.attended_back)

        def between_first():
            self.grad_pass(7)
            self.second_norm_back(1)
            self.grad_relay(4)

        self.attend_back(0, between_first)
        down_grad(3)
        self.grad_pass(8)
        self.collect(3, 0, self.input_terms)
        self.grad_pass(9)
        self.spread_on(3, 1, self.attended_back)
        self.collect_far(3, 0)
        self.spread_sent(2)
        self.grad_relay(5)
        self.spread_end(3, 1, self.attended_back)
        self.grad_make(PO, self.attended_back, self.mixed[...])
        self.grad_pass(10)

        def between_second():
            self.grad_pass(11)
            self.grad_relay(6)
            self.grad_relay(7)

        self.attend_back(1, between_second)
        self.collect(3, 1, self.input_terms)
        self.collect_far(3, 1)
        self.grad_make(PV, self.normed_one, self.values[...])
        self.grad_pass(PO)
        self.grad_cross(4)
        self.grad_cross(5)
        self.grad_make(PQ, self.normed_one, self.queries[...])
        self.grad_make(PK, self.normed_one, self.keys[...])
        self.collect(1, 1, self.wide_terms(self.activated, 5))
        self.collect_far(1, 0)
        self.collect_far(1, 1)
        self.grad_relay(8)
        self.grad_relay(9)
        self.grad_pass(PV)
        self.grad_relay(10)
        self.grad_relay(11)
        self.first_norm_back(0)
        self.first_norm_back(1)
        self.give_vectors()
        self.grad_pass(PQ)
        self.grad_relay(PO)
        self.grad_relay(PV)
        self.grad_pass(PK)
        self.give_result(0)
        for piece in range(4, pieces):
            self.grad_end(piece)
        self.end_vectors()
        self.give_result(1)
        self.last_vectors()
        for piece in (PO, PV, PQ, PK):
            self.grad_end(piece)
        for kind in (0, 1, 3):
            self.spread_sent(kind)
        for one in self.late + self.stage_sends[0] + self.stage_sends[1]:
            one.wait_send()
        for piece in range(pieces):
            self.weight_sent(piece)
            self.grad_sent(piece)
        if self.own_vectors:
            for step in range(1, self.dps):
                self.vector_copy(step).wait_send()
                self.share_copy(step).wait_send()
            for step in range(1, 4):
                self.group_copy(step).wait_send()


def layer_kernel(size, names, *refs):
    named = dict(zip(names, refs))
    named["small"] = [named[name] for name in names if name.startswith("small_")]
    Layer(size, named).run()


def fused_layer(size, counts, tau, images, out_grad, small, weights):
    width, shard, part, rows, pad = (size[key] for key in ("width", "shard", "part", "rows", "pad"))
    lines, dps, pieces = size["lines"], size["dps"], 4 + 2 * size["chunks"]
    units = size["chunks"] * TILE
    vmem = pl.BlockSpec(memory_space=pltpu.VMEM)
    anywhere = pl.BlockSpec(memory_space=pl.ANY)
    vector_shape = (16, 128) if size["own_vectors"] else (16, width)
    outputs = {
        "rows_g": ((2,) + images.shape, BF16),
        "weight_g": ((shard, pieces * TILE + 2 * TILE), F32),
        "vector_g": (vector_shape, F32),
    }
    four = lines == 4
    channels = pieces + (len(PAIR_FIRST) if four else 0)
    pair_slots = pieces * lines - (len(LINE_FIRST) * (lines - 1) if four else 0)
    sum_channels = pieces + (len(LINE_FIRST) if four else 0)
    lines_in = 4 if four else lines - 1
    dma = pltpu.SemaphoreType.DMA
    vm = pltpu.VMEM
    scratch = {
        "weights": vm((pieces, width, TILE), BF16),
        "normed_one": vm((2 * rows, width), BF16),
        "normed_two": vm((2 * rows, width), BF16),
        "proj_back": vm((2 * rows, width), BF16),
        "attended_back": vm((2 * rows, width), BF16),
        "queries": vm((2 * rows, TILE), BF16),
        "keys": vm((2 * rows, TILE), BF16),
        "values": vm((2 * rows, TILE), BF16),
        "mixed": vm((2 * rows, TILE), BF16),
        "mixed_turned": vm((2, TILE, rows), F32),
        "log_total": vm((2, size["heads"], rows), F32),
        "activated": vm((2 * rows, units), BF16),
        "pre_back": vm((2 * rows, units), BF16),
        "turned": vm((TILE, 2 * rows), BF16),
        "mixed_back": vm((rows, TILE), BF16),
        "key_sum": vm((rows, TILE), F32),
        "value_sum": vm((rows, TILE), F32),
        "probs": vm((rows, rows), BF16),
        "score_back": vm((rows, rows), BF16),
        "stage": vm((2, 2, pad, width), BF16),
        "keep": vm((2, 2, 2, pad, width), F32),
        "sib_in": vm((4, 2, 2, pad, width), BF16),
        "far_in": vm((4, 2, pad, width), BF16),
        "after_attn": vm((2, part, width), F32),
        "attn_back": vm((2, part, width), F32),
        "wide_sums": vm((pieces - 4, width, TILE), BF16),
        "pair_in": vm((pair_slots, shard, TILE), BF16),
        "line_in": vm((sum_channels, lines_in, shard, TILE), BF16),
        "vectors": vm((16, width), F32),
        "sums": vm((16, width), F32),
        "wz_send": dma((channels, lines_in)),
        "wz_recv": dma((channels, lines - 1)),
        "wx_send": dma((pieces, lines)),
        "wx_recv": dma((pieces, lines)),
        "wl_sem": dma((pieces,)),
        "ag_send": dma((4, 2, 3)),
        "ag_recv": dma((4, 2, 3)),
        "rs_send": dma((4, 2, 3)),
        "rs_recv": dma((4, 2, 3)),
        "gx_send": dma((pieces, lines)),
        "gx_recv": dma((pieces, lines)),
        "gz_send": dma((sum_channels, lines - 1)),
        "gz_recv": dma((sum_channels, lines_in)),
    }
    if size["own_vectors"]:
        scratch |= {
            "own_packed": vm((16, 128), F32),
            "vectors_in": vm((dps, 16, 128), F32),
            "shares": vm((dps, 16, 128), F32),
            "shares_in": vm((dps - 1, 16, 128), F32),
            "group": vm((4, 16, 128), F32),
            "v_send": dma((2, dps - 1)),
            "v_recv": dma((2, dps - 1)),
            "m_send": dma((3,)),
            "m_recv": dma((3,)),
        }
    inputs = ["counts", "tau", "images", "out_grad"] + [f"small_{at}" for at in range(len(small))]
    inputs += ["query_w", "key_w", "value_w", "out_w", "up_w", "down_w"]
    names = inputs + list(outputs) + list(scratch)
    return pl.pallas_call(
        functools.partial(layer_kernel, size, names),
        out_shape=[jax.ShapeDtypeStruct(*spec) for spec in outputs.values()],
        in_specs=[pl.BlockSpec(memory_space=pltpu.SMEM)] * 2
        + [vmem] * (2 + len(small))
        + [anywhere] * 6,
        out_specs=[vmem] * len(outputs),
        scratch_shapes=list(scratch.values()),
        compiler_params=pltpu.CompilerParams(
            collective_id=0, has_side_effects=True, vmem_limit_bytes=65024 * 2**10
        ),
    )(counts, tau, images, out_grad, *small, *weights)


def on_device(
    images,
    counts,
    first_gain,
    first_shift,
    query_weight,
    query_bias,
    key_weight,
    value_weight,
    value_bias,
    out_weight,
    out_bias,
    second_gain,
    second_shift,
    up_weight,
    up_bias,
    down_weight,
    down_bias,
    clip_tau,
    out_grad,
):
    part, width = images.shape[2:]
    dps = lax.axis_size("dp")
    dp_at = lax.axis_index("dp")
    shard = query_weight.shape[0]
    pad = (part + 15) // 16 * 16
    size = {
        "width": width,
        "shard": shard,
        "part": part,
        "pad": pad,
        "rows": pad * lax.axis_size("mp"),
        "dps": dps,
        "lines": dps // 2,
        "heads": query_weight.shape[1] // HD,
        "chunks": up_weight.shape[1] // TILE,
        "own_vectors": shard == 128,
    }
    bias_cols = query_bias.shape[1]
    parts = [first_gain, first_shift, out_bias, second_gain, second_shift, down_bias, up_bias[0]]
    if size["own_vectors"]:
        small = [one.reshape(1, -1) for one in parts] + [query_bias, value_bias]
    else:
        whole = [lax.all_gather(one, "dp", axis=0, tiled=True) for one in parts]
        rest = [
            jnp.pad(lax.all_gather(one[0], "dp", axis=0, tiled=True), (0, width - TILE))
            for one in (query_bias, value_bias)
        ]
        filler = jnp.zeros((width,), BF16)
        small = [jnp.stack(whole + [filler] + rest + [filler] * 6).astype(F32)]
    weights = (query_weight, key_weight, value_weight, out_weight, up_weight, down_weight)
    rows_g, weight_g, vector_g = fused_layer(
        size, counts.reshape(-1), clip_tau.reshape(1, 1), images, out_grad, small, weights
    )
    columns, units = query_weight.shape[1], up_weight.shape[1]
    edges = [0, columns, 2 * columns, 3 * columns, 4 * columns]
    edges += [edges[-1] + units, edges[-1] + 2 * units]
    query_g, key_g, value_g, out_g, up_g, down_g = (
        weight_g[:, low:high] for low, high in zip(edges[:-1], edges[1:])
    )
    if size["own_vectors"]:
        vectors = [vector_g[row] for row in range(7)]
        query_bias_g = vector_g[DQB : DQB + 1, :bias_cols]
        value_bias_g = vector_g[DVB : DVB + 1, :bias_cols]
        peaks = vector_g[PEAK, : size["heads"]]
        clipped_query = weight_g[:, edges[-1] : edges[-1] + columns]
        clipped_key = weight_g[:, edges[-1] + columns :]
        clipped_bias = vector_g[PEAK + 1 : PEAK + 2, :bias_cols]
    else:
        mine = vector_g[:DUB]
        mine = lax.psum(mine, "mp")
        mine = lax.psum_scatter(mine, "dp", scatter_dimension=1, tiled=True)
        up_bias_g = lax.psum_scatter(vector_g[DUB], "dp", scatter_dimension=0, tiled=True)
        vectors = [mine[row] for row in range(6)] + [up_bias_g]
        both = vector_g[DQB : DVB + 1, :TILE]
        both = lax.psum_scatter(both, "dp", scatter_dimension=1, tiled=True)
        query_bias_g, value_bias_g = both[0:1], both[1:2]
        peaks = lax.pmax(vector_g[PEAK, : size["heads"]], "dp")
        head_root = jnp.sqrt(clip_tau / jnp.maximum(peaks, clip_tau))
        column_root = jnp.repeat(head_root, HD)
        clipped_query = query_weight.astype(F32) * column_root[None, :]
        clipped_key = key_weight.astype(F32) * column_root[None, :]
        bias_root = lax.dynamic_slice(column_root, (dp_at * bias_cols,), (bias_cols,))
        clipped_bias = query_bias.astype(F32) * bias_root[None, :]
    return (
        rows_g[0],
        rows_g[1],
        vectors[DG1],
        vectors[DS1],
        query_g,
        query_bias_g,
        key_g,
        value_g,
        value_bias_g,
        out_g,
        vectors[DOB],
        vectors[DG2],
        vectors[DS2],
        up_g,
        vectors[DUB][None, :],
        down_g,
        vectors[DDB],
        peaks,
        clipped_query,
        clipped_key,
        clipped_bias,
    )


def solution(mesh):
    rows = P(None, "dp", "mp", None)
    wide, small, bias = P("dp", "mp"), P("dp"), P("mp", "dp")
    return jax.shard_map(
        on_device,
        mesh=mesh,
        in_specs=(
            rows,
            P(None, "dp"),
            small,
            small,
            wide,
            bias,
            wide,
            wide,
            bias,
            wide,
            small,
            small,
            small,
            wide,
            bias,
            wide,
            small,
            P(),
            rows,
        ),
        out_specs=(
            rows,
            rows,
            small,
            small,
            wide,
            bias,
            wide,
            wide,
            bias,
            wide,
            small,
            small,
            small,
            wide,
            bias,
            wide,
            small,
            P("mp"),
            wide,
            wide,
            bias,
        ),
        check_vma=False,
    )
```

```python
import functools
import math

import jax
import jax.numpy as jnp
from jax import lax
from jax.experimental import pallas as pl
from jax.experimental.pallas import tpu as pltpu
from jax.sharding import PartitionSpec as P

HD = 64
IMG_LEN = 577
F32 = jnp.float32
BF16 = jnp.bfloat16
MESH = pl.DeviceIdType.MESH
TILE = 256
PQ, PK, PV, PO = 0, 1, 2, 3
PAIR_FIRST = (6, 9)
LINE_FIRST = (4, 5)
DIRECT = (0, 1)
G1, S1, OB, G2, S2, DB, UB, QB, VB = 0, 1, 2, 3, 4, 5, 6, 8, 9
DG1, DS1, DOB, DG2, DS2, DDB, DUB, DQB, DVB, PEAK = 0, 1, 2, 3, 4, 5, 6, 7, 8, 9


def dot_nn(left, right):
    return lax.dot_general(left, right, (((1,), (0,)), ((), ())), preferred_element_type=F32)


def dot_nt(left, right):
    return lax.dot_general(left, right, (((1,), (1,)), ((), ())), preferred_element_type=F32)


def dot_tn(left, right):
    return lax.dot_general(left, right, (((0,), (0,)), ((), ())), preferred_element_type=F32)


def standardize(rows):
    center = rows - jnp.mean(rows, axis=-1, keepdims=True)
    inverse = lax.rsqrt(jnp.mean(center * center, axis=-1, keepdims=True) + 1e-05)
    return center * inverse, inverse


def norm_back(incoming, scaled, inverse, gain):
    upward = incoming * gain
    return inverse * (
        upward
        - jnp.mean(upward, axis=-1, keepdims=True)
        - scaled * jnp.mean(upward * scaled, axis=-1, keepdims=True)
    )


def each(low, high, body):
    if high - low <= 8:
        for at in range(low, high):
            body(at)
    else:

        def step(at, carry):
            body(at)
            return carry

        lax.fori_loop(low, high, step, 0)


def tiles(width, body, at_once=2):
    def step(at, carry):
        for more in range(at_once):
            body(at_once * at + more)
        return carry

    lax.fori_loop(0, width // (at_once * TILE), step, 0)


def sum_rows(rows):
    return jnp.sum(rows, axis=0, keepdims=True)


class Layer:
    def __init__(self, size, refs):
        self.__dict__.update(size)
        self.__dict__.update(refs)
        self.dp_at = lax.axis_index("dp")
        self.mp_at = lax.axis_index("mp")
        self.line_at = self.dp_at // 2
        self.pair_at = lax.rem(self.dp_at, 2)
        self.chip_at = self.mp_at // 2
        self.core_at = lax.rem(self.mp_at, 2)
        self.sib = (self.dp_at, self.chip_at * 2 + 1 - self.core_at)
        self.across = (self.dp_at, (1 - self.chip_at) * 2 + self.core_at)
        self.pair = (self.line_at * 2 + 1 - self.pair_at, self.mp_at)
        self.middle = (self.line_at == 1) | (self.line_at == 2)
        self.pieces = 4 + 2 * self.chunks
        self.pair_first = PAIR_FIRST if self.lines == 4 else ()
        self.line_first = LINE_FIRST if self.lines == 4 else ()
        self.pair_slots = (self.pieces - len(self.line_first)) * self.lines
        self.rest = None
        self.stage_sends = [[], []]
        self.spread_sends = [[], [], [], []]
        self.late = []

    def line_of(self, step):
        return lax.rem(self.line_at + step + self.lines, self.lines)

    def line_peer(self, step):
        return (self.line_of(step) * 2 + self.pair_at, self.mp_at)

    def slot(self, line, pair):
        return pl.ds(pl.multiple_of((line * 2 + pair) * self.shard, self.shard), self.shard)

    def block(self, micro, chip, core):
        start = micro * self.rows + (chip * 2 + core) * self.pad
        return pl.ds(pl.multiple_of(start, 16), self.pad)

    def own_block(self, micro):
        return self.block(micro, self.chip_at, self.core_at)

    def source(self, piece):
        if piece < 4:
            return (self.query_w, self.key_w, self.value_w, self.out_w)[piece]
        which, chunk = (piece - 4) % 2, (piece - 4) // 2
        return (self.up_w, self.down_w)[which].at[:, pl.ds(chunk * TILE, TILE)]

    def copy(self, src, dst, send_sem, recv_sem, device):
        return pltpu.make_async_remote_copy(
            src_ref=src,
            dst_ref=dst,
            send_sem=send_sem,
            recv_sem=recv_sem,
            device_id=device,
            device_id_type=MESH,
        )

    def channels(self, piece):
        if piece in self.pair_first:
            return ((piece, False), (self.pieces + self.pair_first.index(piece), True))
        return ((piece, False),)

    def shard_place(self, piece, line, other):
        pair = 1 - self.pair_at if other else self.pair_at
        return self.weights.at[piece, self.slot(line, pair)]

    def broad(self, piece, channel, other, step):
        place = self.shard_place(piece, self.line_at, other)
        return self.copy(
            place if other else self.source(piece),
            place,
            self.wz_send.at[channel, step - 1],
            self.wz_recv.at[channel, step - 1],
            self.line_peer(step),
        )

    def broad_in(self, piece, channel, other, step):
        place = self.shard_place(piece, self.line_of(-step), other)
        return self.copy(
            place,
            place,
            self.wz_send.at[channel, step - 1],
            self.wz_recv.at[channel, step - 1],
            self.line_peer(-step),
        )

    def broad_each(self, piece, channel, other, act):
        def one(step):
            if self.lines == 4 and step != 2:
                @pl.when(self.line_at != (3 if step == 1 else 0))
                def _():
                    act(self.broad(piece, channel, other, step))
            else:
                act(self.broad(piece, channel, other, step))

        each(1, self.lines, one)

    def relay(self, piece, channel, other, act):
        if self.lines != 4:
            return

        @pl.when(self.middle)
        def _():
            place = self.shard_place(piece, 3 * (2 - self.line_at), other)
            end = (3 * (self.line_at - 1) * 2 + self.pair_at, self.mp_at)
            act(
                self.copy(
                    place,
                    place,
                    self.wz_send.at[channel, 3],
                    self.wz_recv.at[channel, 2 * (self.line_at - 1)],
                    end,
                )
            )

    def weight_pair(self, piece, step, own):
        place = self.shard_place(piece, self.line_of(-step), False)
        return self.copy(
            self.source(piece) if own else place,
            place,
            self.wx_send.at[piece, step],
            self.wx_recv.at[piece, step],
            self.pair,
        )

    def weight_pair_in(self, piece, step):
        place = self.shard_place(piece, self.line_of(-step), True)
        return self.copy(
            place, place, self.wx_send.at[piece, step], self.wx_recv.at[piece, step], self.pair
        )

    def weight_local(self, piece):
        return pltpu.make_async_copy(
            self.source(piece),
            self.shard_place(piece, self.line_at, False),
            self.wl_sem.at[piece],
        )

    def send_pair(self, piece):
        self.weight_pair(piece, 0, True).start()

    def send_weight(self, piece, pair=True):
        if pair:
            self.send_pair(piece)
        self.broad_each(piece, piece, False, lambda one: one.start())
        self.weight_local(piece).start()

    def pass_weight(self, piece):
        self.flush()
        if piece in self.pair_first:
            self.weight_pair_in(piece, 0).wait_recv()
            channel, other = self.channels(piece)[1]
            self.broad_each(piece, channel, other, lambda one: one.start())
            return

        def one(step, last=False):
            self.broad_in(piece, piece, False, step).wait_recv()
            if last:
                self.relay(piece, piece, False, lambda one: one.start())
            self.weight_pair(piece, step, False).start()

        if self.lines == 4:
            second = jnp.where(self.line_at < 2, 3, 1)
            one(2, True)
            one(second)
            self.rest = lambda: one(4 - second)
        else:
            each(1, self.lines, one)

    def flush(self):
        if self.rest is not None:
            self.rest()
        self.rest = None

    def relay_weight(self, piece):
        for channel, other in self.channels(piece):
            if piece in self.pair_first:
                self.broad_in(piece, channel, other, 2).wait_recv()
                self.relay(piece, channel, other, lambda one: one.start())

    def await_weight(self, piece):
        self.weight_local(piece).wait()
        if piece in self.pair_first:
            for channel, other in self.channels(piece):
                for step in (1, 3):
                    self.broad_in(piece, channel, other, step).wait_recv()
        else:
            each(0, self.lines, lambda step: self.weight_pair_in(piece, step).wait_recv())

    def weight_sent(self, piece):
        self.weight_pair(piece, 0, True).wait_send()
        for channel, other in self.channels(piece):
            self.broad_each(piece, channel, other, lambda one: one.wait_send())
            self.relay(piece, channel, other, lambda one: one.wait_send())
        if piece not in self.pair_first:
            each(1, self.lines, lambda step: self.weight_pair(piece, step, False).wait_send())

    def spread_copy(self, kind, micro, ref, which):
        place = ref.at[self.own_block(micro)]
        if which == 2:
            place = ref.at[self.block(micro, 1 - self.chip_at, self.core_at)]
        return self.copy(
            place,
            place,
            self.ag_send.at[kind, micro, which],
            self.ag_recv.at[kind, micro, which],
            self.across if which == 0 else self.sib,
        )

    def spread_in(self, kind, micro, ref, which):
        chip = self.chip_at if which == 1 else 1 - self.chip_at
        core = self.core_at if which == 0 else 1 - self.core_at
        place = ref.at[self.block(micro, chip, core)]
        return self.copy(
            place,
            place,
            self.ag_send.at[kind, micro, which],
            self.ag_recv.at[kind, micro, which],
            self.across if which == 0 else self.sib,
        )

    def spread(self, kind, micro, ref):
        for which in (0, 1):
            self.spread_copy(kind, micro, ref, which).start()
            self.spread_sends[kind].append((micro, ref, which))

    def spread_on(self, kind, micro, ref):
        self.spread_in(kind, micro, ref, 0).wait_recv()
        self.spread_copy(kind, micro, ref, 2).start()
        self.spread_sends[kind].append((micro, ref, 2))

    def spread_sent(self, kind):
        for micro, ref, which in self.spread_sends[kind]:
            self.spread_copy(kind, micro, ref, which).wait_send()
        self.spread_sends[kind] = []

    def spread_end(self, kind, micro, ref):
        self.spread_in(kind, micro, ref, 1).wait_recv()
        self.spread_in(kind, micro, ref, 2).wait_recv()

    def collect(self, kind, micro, terms):
        for one in self.stage_sends[micro]:
            one.wait_send()
        self.stage_sends[micro] = []
        held = 1 if kind == 1 else 0
        for half, chip in ((0, 1 - self.chip_at), (1, self.chip_at)):
            start = pl.multiple_of(micro * self.rows + chip * 2 * self.pad, 16)
            stage, keep = self.stage.at[micro, half], self.keep.at[held, micro, half]

            def tile_of(tile):
                cols = pl.ds(pl.multiple_of(tile * TILE, TILE), TILE)
                product = terms(pl.ds(start, 2 * self.pad), cols)
                low, high = product[: self.pad], product[self.pad :]
                keep[:, cols] = jnp.where(self.core_at == 0, low, high)
                stage[:, cols] = jnp.where(self.core_at == 0, high, low).astype(BF16)

            tiles(self.width, tile_of, 1 if kind == 1 else 4)
            one = self.copy(
                stage,
                self.sib_in.at[kind, micro, half],
                self.rs_send.at[kind, micro, half],
                self.rs_recv.at[kind, micro, half],
                self.sib,
            )
            one.start()
            self.stage_sends[micro].append(one)

    def collect_far(self, kind, micro):
        incoming = self.sib_in.at[kind, micro, 0]
        self.copy(
            incoming,
            incoming,
            self.rs_send.at[kind, micro, 0],
            self.rs_recv.at[kind, micro, 0],
            self.sib,
        ).wait_recv()
        held = self.keep[1 if kind == 1 else 0, micro, 0]
        incoming[...] = (held + incoming[...].astype(F32)).astype(BF16)
        one = self.copy(
            incoming,
            self.far_in.at[kind, micro],
            self.rs_send.at[kind, micro, 2],
            self.rs_recv.at[kind, micro, 2],
            self.across,
        )
        one.start()
        self.late.append(one)

    def collected(self, kind, micro):
        near, far = self.sib_in.at[kind, micro, 1], self.far_in.at[kind, micro]
        self.copy(
            near, near, self.rs_send.at[kind, micro, 1], self.rs_recv.at[kind, micro, 1], self.sib
        ).wait_recv()
        self.copy(
            far, far, self.rs_send.at[kind, micro, 2], self.rs_recv.at[kind, micro, 2], self.across
        ).wait_recv()
        total = self.keep[1 if kind == 1 else 0, micro, 1] + near[...].astype(F32)
        return (total + far[...].astype(F32))[: self.part]

    def summed(self, piece):
        if piece < 4:
            return self.proj_back.at[: self.width, piece * TILE : (piece + 1) * TILE]
        return self.wide_sums.at[piece - 4]

    def sum_place(self, piece, line, other):
        pair = 1 - self.pair_at if other else self.pair_at
        return self.summed(piece).at[self.slot(line, pair)]

    def sum_channels(self, piece):
        if piece in self.line_first:
            return ((piece, False), (self.pieces + self.line_first.index(piece), True))
        return ((piece, False),)

    def relayed(self, piece):
        return self.lines == 4 and piece not in DIRECT

    def out_columns(self, piece):
        at = piece if piece < 4 else 4 + self.chunks * ((piece - 4) % 2) + (piece - 4) // 2
        return self.weight_g.at[:, pl.ds(at * TILE, TILE)]

    def pair_place(self, piece, line):
        if piece in self.line_first:
            return self.pair_in.at[self.pair_slots + self.line_first.index(piece)]
        before = sum(1 for other in self.line_first if other < piece)
        return self.pair_in.at[(piece - before) * self.lines + line]

    def grad_pair(self, piece, line):
        at = 0 if piece in self.line_first else line
        return self.copy(
            self.sum_place(piece, line, True),
            self.pair_place(piece, line),
            self.gx_send.at[piece, at],
            self.gx_recv.at[piece, at],
            self.pair,
        )

    def line_source(self, piece, line, other):
        if piece in self.line_first:
            return self.sum_place(piece, line, other)
        return self.pair_place(piece, line)

    def grad_line(self, piece, channel, other, step):
        line = self.line_of(step)
        target, at = line, step - 1
        if self.relayed(piece) and step != 2:
            far = self.line_at == (3 if step == 1 else 0)
            target = jnp.where(far, 2 if step == 1 else 1, line)
            at = jnp.where(far, 3, step - 1)
        return self.copy(
            self.line_source(piece, line, other),
            self.line_in.at[channel, at],
            self.gz_send.at[channel, step - 1],
            self.gz_recv.at[channel, at],
            (target * 2 + self.pair_at, self.mp_at),
        )

    def grad_line_in(self, channel, at):
        place = self.line_in.at[channel, at]
        return self.copy(
            place, place, self.gz_send.at[channel, 0], self.gz_recv.at[channel, at], self.pair
        )

    def grad_make(self, piece, left, right, send=True):
        out = self.summed(piece)

        def one(tile):
            cols = pl.ds(pl.multiple_of(tile * TILE, TILE), TILE)
            out[cols, :] = dot_tn(left[:, cols], right).astype(BF16)

        tiles(self.width, one)
        if send:
            self.grad_send(piece)

    def grad_send(self, piece):
        if piece in self.line_first:
            for channel, other in self.sum_channels(piece):
                for step in (1, 3):
                    self.grad_line(piece, channel, other, step).start()

                @pl.when(jnp.logical_not(self.middle))
                def _():
                    self.grad_line(piece, channel, other, 2).start()
        else:
            each(0, self.lines, lambda line: self.grad_pair(piece, line).start())

    def grad_pass(self, piece):
        def one(step, wait=True):
            line = self.line_of(step)
            if wait:
                self.grad_pair(piece, line).wait_recv()
            ref = self.pair_place(piece, line)
            total = self.sum_place(piece, line, False)[...].astype(F32) + ref[...].astype(F32)
            ref[...] = total.astype(BF16)
            self.grad_line(piece, piece, False, step).start()

        if piece in self.line_first:
            return
        if self.relayed(piece):
            one(1)
            one(3)
            self.grad_pair(piece, self.line_of(2)).wait_recv()
            pl.when(jnp.logical_not(self.middle))(lambda: one(2, False))
        else:
            each(1, self.lines, one)

    def grad_relay(self, piece):
        if not self.relayed(piece):
            return

        @pl.when(self.middle)
        def _():
            for channel, other in self.sum_channels(piece):
                line = self.line_of(2)
                self.grad_line_in(channel, 3).wait_recv()
                ref = self.line_source(piece, line, other)
                total = ref[...].astype(F32) + self.line_in[channel, 3].astype(F32)
                if piece not in self.line_first:
                    total = total + self.sum_place(piece, line, False)[...].astype(F32)
                ref[...] = total.astype(BF16)
                self.grad_line(piece, channel, other, 2).start()

    def line_total(self, piece, channel, ref):
        for step in range(1, self.lines):

            def one():
                self.grad_line_in(channel, step - 1).wait_recv()
                ref[...] += self.line_in[channel, step - 1].astype(F32)

            if self.relayed(piece) and step != 2:
                pl.when(self.line_at != (0 if step == 1 else 3))(one)
            else:
                one()

    def grad_cross(self, piece):
        if piece not in self.line_first:
            return
        ref = self.sum_place(piece, self.line_at, True)
        total = self.out_columns(piece)
        total[...] = ref[...].astype(F32)
        self.line_total(piece, self.sum_channels(piece)[1][0], total)
        ref[...] = total[...].astype(BF16)
        self.grad_pair(piece, self.line_at).start()

    def grad_end(self, piece):
        ref = self.out_columns(piece)
        self.grad_pair(piece, self.line_at).wait_recv()
        came = self.pair_place(piece, self.line_at)[...].astype(F32)
        ref[...] = self.sum_place(piece, self.line_at, False)[...].astype(F32) + came
        self.line_total(piece, piece, ref)

    def grad_sent(self, piece):
        if piece in self.line_first:
            self.grad_pair(piece, self.line_at).wait_send()
        else:
            each(0, self.lines, lambda line: self.grad_pair(piece, line).wait_send())
        for channel, other in self.sum_channels(piece):
            each(
                1,
                self.lines,
                lambda step: self.grad_line(piece, channel, other, step).wait_send(),
            )

    def clip(self, peaks):
        root = jnp.sqrt(self.tau[0, 0] / jnp.maximum(peaks, self.tau[0, 0]))
        head = lax.broadcasted_iota(jnp.int32, (1, TILE), 1) // HD
        roots = jnp.zeros((1, TILE), F32)
        for at in range(self.heads):
            roots = jnp.where(head == at, root[:, at : at + 1], roots)
        first = (4 + 2 * self.chunks) * TILE
        mine = self.slot(self.line_at, self.pair_at)
        for at, piece in enumerate((PQ, PK)):
            cols = slice(first + at * TILE, first + (at + 1) * TILE)
            self.weight_g[:, cols] = self.weights[piece, mine, :].astype(F32) * roots
        low, high = self.own_packed[8:9, :], self.own_packed[9:10, :]
        bias = low * roots[:, 0:128] + high * roots[:, 128:256]
        return bias

    def vector_copy(self, step):
        return self.copy(
            self.own_packed,
            self.vectors_in.at[self.dp_at],
            self.v_send.at[0, step - 1],
            self.v_recv.at[0, step - 1],
            (lax.rem(self.dp_at + step, self.dps), self.mp_at),
        )

    def vector_copy_in(self, step):
        origin = lax.rem(self.dp_at - step + self.dps, self.dps)
        place = self.vectors_in.at[origin]
        return self.copy(
            place,
            place,
            self.v_send.at[0, step - 1],
            self.v_recv.at[0, step - 1],
            (origin, self.mp_at),
        )

    def share_copy(self, step):
        target = lax.rem(self.dp_at + step, self.dps)
        return self.copy(
            self.shares.at[target],
            self.shares_in.at[step - 1],
            self.v_send.at[1, step - 1],
            self.v_recv.at[1, step - 1],
            (target, self.mp_at),
        )

    def group_copy(self, step):
        return self.copy(
            self.group.at[0],
            self.group.at[step],
            self.m_send.at[step - 1],
            self.m_recv.at[step - 1],
            (self.dp_at, lax.rem(self.mp_at + step, 4)),
        )

    def pack_vectors(self):
        if not self.own_vectors:
            return
        rows = [ref[...].astype(F32) for ref in self.small[:7]] + [jnp.zeros((1, 128), F32)]
        shift = lax.rem(self.dp_at * 32, 128)
        for ref in self.small[7:]:
            wide = jnp.concatenate([ref[...].astype(F32), jnp.zeros((1, 96), F32)], axis=1)
            wide = pltpu.roll(wide, shift, 1)
            rows.append(jnp.where(self.dp_at < 4, wide, 0.0))
            rows.append(jnp.where(self.dp_at < 4, 0.0, wide))
        self.own_packed[...] = jnp.concatenate(rows + [jnp.zeros((4, 128), F32)], axis=0)

    def take_vectors(self):
        if not self.own_vectors:
            self.vectors[...] = self.small[0][...]
            return
        self.vectors_in[self.dp_at] = self.own_packed[...]
        for step in range(1, self.dps):
            self.vector_copy_in(step).wait_recv()
        rest = self.vectors_in[0, 8:16, :]
        for at in range(1, self.dps):
            rest = rest + self.vectors_in[at, 8:16, :]
        for at in range(self.dps):
            self.vectors[0:8, at * 128 : (at + 1) * 128] = self.vectors_in[at, 0:8, :]
        for row, first in ((QB, 0), (VB, 2)):
            self.vectors[row : row + 1, 0:128] = rest[first : first + 1]
            self.vectors[row : row + 1, 128:256] = rest[first + 1 : first + 2]

    def give_vectors(self):
        if not self.own_vectors:
            self.vector_g[...] = self.sums[...]
            return
        for at in range(self.dps):
            half = (at * 32 // 128) * 128
            self.shares[at, 0:7, :] = self.sums[0:7, at * 128 : (at + 1) * 128]
            self.shares[at, 7:9, :] = self.sums[7:9, half : half + 128]
            self.shares[at, 9:16, :] = self.sums[9:16, 0:128]
        for step in range(1, self.dps):
            self.share_copy(step).start()

    def end_vectors(self):
        if not self.own_vectors:
            return
        total = self.shares[self.dp_at]
        most = total[PEAK : PEAK + 1]
        for step in range(1, self.dps):
            self.share_copy(step).wait_recv()
            came = self.shares_in[step - 1]
            total = total + came
            most = jnp.maximum(most, came[PEAK : PEAK + 1])
        self.group[0] = jnp.concatenate([total[:PEAK], most, total[PEAK + 1 :]], axis=0)
        for step in range(1, 4):
            self.group_copy(step).start()

    def last_vectors(self):
        if not self.own_vectors:
            return
        total = self.group[0]
        most = total[PEAK : PEAK + 1]
        whole = total[0:6]
        for step in range(1, 4):
            self.group_copy(step).wait_recv()
            whole = whole + self.group[step, 0:6, :]
        narrow = jnp.concatenate([total[7:9], self.clip(most), jnp.zeros((5, 128), F32)], axis=0)
        shift = lax.rem(128 - lax.rem(self.dp_at * 32, 128), 128)
        narrow = pltpu.roll(narrow, shift, 1)
        self.vector_g[0:6, :] = whole
        self.vector_g[6:7, :] = total[6:7]
        self.vector_g[7:9, :] = narrow[0:2]
        self.vector_g[9:10, :] = most
        self.vector_g[10:11, :] = narrow[2:3]
        self.vector_g[11:16, :] = jnp.zeros((5, 128), F32)

    def vector(self, row, start=0, size=None):
        size = self.width if size is None else size
        return self.vectors[row : row + 1, pl.ds(start, size)]

    def add_sum(self, row, value, start=0):
        cols = pl.ds(start, value.shape[1])
        self.sums[row : row + 1, cols] = self.sums[row : row + 1, cols] + value

    def mask(self, micro):
        row = self.mp_at * self.part + lax.broadcasted_iota(jnp.int32, (self.part, 1), 0)
        live = jnp.where(self.counts[micro] > 0, 1.0, 0.0).astype(F32)
        return jnp.where(row < IMG_LEN, live, 0.0)

    def put_rows(self, ref, micro, rows):
        filler = jnp.zeros((self.pad - self.part, self.width), F32)
        ref[self.own_block(micro), :] = jnp.concatenate([rows, filler], axis=0).astype(BF16)

    def first_norm(self, micro):
        scaled, _ = standardize(self.images[micro, 0].astype(F32))
        self.put_rows(self.normed_one, micro, scaled * self.vector(G1) + self.vector(S1))
        self.spread(0, micro, self.normed_one)

    def out_rows(self, micro):
        return self.out_grad[micro, 0].astype(F32) * self.mask(micro)

    def project_back(self, micro):
        rows = self.out_rows(micro)
        self.put_rows(self.proj_back, micro, rows)
        self.add_sum(DDB, sum_rows(rows.astype(BF16).astype(F32)))
        self.spread(2, micro, self.proj_back)

    def second_norm(self, micro):
        rows = self.images[micro, 0].astype(F32) + self.collected(0, micro) + self.vector(OB)
        self.after_attn[micro] = rows
        scaled, _ = standardize(rows)
        self.put_rows(self.normed_two, micro, scaled * self.vector(G2) + self.vector(S2))
        self.spread(1, micro, self.normed_two)

    def give_result(self, micro):
        rows = self.after_attn[micro] + self.collected(1, micro) + self.vector(DB)
        self.rows_g[0, micro, 0] = (self.mask(micro) * rows).astype(BF16)

    def second_norm_back(self, micro):
        incoming = self.collected(2, micro)
        scaled, inverse = standardize(self.after_attn[micro])
        rows = self.out_rows(micro) + norm_back(incoming, scaled, inverse, self.vector(G2))
        self.attn_back[micro] = rows
        self.add_sum(DOB, sum_rows(rows.astype(BF16).astype(F32)))
        self.add_sum(DG2, sum_rows(incoming * scaled))
        self.add_sum(DS2, sum_rows(incoming))
        self.put_rows(self.attended_back, micro, rows)
        self.spread(3, micro, self.attended_back)

    def first_norm_back(self, micro):
        incoming = self.collected(3, micro)
        scaled, inverse = standardize(self.images[micro, 0].astype(F32))
        self.add_sum(DG1, sum_rows(incoming * scaled))
        self.add_sum(DS1, sum_rows(incoming))
        rows = self.attn_back[micro] + norm_back(incoming, scaled, inverse, self.vector(G1))
        self.rows_g[1, micro, 0] = rows.astype(BF16)

    def image_rows(self, micro):
        return pl.ds(micro * self.rows, self.rows)

    def counted(self, axis):
        shape = (self.rows, 1) if axis == 0 else (1, self.rows)
        row = lax.broadcasted_iota(jnp.int32, shape, axis)
        block = row // self.pad
        inside = row - block * self.pad
        return (inside < self.part) & (block * self.part + inside < IMG_LEN)

    def head_columns(self, head):
        column = lax.broadcasted_iota(jnp.int32, (self.rows, TILE), 1)
        return column // HD == head

    def project_heads(self, micro):
        scale = 1.0 / math.sqrt(HD)
        part = self.rows // 2

        def half(at, carry):
            rows = pl.ds(pl.multiple_of(micro * self.rows + at * part, 16), part)
            normed = self.normed_one[rows, :]
            query = dot_nn(normed, self.weights[PQ]) + self.vector(QB, 0, TILE)
            self.queries[rows, :] = (query.astype(BF16).astype(F32) * scale).astype(BF16)
            self.keys[rows, :] = dot_nn(normed, self.weights[PK]).astype(BF16)
            value = dot_nn(normed, self.weights[PV]) + self.vector(VB, 0, TILE)
            self.values[rows, :] = value.astype(BF16)
            return carry

        lax.fori_loop(0, 2, half, 0)

    def attend(self, micro, between):
        rows = self.image_rows(micro)
        values = self.turned.at[:, : self.rows]
        values[...] = self.values[rows, :].T
        live = jnp.where(self.counts[micro] > 0, 0.0, -1e30).astype(F32)
        split = (self.rows // 2 + 127) // 128 * 128

        def one_head(head):
            query = jnp.where(self.head_columns(head), self.queries[rows, :], jnp.zeros((), BF16))
            cols = pl.ds(pl.multiple_of(head * HD, HD), HD)
            top = total = mixed = None
            for low, high in ((0, split), (split, self.rows)):
                part = pl.ds(micro * self.rows + low, high - low)
                scores = dot_nt(self.keys[part, :], query)
                scores = jnp.where(self.counted(0)[low:high], scores, -1e30)
                most = jnp.max(scores, axis=0, keepdims=True)
                if top is None:
                    expo = jnp.exp(scores - most)
                    total = jnp.sum(expo, axis=0, keepdims=True)
                    mixed = dot_nn(values[cols, low:high], expo.astype(BF16))
                    top = most
                else:
                    most = jnp.maximum(top, most)
                    again = jnp.exp(top - most)
                    expo = jnp.exp(scores - most)
                    total = total * again + jnp.sum(expo, axis=0, keepdims=True)
                    added = dot_nn(values[cols, low:high], expo.astype(BF16))
                    mixed = mixed * again + added
                    top = most
            self.log_total[micro, pl.ds(head, 1), :] = top + jnp.log(total)
            self.mixed_turned[micro, cols, :] = mixed * (1.0 / total)
            peak = jnp.max(jnp.where(self.counted(1), top, -1e30), axis=1, keepdims=True)
            peak = jnp.where(live < 0.0, -1e30, peak)
            lane = lax.broadcasted_iota(jnp.int32, (1, 128), 1)
            seen = self.sums[PEAK : PEAK + 1, 0:128]
            self.sums[PEAK : PEAK + 1, 0:128] = jnp.where(
                lane == head, jnp.maximum(seen, peak), seen
            )

        def two_heads(at, carry):
            pl.when(at == 1)(between)
            one_head(2 * at)
            one_head(2 * at + 1)
            return carry

        lax.fori_loop(0, self.heads // 2, two_heads, 0)
        self.mixed[rows, :] = self.mixed_turned[micro].T.astype(BF16)

    def attend_back(self, micro, between):
        rows = self.image_rows(micro)
        self.mixed_back[...] = dot_nn(self.attended_back[rows, :], self.weights[PO]).astype(BF16)
        keys = self.turned.at[:, : self.rows]
        outwards = self.turned.at[:, self.rows :]
        keys[...] = self.keys[rows, :].T
        outwards[...] = self.mixed_back[...].T
        self.key_sum[...] = jnp.zeros_like(self.key_sum)
        self.value_sum[...] = jnp.zeros_like(self.value_sum)
        chunk = self.rows // 2

        def one_head(head, carry):
            columns = self.head_columns(head)
            none = jnp.zeros((), BF16)
            query = jnp.where(columns, self.queries[rows, :], none)
            outward = jnp.where(columns, self.mixed_back[...], none)
            cols = pl.ds(pl.multiple_of(head * HD, HD), HD)
            dots = outwards[cols, :].astype(F32) * self.mixed_turned[micro, cols, :]
            delta = jnp.sum(dots, axis=0, keepdims=True)
            log_total = self.log_total[micro, pl.ds(head, 1), :]
            for at in range(2):
                part = pl.ds(micro * self.rows + at * chunk, chunk)
                here = pl.ds(at * chunk, chunk)
                scores = dot_nt(self.keys[part, :], query)
                counted = self.counted(0)[at * chunk : (at + 1) * chunk]
                probs = jnp.where(counted, jnp.exp(scores - log_total), 0.0)
                prob_back = dot_nt(self.values[part, :], outward)
                self.probs[here, :] = probs.astype(BF16)
                self.score_back[here, :] = (probs * (prob_back - delta)).astype(BF16)
            self.value_sum[...] += dot_nn(self.probs[...], outward)
            self.key_sum[...] += dot_nn(self.score_back[...], query)
            self.mixed_turned[micro, cols, :] = dot_nn(keys[cols, :], self.score_back[...])
            return carry

        def with_between(head, carry):
            pl.when(head == self.heads // 2)(between)
            return one_head(head, carry)

        if micro == 0:
            lax.fori_loop(0, self.heads // 2, one_head, 0)
            between()
            lax.fori_loop(self.heads // 2, self.heads, one_head, 0)
        else:
            lax.fori_loop(0, self.heads, with_between, 0)
        scale = 1.0 / math.sqrt(HD)
        query_back = (self.mixed_turned[micro] * scale).T.astype(BF16)
        value_back = self.value_sum[...].astype(BF16)
        self.queries[rows, :] = query_back
        self.keys[rows, :] = self.key_sum[...].astype(BF16)
        self.values[rows, :] = value_back
        self.add_sum(DQB, sum_rows(query_back.astype(F32)))
        self.add_sum(DVB, sum_rows(value_back.astype(F32)))

    def feed(self, micro, chunk):
        cols = pl.ds(chunk * TILE, TILE)
        up, down = self.weights.at[4 + 2 * chunk], self.weights.at[5 + 2 * chunk]
        part = self.rows // 2

        def half(at, carry):
            rows = pl.ds(pl.multiple_of(micro * self.rows + at * part, 16), part)
            hidden = dot_nn(self.normed_two[rows, :], up[...])
            hidden = hidden + self.vector(UB, chunk * TILE, TILE)
            gate = jax.nn.sigmoid(1.702 * hidden)
            self.activated[rows, cols] = (hidden * gate).astype(BF16)
            back = dot_nn(self.proj_back[rows, :], down[...])
            back = back * (gate + 1.702 * hidden * gate * (1.0 - gate))
            back = back.astype(BF16)
            self.pre_back[rows, cols] = back
            self.add_sum(DUB, sum_rows(back.astype(F32)), chunk * TILE)
            return carry

        lax.fori_loop(0, 2, half, 0)

    def out_terms(self, rows, cols):
        return dot_nt(self.mixed[rows, :], self.weights[PO, cols, :])

    def wide_terms(self, ref, first):
        def terms(rows, cols):
            total = None
            for chunk in range(self.chunks):
                one = dot_nt(
                    ref[rows, chunk * TILE : (chunk + 1) * TILE],
                    self.weights[first + 2 * chunk, cols, :],
                )
                total = one if total is None else total + one
            return total

        return terms

    def input_terms(self, rows, cols):
        total = dot_nt(self.queries[rows, :], self.weights[PQ, cols, :])
        total = total + dot_nt(self.keys[rows, :], self.weights[PK, cols, :])
        return total + dot_nt(self.values[rows, :], self.weights[PV, cols, :])

    def enter(self):
        barrier = pltpu.get_barrier_semaphore()
        peers = [self.sib, self.across]
        if self.own_vectors:
            peers.append((self.dp_at, (1 - self.chip_at) * 2 + 1 - self.core_at))
        for peer in peers:
            pl.semaphore_signal(barrier, inc=1, device_id=peer, device_id_type=MESH)
        if self.own_vectors:

            def hail(step):
                peer = (lax.rem(self.dp_at + step, self.dps), self.mp_at)
                pl.semaphore_signal(barrier, inc=1, device_id=peer, device_id_type=MESH)

            each(1, self.dps, hail)
            pl.semaphore_wait(barrier, 3 + self.dps - 1)
        else:
            pl.semaphore_signal(barrier, inc=1, device_id=self.pair, device_id_type=MESH)

            def hail(step):
                peer = self.line_peer(step)
                pl.semaphore_signal(barrier, inc=1, device_id=peer, device_id_type=MESH)

            each(1, self.lines, hail)
            pl.semaphore_wait(barrier, 2 + self.lines)

    def run(self):
        pieces = self.pieces
        last = self.chunks - 1
        self.pack_vectors()
        self.enter()
        if self.own_vectors:
            for step in range(1, self.dps):
                self.vector_copy(step).start()
        for piece in (PQ, PK, PV):
            self.send_weight(piece)
        self.sums[...] = jnp.zeros_like(self.sums)
        self.sums[PEAK : PEAK + 1, :] = jnp.full((1, self.width), -1e30, F32)
        self.take_vectors()
        for micro in (0, 1):
            self.first_norm(micro)
        self.pass_weight(PQ)
        self.pass_weight(PK)
        self.send_weight(PO)
        self.spread_on(0, 0, self.normed_one)
        self.pass_weight(PV)
        self.await_weight(PQ)
        self.spread_on(0, 1, self.normed_one)
        self.project_back(0)
        self.project_back(1)
        self.flush()
        self.send_weight(4)
        self.await_weight(PK)
        self.await_weight(PV)
        self.spread_end(0, 0, self.normed_one)
        self.project_heads(0)
        self.pass_weight(PO)
        self.send_weight(5)
        self.send_weight(6)
        self.spread_end(0, 1, self.normed_one)
        self.project_heads(1)
        self.flush()
        self.attend(0, lambda: None)
        self.await_weight(PO)
        self.collect(0, 0, self.out_terms)
        self.collect_far(0, 0)
        self.pass_weight(4)
        self.send_weight(7)
        self.spread_on(2, 0, self.proj_back)
        self.pass_weight(5)
        self.send_weight(8)
        self.send_pair(9)
        self.attend(1, self.flush)
        self.pass_weight(6)
        self.collect(0, 1, self.out_terms)
        self.collect_far(0, 1)
        self.spread_on(2, 1, self.proj_back)
        self.send_weight(9, False)
        self.second_norm(0)
        self.pass_weight(7)
        self.send_weight(10)
        self.pass_weight(8)
        self.send_weight(11)
        self.second_norm(1)
        self.relay_weight(6)
        self.pass_weight(9)
        self.spread_on(1, 0, self.normed_two)
        self.pass_weight(10)
        self.spread_end(1, 0, self.normed_two)
        self.spread_end(2, 0, self.proj_back)
        self.await_weight(4)
        self.await_weight(5)
        self.feed(0, 0)
        self.await_weight(6)
        self.await_weight(7)
        self.feed(0, 1)
        self.spread_on(1, 1, self.normed_two)
        self.pass_weight(11)
        self.relay_weight(9)

        def up_grad(chunk, send=True):
            cols = slice(chunk * TILE, (chunk + 1) * TILE)
            self.grad_make(4 + 2 * chunk, self.normed_two, self.pre_back[:, cols], send)

        def down_grad(chunk, send=True):
            cols = slice(chunk * TILE, (chunk + 1) * TILE)
            self.grad_make(5 + 2 * chunk, self.proj_back, self.activated[:, cols], send)

        self.await_weight(8)
        self.await_weight(9)
        self.feed(0, 2)
        self.flush()
        self.spread_end(1, 1, self.normed_two)
        self.spread_end(2, 1, self.proj_back)
        self.feed(1, 0)
        self.await_weight(10)
        self.await_weight(11)
        self.feed(0, last)
        self.collect(2, 0, self.wide_terms(self.pre_back, 4))
        self.collect_far(2, 0)
        self.feed(1, 1)
        up_grad(1)
        down_grad(1)
        self.feed(1, 2)
        self.feed(1, last)
        self.collect(2, 1, self.wide_terms(self.pre_back, 4))
        self.second_norm_back(0)
        up_grad(0)
        down_grad(0)
        self.collect_far(2, 1)
        up_grad(2)
        self.collect(1, 0, self.wide_terms(self.activated, 5))
        self.grad_pass(6)
        down_grad(2)
        self.spread_on(3, 0, self.attended_back)
        up_grad(3)
        self.spread_end(3, 0, self.attended_back)

        def between_first():
            self.grad_pass(7)
            self.second_norm_back(1)
            self.grad_relay(4)

        self.attend_back(0, between_first)
        down_grad(3)
        self.grad_pass(8)
        self.collect(3, 0, self.input_terms)
        self.grad_pass(9)
        self.spread_on(3, 1, self.attended_back)
        self.collect_far(3, 0)
        self.spread_sent(2)
        self.grad_relay(5)
        self.spread_end(3, 1, self.attended_back)
        self.grad_make(PO, self.attended_back, self.mixed[...])
        self.grad_pass(10)

        def between_second():
            self.grad_pass(11)
            self.grad_relay(6)
            self.grad_relay(7)

        self.attend_back(1, between_second)
        self.collect(3, 1, self.input_terms)
        self.collect_far(3, 1)
        self.grad_make(PV, self.normed_one, self.values[...])
        self.grad_pass(PO)
        self.grad_cross(4)
        self.grad_cross(5)
        self.grad_make(PQ, self.normed_one, self.queries[...])
        self.grad_make(PK, self.normed_one, self.keys[...])
        self.collect(1, 1, self.wide_terms(self.activated, 5))
        self.collect_far(1, 0)
        self.collect_far(1, 1)
        self.grad_relay(8)
        self.grad_relay(9)
        self.grad_pass(PV)
        self.grad_relay(10)
        self.grad_relay(11)
        self.first_norm_back(0)
        self.first_norm_back(1)
        self.give_vectors()
        self.grad_pass(PQ)
        self.grad_relay(PO)
        self.grad_relay(PV)
        self.grad_pass(PK)
        self.give_result(0)
        for piece in range(4, pieces):
            self.grad_end(piece)
        self.end_vectors()
        self.give_result(1)
        self.last_vectors()
        for piece in (PO, PV, PQ, PK):
            self.grad_end(piece)
        for kind in (0, 1, 3):
            self.spread_sent(kind)
        for one in self.late + self.stage_sends[0] + self.stage_sends[1]:
            one.wait_send()
        for piece in range(pieces):
            self.weight_sent(piece)
            self.grad_sent(piece)
        if self.own_vectors:
            for step in range(1, self.dps):
                self.vector_copy(step).wait_send()
                self.share_copy(step).wait_send()
            for step in range(1, 4):
                self.group_copy(step).wait_send()


def layer_kernel(size, names, *refs):
    named = dict(zip(names, refs))
    named["small"] = [named[name] for name in names if name.startswith("small_")]
    Layer(size, named).run()


def fused_layer(size, counts, tau, images, out_grad, small, weights):
    width, shard, part, rows, pad = (size[key] for key in ("width", "shard", "part", "rows", "pad"))
    lines, dps, pieces = size["lines"], size["dps"], 4 + 2 * size["chunks"]
    units = size["chunks"] * TILE
    vmem = pl.BlockSpec(memory_space=pltpu.VMEM)
    anywhere = pl.BlockSpec(memory_space=pl.ANY)
    vector_shape = (16, 128) if size["own_vectors"] else (16, width)
    outputs = {
        "rows_g": ((2,) + images.shape, BF16),
        "weight_g": ((shard, pieces * TILE + 2 * TILE), F32),
        "vector_g": (vector_shape, F32),
    }
    four = lines == 4
    channels = pieces + (len(PAIR_FIRST) if four else 0)
    pair_slots = pieces * lines - (len(LINE_FIRST) * (lines - 1) if four else 0)
    sum_channels = pieces + (len(LINE_FIRST) if four else 0)
    lines_in = 4 if four else lines - 1
    dma = pltpu.SemaphoreType.DMA
    vm = pltpu.VMEM
    scratch = {
        "weights": vm((pieces, width, TILE), BF16),
        "normed_one": vm((2 * rows, width), BF16),
        "normed_two": vm((2 * rows, width), BF16),
        "proj_back": vm((2 * rows, width), BF16),
        "attended_back": vm((2 * rows, width), BF16),
        "queries": vm((2 * rows, TILE), BF16),
        "keys": vm((2 * rows, TILE), BF16),
        "values": vm((2 * rows, TILE), BF16),
        "mixed": vm((2 * rows, TILE), BF16),
        "mixed_turned": vm((2, TILE, rows), F32),
        "log_total": vm((2, size["heads"], rows), F32),
        "activated": vm((2 * rows, units), BF16),
        "pre_back": vm((2 * rows, units), BF16),
        "turned": vm((TILE, 2 * rows), BF16),
        "mixed_back": vm((rows, TILE), BF16),
        "key_sum": vm((rows, TILE), F32),
        "value_sum": vm((rows, TILE), F32),
        "probs": vm((rows, rows), BF16),
        "score_back": vm((rows, rows), BF16),
        "stage": vm((2, 2, pad, width), BF16),
        "keep": vm((2, 2, 2, pad, width), F32),
        "sib_in": vm((4, 2, 2, pad, width), BF16),
        "far_in": vm((4, 2, pad, width), BF16),
        "after_attn": vm((2, part, width), F32),
        "attn_back": vm((2, part, width), F32),
        "wide_sums": vm((pieces - 4, width, TILE), BF16),
        "pair_in": vm((pair_slots, shard, TILE), BF16),
        "line_in": vm((sum_channels, lines_in, shard, TILE), BF16),
        "vectors": vm((16, width), F32),
        "sums": vm((16, width), F32),
        "wz_send": dma((channels, lines_in)),
        "wz_recv": dma((channels, lines - 1)),
        "wx_send": dma((pieces, lines)),
        "wx_recv": dma((pieces, lines)),
        "wl_sem": dma((pieces,)),
        "ag_send": dma((4, 2, 3)),
        "ag_recv": dma((4, 2, 3)),
        "rs_send": dma((4, 2, 3)),
        "rs_recv": dma((4, 2, 3)),
        "gx_send": dma((pieces, lines)),
        "gx_recv": dma((pieces, lines)),
        "gz_send": dma((sum_channels, lines - 1)),
        "gz_recv": dma((sum_channels, lines_in)),
    }
    if size["own_vectors"]:
        scratch |= {
            "own_packed": vm((16, 128), F32),
            "vectors_in": vm((dps, 16, 128), F32),
            "shares": vm((dps, 16, 128), F32),
            "shares_in": vm((dps - 1, 16, 128), F32),
            "group": vm((4, 16, 128), F32),
            "v_send": dma((2, dps - 1)),
            "v_recv": dma((2, dps - 1)),
            "m_send": dma((3,)),
            "m_recv": dma((3,)),
        }
    inputs = ["counts", "tau", "images", "out_grad"] + [f"small_{at}" for at in range(len(small))]
    inputs += ["query_w", "key_w", "value_w", "out_w", "up_w", "down_w"]
    names = inputs + list(outputs) + list(scratch)
    return pl.pallas_call(
        functools.partial(layer_kernel, size, names),
        out_shape=[jax.ShapeDtypeStruct(*spec) for spec in outputs.values()],
        in_specs=[pl.BlockSpec(memory_space=pltpu.SMEM)] * 2
        + [vmem] * (2 + len(small))
        + [anywhere] * 6,
        out_specs=[vmem] * len(outputs),
        scratch_shapes=list(scratch.values()),
        compiler_params=pltpu.CompilerParams(
            collective_id=0, has_side_effects=True, vmem_limit_bytes=65024 * 2**10
        ),
    )(counts, tau, images, out_grad, *small, *weights)


def on_device(
    images,
    counts,
    first_gain,
    first_shift,
    query_weight,
    query_bias,
    key_weight,
    value_weight,
    value_bias,
    out_weight,
    out_bias,
    second_gain,
    second_shift,
    up_weight,
    up_bias,
    down_weight,
    down_bias,
    clip_tau,
    out_grad,
):
    part, width = images.shape[2:]
    dps = lax.axis_size("dp")
    dp_at = lax.axis_index("dp")
    shard = query_weight.shape[0]
    pad = (part + 15) // 16 * 16
    size = {
        "width": width,
        "shard": shard,
        "part": part,
        "pad": pad,
        "rows": pad * lax.axis_size("mp"),
        "dps": dps,
        "lines": dps // 2,
        "heads": query_weight.shape[1] // HD,
        "chunks": up_weight.shape[1] // TILE,
        "own_vectors": shard == 128,
    }
    bias_cols = query_bias.shape[1]
    parts = [first_gain, first_shift, out_bias, second_gain, second_shift, down_bias, up_bias[0]]
    if size["own_vectors"]:
        small = [one.reshape(1, -1) for one in parts] + [query_bias, value_bias]
    else:
        whole = [lax.all_gather(one, "dp", axis=0, tiled=True) for one in parts]
        rest = [
            jnp.pad(lax.all_gather(one[0], "dp", axis=0, tiled=True), (0, width - TILE))
            for one in (query_bias, value_bias)
        ]
        filler = jnp.zeros((width,), BF16)
        small = [jnp.stack(whole + [filler] + rest + [filler] * 6).astype(F32)]
    weights = (query_weight, key_weight, value_weight, out_weight, up_weight, down_weight)
    rows_g, weight_g, vector_g = fused_layer(
        size, counts.reshape(-1), clip_tau.reshape(1, 1), images, out_grad, small, weights
    )
    columns, units = query_weight.shape[1], up_weight.shape[1]
    edges = [0, columns, 2 * columns, 3 * columns, 4 * columns]
    edges += [edges[-1] + units, edges[-1] + 2 * units]
    query_g, key_g, value_g, out_g, up_g, down_g = (
        weight_g[:, low:high] for low, high in zip(edges[:-1], edges[1:])
    )
    if size["own_vectors"]:
        vectors = [vector_g[row] for row in range(7)]
        query_bias_g = vector_g[DQB : DQB + 1, :bias_cols]
        value_bias_g = vector_g[DVB : DVB + 1, :bias_cols]
        peaks = vector_g[PEAK, : size["heads"]]
        clipped_query = weight_g[:, edges[-1] : edges[-1] + columns]
        clipped_key = weight_g[:, edges[-1] + columns :]
        clipped_bias = vector_g[PEAK + 1 : PEAK + 2, :bias_cols]
    else:
        mine = vector_g[:DUB]
        mine = lax.psum(mine, "mp")
        mine = lax.psum_scatter(mine, "dp", scatter_dimension=1, tiled=True)
        up_bias_g = lax.psum_scatter(vector_g[DUB], "dp", scatter_dimension=0, tiled=True)
        vectors = [mine[row] for row in range(6)] + [up_bias_g]
        both = vector_g[DQB : DVB + 1, :TILE]
        both = lax.psum_scatter(both, "dp", scatter_dimension=1, tiled=True)
        query_bias_g, value_bias_g = both[0:1], both[1:2]
        peaks = lax.pmax(vector_g[PEAK, : size["heads"]], "dp")
        head_root = jnp.sqrt(clip_tau / jnp.maximum(peaks, clip_tau))
        column_root = jnp.repeat(head_root, HD)
        clipped_query = query_weight.astype(F32) * column_root[None, :]
        clipped_key = key_weight.astype(F32) * column_root[None, :]
        bias_root = lax.dynamic_slice(column_root, (dp_at * bias_cols,), (bias_cols,))
        clipped_bias = query_bias.astype(F32) * bias_root[None, :]
    return (
        rows_g[0],
        rows_g[1],
        vectors[DG1],
        vectors[DS1],
        query_g,
        query_bias_g,
        key_g,
        value_g,
        value_bias_g,
        out_g,
        vectors[DOB],
        vectors[DG2],
        vectors[DS2],
        up_g,
        vectors[DUB][None, :],
        down_g,
        vectors[DDB],
        peaks,
        clipped_query,
        clipped_key,
        clipped_bias,
    )


def solution(mesh):
    rows = P(None, "dp", "mp", None)
    wide, small, bias = P("dp", "mp"), P("dp"), P("mp", "dp")
    return jax.shard_map(
        on_device,
        mesh=mesh,
        in_specs=(
            rows,
            P(None, "dp"),
            small,
            small,
            wide,
            bias,
            wide,
            wide,
            bias,
            wide,
            small,
            small,
            small,
            wide,
            bias,
            wide,
            small,
            P(),
            rows,
        ),
        out_specs=(
            rows,
            rows,
            small,
            small,
            wide,
            bias,
            wide,
            wide,
            bias,
            wide,
            small,
            small,
            small,
            wide,
            bias,
            wide,
            small,
            P("mp"),
            wide,
            wide,
            bias,
        ),
        check_vma=False,
    )
```

```python
import functools
import math

import jax
import jax.numpy as jnp
from jax import lax
from jax.experimental import pallas as pl
from jax.experimental.pallas import tpu as pltpu
from jax.sharding import PartitionSpec as P

HD = 64
IMG_LEN = 577
F32 = jnp.float32
BF16 = jnp.bfloat16
MESH = pl.DeviceIdType.MESH
TILE = 256
PQ, PK, PV, PO = 0, 1, 2, 3
PAIR_FIRST = (6, 9)
LINE_FIRST = (4, 5, 8)
DIRECT = (0, 1)
G1, S1, OB, G2, S2, DB, UB, QB, VB = 0, 1, 2, 3, 4, 5, 6, 8, 9
DG1, DS1, DOB, DG2, DS2, DDB, DUB, DQB, DVB, PEAK = 0, 1, 2, 3, 4, 5, 6, 7, 8, 9


def dot_nn(left, right):
    return lax.dot_general(left, right, (((1,), (0,)), ((), ())), preferred_element_type=F32)


def dot_nt(left, right):
    return lax.dot_general(left, right, (((1,), (1,)), ((), ())), preferred_element_type=F32)


def dot_tn(left, right):
    return lax.dot_general(left, right, (((0,), (0,)), ((), ())), preferred_element_type=F32)


def standardize(rows):
    center = rows - jnp.mean(rows, axis=-1, keepdims=True)
    inverse = lax.rsqrt(jnp.mean(center * center, axis=-1, keepdims=True) + 1e-05)
    return center * inverse, inverse


def norm_back(incoming, scaled, inverse, gain):
    upward = incoming * gain
    return inverse * (
        upward
        - jnp.mean(upward, axis=-1, keepdims=True)
        - scaled * jnp.mean(upward * scaled, axis=-1, keepdims=True)
    )


def each(low, high, body):
    if high - low <= 8:
        for at in range(low, high):
            body(at)
    else:

        def step(at, carry):
            body(at)
            return carry

        lax.fori_loop(low, high, step, 0)


def tiles(width, body, at_once=2):
    def step(at, carry):
        for more in range(at_once):
            body(at_once * at + more)
        return carry

    lax.fori_loop(0, width // (at_once * TILE), step, 0)


def sum_rows(rows):
    return jnp.sum(rows, axis=0, keepdims=True)


class Layer:
    def __init__(self, size, refs):
        self.__dict__.update(size)
        self.__dict__.update(refs)
        self.dp_at = lax.axis_index("dp")
        self.mp_at = lax.axis_index("mp")
        self.line_at = self.dp_at // 2
        self.pair_at = lax.rem(self.dp_at, 2)
        self.chip_at = self.mp_at // 2
        self.core_at = lax.rem(self.mp_at, 2)
        self.sib = (self.dp_at, self.chip_at * 2 + 1 - self.core_at)
        self.across = (self.dp_at, (1 - self.chip_at) * 2 + self.core_at)
        self.pair = (self.line_at * 2 + 1 - self.pair_at, self.mp_at)
        self.middle = (self.line_at == 1) | (self.line_at == 2)
        self.pieces = 4 + 2 * self.chunks
        self.pair_first = PAIR_FIRST if self.lines == 4 else ()
        self.line_first = LINE_FIRST if self.lines == 4 else ()
        self.pair_slots = (self.pieces - len(self.line_first)) * self.lines
        self.rest = None
        self.stage_sends = [[], []]
        self.spread_sends = [[], [], [], []]
        self.late = []

    def line_of(self, step):
        return lax.rem(self.line_at + step + self.lines, self.lines)

    def line_peer(self, step):
        return (self.line_of(step) * 2 + self.pair_at, self.mp_at)

    def slot(self, line, pair):
        return pl.ds(pl.multiple_of((line * 2 + pair) * self.shard, self.shard), self.shard)

    def block(self, micro, chip, core):
        start = micro * self.rows + (chip * 2 + core) * self.pad
        return pl.ds(pl.multiple_of(start, 16), self.pad)

    def own_block(self, micro):
        return self.block(micro, self.chip_at, self.core_at)

    def source(self, piece):
        if piece < 4:
            return (self.query_w, self.key_w, self.value_w, self.out_w)[piece]
        which, chunk = (piece - 4) % 2, (piece - 4) // 2
        return (self.up_w, self.down_w)[which].at[:, pl.ds(chunk * TILE, TILE)]

    def copy(self, src, dst, send_sem, recv_sem, device):
        return pltpu.make_async_remote_copy(
            src_ref=src,
            dst_ref=dst,
            send_sem=send_sem,
            recv_sem=recv_sem,
            device_id=device,
            device_id_type=MESH,
        )

    def channels(self, piece):
        if piece in self.pair_first:
            return ((piece, False), (self.pieces + self.pair_first.index(piece), True))
        return ((piece, False),)

    def shard_place(self, piece, line, other):
        pair = 1 - self.pair_at if other else self.pair_at
        return self.weights.at[piece, self.slot(line, pair)]

    def broad(self, piece, channel, other, step):
        place = self.shard_place(piece, self.line_at, other)
        return self.copy(
            place if other else self.source(piece),
            place,
            self.wz_send.at[channel, step - 1],
            self.wz_recv.at[channel, step - 1],
            self.line_peer(step),
        )

    def broad_in(self, piece, channel, other, step):
        place = self.shard_place(piece, self.line_of(-step), other)
        return self.copy(
            place,
            place,
            self.wz_send.at[channel, step - 1],
            self.wz_recv.at[channel, step - 1],
            self.line_peer(-step),
        )

    def broad_each(self, piece, channel, other, act):
        def one(step):
            if self.lines == 4 and step != 2:
                @pl.when(self.line_at != (3 if step == 1 else 0))
                def _():
                    act(self.broad(piece, channel, other, step))
            else:
                act(self.broad(piece, channel, other, step))

        each(1, self.lines, one)

    def relay(self, piece, channel, other, act):
        if self.lines != 4:
            return

        @pl.when(self.middle)
        def _():
            place = self.shard_place(piece, 3 * (2 - self.line_at), other)
            end = (3 * (self.line_at - 1) * 2 + self.pair_at, self.mp_at)
            act(
                self.copy(
                    place,
                    place,
                    self.wz_send.at[channel, 3],
                    self.wz_recv.at[channel, 2 * (self.line_at - 1)],
                    end,
                )
            )

    def weight_pair(self, piece, step, own):
        place = self.shard_place(piece, self.line_of(-step), False)
        return self.copy(
            self.source(piece) if own else place,
            place,
            self.wx_send.at[piece, step],
            self.wx_recv.at[piece, step],
            self.pair,
        )

    def weight_pair_in(self, piece, step):
        place = self.shard_place(piece, self.line_of(-step), True)
        return self.copy(
            place, place, self.wx_send.at[piece, step], self.wx_recv.at[piece, step], self.pair
        )

    def weight_local(self, piece):
        return pltpu.make_async_copy(
            self.source(piece),
            self.shard_place(piece, self.line_at, False),
            self.wl_sem.at[piece],
        )

    def send_pair(self, piece):
        self.weight_pair(piece, 0, True).start()

    def send_weight(self, piece, pair=True):
        if pair:
            self.send_pair(piece)
        self.broad_each(piece, piece, False, lambda one: one.start())
        self.weight_local(piece).start()

    def pass_weight(self, piece):
        self.flush()
        if piece in self.pair_first:
            self.weight_pair_in(piece, 0).wait_recv()
            channel, other = self.channels(piece)[1]
            self.broad_each(piece, channel, other, lambda one: one.start())
            return

        def one(step, last=False):
            self.broad_in(piece, piece, False, step).wait_recv()
            if last:
                self.relay(piece, piece, False, lambda one: one.start())
            self.weight_pair(piece, step, False).start()

        if self.lines == 4:
            second = jnp.where(self.line_at < 2, 3, 1)
            one(2, True)
            one(second)
            self.rest = lambda: one(4 - second)
        else:
            each(1, self.lines, one)

    def flush(self):
        if self.rest is not None:
            self.rest()
        self.rest = None

    def relay_weight(self, piece):
        for channel, other in self.channels(piece):
            if piece in self.pair_first:
                self.broad_in(piece, channel, other, 2).wait_recv()
                self.relay(piece, channel, other, lambda one: one.start())

    def await_weight(self, piece):
        self.weight_local(piece).wait()
        if piece in self.pair_first:
            for channel, other in self.channels(piece):
                for step in (1, 3):
                    self.broad_in(piece, channel, other, step).wait_recv()
        else:
            each(0, self.lines, lambda step: self.weight_pair_in(piece, step).wait_recv())

    def weight_sent(self, piece):
        self.weight_pair(piece, 0, True).wait_send()
        for channel, other in self.channels(piece):
            self.broad_each(piece, channel, other, lambda one: one.wait_send())
            self.relay(piece, channel, other, lambda one: one.wait_send())
        if piece not in self.pair_first:
            each(1, self.lines, lambda step: self.weight_pair(piece, step, False).wait_send())

    def spread_copy(self, kind, micro, ref, which):
        place = ref.at[self.own_block(micro)]
        if which == 2:
            place = ref.at[self.block(micro, 1 - self.chip_at, self.core_at)]
        return self.copy(
            place,
            place,
            self.ag_send.at[kind, micro, which],
            self.ag_recv.at[kind, micro, which],
            self.across if which == 0 else self.sib,
        )

    def spread_in(self, kind, micro, ref, which):
        chip = self.chip_at if which == 1 else 1 - self.chip_at
        core = self.core_at if which == 0 else 1 - self.core_at
        place = ref.at[self.block(micro, chip, core)]
        return self.copy(
            place,
            place,
            self.ag_send.at[kind, micro, which],
            self.ag_recv.at[kind, micro, which],
            self.across if which == 0 else self.sib,
        )

    def spread(self, kind, micro, ref):
        for which in (0, 1):
            self.spread_copy(kind, micro, ref, which).start()
            self.spread_sends[kind].append((micro, ref, which))

    def spread_on(self, kind, micro, ref):
        self.spread_in(kind, micro, ref, 0).wait_recv()
        self.spread_copy(kind, micro, ref, 2).start()
        self.spread_sends[kind].append((micro, ref, 2))

    def spread_sent(self, kind):
        for micro, ref, which in self.spread_sends[kind]:
            self.spread_copy(kind, micro, ref, which).wait_send()
        self.spread_sends[kind] = []

    def spread_end(self, kind, micro, ref):
        self.spread_in(kind, micro, ref, 1).wait_recv()
        self.spread_in(kind, micro, ref, 2).wait_recv()

    def collect(self, kind, micro, terms):
        for one in self.stage_sends[micro]:
            one.wait_send()
        self.stage_sends[micro] = []
        held = 1 if kind == 1 else 0
        for half, chip in ((0, 1 - self.chip_at), (1, self.chip_at)):
            start = pl.multiple_of(micro * self.rows + chip * 2 * self.pad, 16)
            stage, keep = self.stage.at[micro, half], self.keep.at[held, micro, half]

            def tile_of(tile):
                cols = pl.ds(pl.multiple_of(tile * TILE, TILE), TILE)
                product = terms(pl.ds(start, 2 * self.pad), cols)
                low, high = product[: self.pad], product[self.pad :]
                keep[:, cols] = jnp.where(self.core_at == 0, low, high)
                stage[:, cols] = jnp.where(self.core_at == 0, high, low).astype(BF16)

            tiles(self.width, tile_of, 1 if kind == 1 else 4)
            one = self.copy(
                stage,
                self.sib_in.at[kind, micro, half],
                self.rs_send.at[kind, micro, half],
                self.rs_recv.at[kind, micro, half],
                self.sib,
            )
            one.start()
            self.stage_sends[micro].append(one)

    def collect_far(self, kind, micro):
        incoming = self.sib_in.at[kind, micro, 0]
        self.copy(
            incoming,
            incoming,
            self.rs_send.at[kind, micro, 0],
            self.rs_recv.at[kind, micro, 0],
            self.sib,
        ).wait_recv()
        held = self.keep[1 if kind == 1 else 0, micro, 0]
        incoming[...] = (held + incoming[...].astype(F32)).astype(BF16)
        one = self.copy(
            incoming,
            self.far_in.at[kind, micro],
            self.rs_send.at[kind, micro, 2],
            self.rs_recv.at[kind, micro, 2],
            self.across,
        )
        one.start()
        self.late.append(one)

    def collected(self, kind, micro):
        near, far = self.sib_in.at[kind, micro, 1], self.far_in.at[kind, micro]
        self.copy(
            near, near, self.rs_send.at[kind, micro, 1], self.rs_recv.at[kind, micro, 1], self.sib
        ).wait_recv()
        self.copy(
            far, far, self.rs_send.at[kind, micro, 2], self.rs_recv.at[kind, micro, 2], self.across
        ).wait_recv()
        total = self.keep[1 if kind == 1 else 0, micro, 1] + near[...].astype(F32)
        return (total + far[...].astype(F32))[: self.part]

    def summed(self, piece):
        if piece < 4:
            return self.proj_back.at[: self.width, piece * TILE : (piece + 1) * TILE]
        return self.wide_sums.at[piece - 4]

    def sum_place(self, piece, line, other):
        pair = 1 - self.pair_at if other else self.pair_at
        return self.summed(piece).at[self.slot(line, pair)]

    def sum_channels(self, piece):
        if piece in self.line_first:
            return ((piece, False), (self.pieces + self.line_first.index(piece), True))
        return ((piece, False),)

    def relayed(self, piece):
        return self.lines == 4 and piece not in DIRECT

    def out_columns(self, piece):
        at = piece if piece < 4 else 4 + self.chunks * ((piece - 4) % 2) + (piece - 4) // 2
        return self.weight_g.at[:, pl.ds(at * TILE, TILE)]

    def pair_place(self, piece, line):
        if piece in self.line_first:
            return self.pair_in.at[self.pair_slots + self.line_first.index(piece)]
        before = sum(1 for other in self.line_first if other < piece)
        return self.pair_in.at[(piece - before) * self.lines + line]

    def grad_pair(self, piece, line):
        at = 0 if piece in self.line_first else line
        return self.copy(
            self.sum_place(piece, line, True),
            self.pair_place(piece, line),
            self.gx_send.at[piece, at],
            self.gx_recv.at[piece, at],
            self.pair,
        )

    def line_source(self, piece, line, other):
        if piece in self.line_first:
            return self.sum_place(piece, line, other)
        return self.pair_place(piece, line)

    def grad_line(self, piece, channel, other, step):
        line = self.line_of(step)
        target, at = line, step - 1
        if self.relayed(piece) and step != 2:
            far = self.line_at == (3 if step == 1 else 0)
            target = jnp.where(far, 2 if step == 1 else 1, line)
            at = jnp.where(far, 3, step - 1)
        return self.copy(
            self.line_source(piece, line, other),
            self.line_in.at[channel, at],
            self.gz_send.at[channel, step - 1],
            self.gz_recv.at[channel, at],
            (target * 2 + self.pair_at, self.mp_at),
        )

    def grad_line_in(self, channel, at):
        place = self.line_in.at[channel, at]
        return self.copy(
            place, place, self.gz_send.at[channel, 0], self.gz_recv.at[channel, at], self.pair
        )

    def grad_make(self, piece, left, right, send=True):
        out = self.summed(piece)

        def one(tile):
            cols = pl.ds(pl.multiple_of(tile * TILE, TILE), TILE)
            out[cols, :] = dot_tn(left[:, cols], right).astype(BF16)

        tiles(self.width, one)
        if send:
            self.grad_send(piece)

    def grad_send(self, piece):
        if piece in self.line_first:
            for channel, other in self.sum_channels(piece):
                for step in (1, 3):
                    self.grad_line(piece, channel, other, step).start()

                @pl.when(jnp.logical_not(self.middle))
                def _():
                    self.grad_line(piece, channel, other, 2).start()
        else:
            each(0, self.lines, lambda line: self.grad_pair(piece, line).start())

    def grad_pass(self, piece):
        def one(step, wait=True):
            line = self.line_of(step)
            if wait:
                self.grad_pair(piece, line).wait_recv()
            ref = self.pair_place(piece, line)
            total = self.sum_place(piece, line, False)[...].astype(F32) + ref[...].astype(F32)
            ref[...] = total.astype(BF16)
            self.grad_line(piece, piece, False, step).start()

        if piece in self.line_first:
            return
        if self.relayed(piece):
            one(1)
            one(3)
            self.grad_pair(piece, self.line_of(2)).wait_recv()
            pl.when(jnp.logical_not(self.middle))(lambda: one(2, False))
        else:
            each(1, self.lines, one)

    def grad_relay(self, piece):
        if not self.relayed(piece):
            return

        @pl.when(self.middle)
        def _():
            for channel, other in self.sum_channels(piece):
                line = self.line_of(2)
                self.grad_line_in(channel, 3).wait_recv()
                ref = self.line_source(piece, line, other)
                total = ref[...].astype(F32) + self.line_in[channel, 3].astype(F32)
                if piece not in self.line_first:
                    total = total + self.sum_place(piece, line, False)[...].astype(F32)
                ref[...] = total.astype(BF16)
                self.grad_line(piece, channel, other, 2).start()

    def line_total(self, piece, channel, ref):
        for step in range(1, self.lines):

            def one():
                self.grad_line_in(channel, step - 1).wait_recv()
                ref[...] += self.line_in[channel, step - 1].astype(F32)

            if self.relayed(piece) and step != 2:
                pl.when(self.line_at != (0 if step == 1 else 3))(one)
            else:
                one()

    def grad_cross(self, piece):
        if piece not in self.line_first:
            return
        ref = self.sum_place(piece, self.line_at, True)
        total = self.out_columns(piece)
        total[...] = ref[...].astype(F32)
        self.line_total(piece, self.sum_channels(piece)[1][0], total)
        ref[...] = total[...].astype(BF16)
        self.grad_pair(piece, self.line_at).start()

    def grad_end(self, piece):
        ref = self.out_columns(piece)
        self.grad_pair(piece, self.line_at).wait_recv()
        came = self.pair_place(piece, self.line_at)[...].astype(F32)
        ref[...] = self.sum_place(piece, self.line_at, False)[...].astype(F32) + came
        self.line_total(piece, piece, ref)

    def grad_sent(self, piece):
        if piece in self.line_first:
            self.grad_pair(piece, self.line_at).wait_send()
        else:
            each(0, self.lines, lambda line: self.grad_pair(piece, line).wait_send())
        for channel, other in self.sum_channels(piece):
            each(
                1,
                self.lines,
                lambda step: self.grad_line(piece, channel, other, step).wait_send(),
            )

    def clip(self, peaks):
        root = jnp.sqrt(self.tau[0, 0] / jnp.maximum(peaks, self.tau[0, 0]))
        head = lax.broadcasted_iota(jnp.int32, (1, TILE), 1) // HD
        roots = jnp.zeros((1, TILE), F32)
        for at in range(self.heads):
            roots = jnp.where(head == at, root[:, at : at + 1], roots)
        first = (4 + 2 * self.chunks) * TILE
        mine = self.slot(self.line_at, self.pair_at)
        for at, piece in enumerate((PQ, PK)):
            cols = slice(first + at * TILE, first + (at + 1) * TILE)
            self.weight_g[:, cols] = self.weights[piece, mine, :].astype(F32) * roots
        low, high = self.own_packed[8:9, :], self.own_packed[9:10, :]
        bias = low * roots[:, 0:128] + high * roots[:, 128:256]
        return bias

    def vector_copy(self, step):
        return self.copy(
            self.own_packed,
            self.vectors_in.at[self.dp_at],
            self.v_send.at[0, step - 1],
            self.v_recv.at[0, step - 1],
            (lax.rem(self.dp_at + step, self.dps), self.mp_at),
        )

    def vector_copy_in(self, step):
        origin = lax.rem(self.dp_at - step + self.dps, self.dps)
        place = self.vectors_in.at[origin]
        return self.copy(
            place,
            place,
            self.v_send.at[0, step - 1],
            self.v_recv.at[0, step - 1],
            (origin, self.mp_at),
        )

    def share_copy(self, step):
        target = lax.rem(self.dp_at + step, self.dps)
        return self.copy(
            self.shares.at[target],
            self.shares_in.at[step - 1],
            self.v_send.at[1, step - 1],
            self.v_recv.at[1, step - 1],
            (target, self.mp_at),
        )

    def group_copy(self, step):
        return self.copy(
            self.group.at[0],
            self.group.at[step],
            self.m_send.at[step - 1],
            self.m_recv.at[step - 1],
            (self.dp_at, lax.rem(self.mp_at + step, 4)),
        )

    def pack_vectors(self):
        if not self.own_vectors:
            return
        rows = [ref[...].astype(F32) for ref in self.small[:7]] + [jnp.zeros((1, 128), F32)]
        shift = lax.rem(self.dp_at * 32, 128)
        for ref in self.small[7:]:
            wide = jnp.concatenate([ref[...].astype(F32), jnp.zeros((1, 96), F32)], axis=1)
            wide = pltpu.roll(wide, shift, 1)
            rows.append(jnp.where(self.dp_at < 4, wide, 0.0))
            rows.append(jnp.where(self.dp_at < 4, 0.0, wide))
        self.own_packed[...] = jnp.concatenate(rows + [jnp.zeros((4, 128), F32)], axis=0)

    def take_vectors(self):
        if not self.own_vectors:
            self.vectors[...] = self.small[0][...]
            return
        self.vectors_in[self.dp_at] = self.own_packed[...]
        for step in range(1, self.dps):
            self.vector_copy_in(step).wait_recv()
        rest = self.vectors_in[0, 8:16, :]
        for at in range(1, self.dps):
            rest = rest + self.vectors_in[at, 8:16, :]
        for at in range(self.dps):
            self.vectors[0:8, at * 128 : (at + 1) * 128] = self.vectors_in[at, 0:8, :]
        for row, first in ((QB, 0), (VB, 2)):
            self.vectors[row : row + 1, 0:128] = rest[first : first + 1]
            self.vectors[row : row + 1, 128:256] = rest[first + 1 : first + 2]

    def give_vectors(self):
        if not self.own_vectors:
            self.vector_g[...] = self.sums[...]
            return
        for at in range(self.dps):
            half = (at * 32 // 128) * 128
            self.shares[at, 0:7, :] = self.sums[0:7, at * 128 : (at + 1) * 128]
            self.shares[at, 7:9, :] = self.sums[7:9, half : half + 128]
            self.shares[at, 9:16, :] = self.sums[9:16, 0:128]
        for step in range(1, self.dps):
            self.share_copy(step).start()

    def end_vectors(self):
        if not self.own_vectors:
            return
        total = self.shares[self.dp_at]
        most = total[PEAK : PEAK + 1]
        for step in range(1, self.dps):
            self.share_copy(step).wait_recv()
            came = self.shares_in[step - 1]
            total = total + came
            most = jnp.maximum(most, came[PEAK : PEAK + 1])
        self.group[0] = jnp.concatenate([total[:PEAK], most, total[PEAK + 1 :]], axis=0)
        for step in range(1, 4):
            self.group_copy(step).start()

    def last_vectors(self):
        if not self.own_vectors:
            return
        total = self.group[0]
        most = total[PEAK : PEAK + 1]
        whole = total[0:6]
        for step in range(1, 4):
            self.group_copy(step).wait_recv()
            whole = whole + self.group[step, 0:6, :]
        narrow = jnp.concatenate([total[7:9], self.clip(most), jnp.zeros((5, 128), F32)], axis=0)
        shift = lax.rem(128 - lax.rem(self.dp_at * 32, 128), 128)
        narrow = pltpu.roll(narrow, shift, 1)
        self.vector_g[0:6, :] = whole
        self.vector_g[6:7, :] = total[6:7]
        self.vector_g[7:9, :] = narrow[0:2]
        self.vector_g[9:10, :] = most
        self.vector_g[10:11, :] = narrow[2:3]
        self.vector_g[11:16, :] = jnp.zeros((5, 128), F32)

    def vector(self, row, start=0, size=None):
        size = self.width if size is None else size
        return self.vectors[row : row + 1, pl.ds(start, size)]

    def add_sum(self, row, value, start=0):
        cols = pl.ds(start, value.shape[1])
        self.sums[row : row + 1, cols] = self.sums[row : row + 1, cols] + value

    def mask(self, micro):
        row = self.mp_at * self.part + lax.broadcasted_iota(jnp.int32, (self.part, 1), 0)
        live = jnp.where(self.counts[micro] > 0, 1.0, 0.0).astype(F32)
        return jnp.where(row < IMG_LEN, live, 0.0)

    def put_rows(self, ref, micro, rows):
        filler = jnp.zeros((self.pad - self.part, self.width), F32)
        ref[self.own_block(micro), :] = jnp.concatenate([rows, filler], axis=0).astype(BF16)

    def first_norm(self, micro):
        scaled, _ = standardize(self.images[micro, 0].astype(F32))
        self.put_rows(self.normed_one, micro, scaled * self.vector(G1) + self.vector(S1))
        self.spread(0, micro, self.normed_one)

    def out_rows(self, micro):
        return self.out_grad[micro, 0].astype(F32) * self.mask(micro)

    def project_back(self, micro):
        rows = self.out_rows(micro)
        self.put_rows(self.proj_back, micro, rows)
        self.add_sum(DDB, sum_rows(rows.astype(BF16).astype(F32)))
        self.spread(2, micro, self.proj_back)

    def second_norm(self, micro):
        rows = self.images[micro, 0].astype(F32) + self.collected(0, micro) + self.vector(OB)
        self.after_attn[micro] = rows
        scaled, _ = standardize(rows)
        self.put_rows(self.normed_two, micro, scaled * self.vector(G2) + self.vector(S2))
        self.spread(1, micro, self.normed_two)

    def give_result(self, micro):
        rows = self.after_attn[micro] + self.collected(1, micro) + self.vector(DB)
        self.rows_g[0, micro, 0] = (self.mask(micro) * rows).astype(BF16)

    def second_norm_back(self, micro):
        incoming = self.collected(2, micro)
        scaled, inverse = standardize(self.after_attn[micro])
        rows = self.out_rows(micro) + norm_back(incoming, scaled, inverse, self.vector(G2))
        self.attn_back[micro] = rows
        self.add_sum(DOB, sum_rows(rows.astype(BF16).astype(F32)))
        self.add_sum(DG2, sum_rows(incoming * scaled))
        self.add_sum(DS2, sum_rows(incoming))
        self.put_rows(self.attended_back, micro, rows)
        self.spread(3, micro, self.attended_back)

    def first_norm_back(self, micro):
        incoming = self.collected(3, micro)
        scaled, inverse = standardize(self.images[micro, 0].astype(F32))
        self.add_sum(DG1, sum_rows(incoming * scaled))
        self.add_sum(DS1, sum_rows(incoming))
        rows = self.attn_back[micro] + norm_back(incoming, scaled, inverse, self.vector(G1))
        self.rows_g[1, micro, 0] = rows.astype(BF16)

    def image_rows(self, micro):
        return pl.ds(micro * self.rows, self.rows)

    def counted(self, axis):
        shape = (self.rows, 1) if axis == 0 else (1, self.rows)
        row = lax.broadcasted_iota(jnp.int32, shape, axis)
        block = row // self.pad
        inside = row - block * self.pad
        return (inside < self.part) & (block * self.part + inside < IMG_LEN)

    def head_columns(self, head):
        column = lax.broadcasted_iota(jnp.int32, (self.rows, TILE), 1)
        return column // HD == head

    def project_heads(self, micro):
        scale = 1.0 / math.sqrt(HD)
        part = self.rows // 2

        def half(at, carry):
            rows = pl.ds(pl.multiple_of(micro * self.rows + at * part, 16), part)
            normed = self.normed_one[rows, :]
            query = dot_nn(normed, self.weights[PQ]) + self.vector(QB, 0, TILE)
            self.queries[rows, :] = (query.astype(BF16).astype(F32) * scale).astype(BF16)
            self.keys[rows, :] = dot_nn(normed, self.weights[PK]).astype(BF16)
            value = dot_nn(normed, self.weights[PV]) + self.vector(VB, 0, TILE)
            self.values[rows, :] = value.astype(BF16)
            return carry

        lax.fori_loop(0, 2, half, 0)

    def attend(self, micro, between):
        rows = self.image_rows(micro)
        values = self.turned.at[:, : self.rows]
        values[...] = self.values[rows, :].T
        live = jnp.where(self.counts[micro] > 0, 0.0, -1e30).astype(F32)
        split = (self.rows // 2 + 127) // 128 * 128

        def one_head(head):
            query = jnp.where(self.head_columns(head), self.queries[rows, :], jnp.zeros((), BF16))
            cols = pl.ds(pl.multiple_of(head * HD, HD), HD)
            top = total = mixed = None
            for low, high in ((0, split), (split, self.rows)):
                part = pl.ds(micro * self.rows + low, high - low)
                scores = dot_nt(self.keys[part, :], query)
                scores = jnp.where(self.counted(0)[low:high], scores, -1e30)
                most = jnp.max(scores, axis=0, keepdims=True)
                if top is None:
                    expo = jnp.exp(scores - most)
                    total = jnp.sum(expo, axis=0, keepdims=True)
                    mixed = dot_nn(values[cols, low:high], expo.astype(BF16))
                    top = most
                else:
                    most = jnp.maximum(top, most)
                    again = jnp.exp(top - most)
                    expo = jnp.exp(scores - most)
                    total = total * again + jnp.sum(expo, axis=0, keepdims=True)
                    added = dot_nn(values[cols, low:high], expo.astype(BF16))
                    mixed = mixed * again + added
                    top = most
            self.log_total[micro, pl.ds(head, 1), :] = top + jnp.log(total)
            self.mixed_turned[micro, cols, :] = mixed * (1.0 / total)
            peak = jnp.max(jnp.where(self.counted(1), top, -1e30), axis=1, keepdims=True)
            peak = jnp.where(live < 0.0, -1e30, peak)
            lane = lax.broadcasted_iota(jnp.int32, (1, 128), 1)
            seen = self.sums[PEAK : PEAK + 1, 0:128]
            self.sums[PEAK : PEAK + 1, 0:128] = jnp.where(
                lane == head, jnp.maximum(seen, peak), seen
            )

        def two_heads(at, carry):
            pl.when(at == 1)(between)
            one_head(2 * at)
            one_head(2 * at + 1)
            return carry

        lax.fori_loop(0, self.heads // 2, two_heads, 0)
        self.mixed[rows, :] = self.mixed_turned[micro].T.astype(BF16)

    def attend_back(self, micro, between):
        rows = self.image_rows(micro)
        self.mixed_back[...] = dot_nn(self.attended_back[rows, :], self.weights[PO]).astype(BF16)
        keys = self.turned.at[:, : self.rows]
        outwards = self.turned.at[:, self.rows :]
        keys[...] = self.keys[rows, :].T
        outwards[...] = self.mixed_back[...].T
        self.key_sum[...] = jnp.zeros_like(self.key_sum)
        self.value_sum[...] = jnp.zeros_like(self.value_sum)
        chunk = self.rows // 2

        def one_head(head, carry):
            columns = self.head_columns(head)
            none = jnp.zeros((), BF16)
            query = jnp.where(columns, self.queries[rows, :], none)
            outward = jnp.where(columns, self.mixed_back[...], none)
            cols = pl.ds(pl.multiple_of(head * HD, HD), HD)
            dots = outwards[cols, :].astype(F32) * self.mixed_turned[micro, cols, :]
            delta = jnp.sum(dots, axis=0, keepdims=True)
            log_total = self.log_total[micro, pl.ds(head, 1), :]
            for at in range(2):
                part = pl.ds(micro * self.rows + at * chunk, chunk)
                here = pl.ds(at * chunk, chunk)
                scores = dot_nt(self.keys[part, :], query)
                counted = self.counted(0)[at * chunk : (at + 1) * chunk]
                probs = jnp.where(counted, jnp.exp(scores - log_total), 0.0)
                prob_back = dot_nt(self.values[part, :], outward)
                self.probs[here, :] = probs.astype(BF16)
                self.score_back[here, :] = (probs * (prob_back - delta)).astype(BF16)
            self.value_sum[...] += dot_nn(self.probs[...], outward)
            self.key_sum[...] += dot_nn(self.score_back[...], query)
            self.mixed_turned[micro, cols, :] = dot_nn(keys[cols, :], self.score_back[...])
            return carry

        def with_between(head, carry):
            pl.when(head == self.heads // 2)(between)
            return one_head(head, carry)

        if micro == 0:
            lax.fori_loop(0, self.heads // 2, one_head, 0)
            between()
            lax.fori_loop(self.heads // 2, self.heads, one_head, 0)
        else:
            lax.fori_loop(0, self.heads, with_between, 0)
        scale = 1.0 / math.sqrt(HD)
        query_back = (self.mixed_turned[micro] * scale).T.astype(BF16)
        value_back = self.value_sum[...].astype(BF16)
        self.queries[rows, :] = query_back
        self.keys[rows, :] = self.key_sum[...].astype(BF16)
        self.values[rows, :] = value_back
        self.add_sum(DQB, sum_rows(query_back.astype(F32)))
        self.add_sum(DVB, sum_rows(value_back.astype(F32)))

    def feed(self, micro, chunk):
        cols = pl.ds(chunk * TILE, TILE)
        up, down = self.weights.at[4 + 2 * chunk], self.weights.at[5 + 2 * chunk]
        part = self.rows // 2

        def half(at, carry):
            rows = pl.ds(pl.multiple_of(micro * self.rows + at * part, 16), part)
            hidden = dot_nn(self.normed_two[rows, :], up[...])
            hidden = hidden + self.vector(UB, chunk * TILE, TILE)
            gate = jax.nn.sigmoid(1.702 * hidden)
            self.activated[rows, cols] = (hidden * gate).astype(BF16)
            back = dot_nn(self.proj_back[rows, :], down[...])
            back = back * (gate + 1.702 * hidden * gate * (1.0 - gate))
            back = back.astype(BF16)
            self.pre_back[rows, cols] = back
            self.add_sum(DUB, sum_rows(back.astype(F32)), chunk * TILE)
            return carry

        lax.fori_loop(0, 2, half, 0)

    def out_terms(self, rows, cols):
        return dot_nt(self.mixed[rows, :], self.weights[PO, cols, :])

    def wide_terms(self, ref, first):
        def terms(rows, cols):
            total = None
            for chunk in range(self.chunks):
                one = dot_nt(
                    ref[rows, chunk * TILE : (chunk + 1) * TILE],
                    self.weights[first + 2 * chunk, cols, :],
                )
                total = one if total is None else total + one
            return total

        return terms

    def input_terms(self, rows, cols):
        total = dot_nt(self.queries[rows, :], self.weights[PQ, cols, :])
        total = total + dot_nt(self.keys[rows, :], self.weights[PK, cols, :])
        return total + dot_nt(self.values[rows, :], self.weights[PV, cols, :])

    def enter(self):
        barrier = pltpu.get_barrier_semaphore()
        peers = [self.sib, self.across]
        if self.own_vectors:
            peers.append((self.dp_at, (1 - self.chip_at) * 2 + 1 - self.core_at))
        for peer in peers:
            pl.semaphore_signal(barrier, inc=1, device_id=peer, device_id_type=MESH)
        if self.own_vectors:

            def hail(step):
                peer = (lax.rem(self.dp_at + step, self.dps), self.mp_at)
                pl.semaphore_signal(barrier, inc=1, device_id=peer, device_id_type=MESH)

            each(1, self.dps, hail)
            pl.semaphore_wait(barrier, 3 + self.dps - 1)
        else:
            pl.semaphore_signal(barrier, inc=1, device_id=self.pair, device_id_type=MESH)

            def hail(step):
                peer = self.line_peer(step)
                pl.semaphore_signal(barrier, inc=1, device_id=peer, device_id_type=MESH)

            each(1, self.lines, hail)
            pl.semaphore_wait(barrier, 2 + self.lines)

    def run(self):
        pieces = self.pieces
        last = self.chunks - 1
        self.pack_vectors()
        self.enter()
        if self.own_vectors:
            for step in range(1, self.dps):
                self.vector_copy(step).start()
        for piece in (PQ, PK, PV):
            self.send_weight(piece)
        self.sums[...] = jnp.zeros_like(self.sums)
        self.sums[PEAK : PEAK + 1, :] = jnp.full((1, self.width), -1e30, F32)
        self.take_vectors()
        for micro in (0, 1):
            self.first_norm(micro)
        self.pass_weight(PQ)
        self.pass_weight(PK)
        self.send_weight(PO)
        self.spread_on(0, 0, self.normed_one)
        self.pass_weight(PV)
        self.await_weight(PQ)
        self.spread_on(0, 1, self.normed_one)
        self.project_back(0)
        self.project_back(1)
        self.flush()
        self.send_weight(4)
        self.await_weight(PK)
        self.await_weight(PV)
        self.spread_end(0, 0, self.normed_one)
        self.project_heads(0)
        self.pass_weight(PO)
        self.send_weight(5)
        self.send_weight(6)
        self.spread_end(0, 1, self.normed_one)
        self.project_heads(1)
        self.flush()
        self.attend(0, lambda: None)
        self.await_weight(PO)
        self.collect(0, 0, self.out_terms)
        self.collect_far(0, 0)
        self.pass_weight(4)
        self.send_weight(7)
        self.spread_on(2, 0, self.proj_back)
        self.pass_weight(5)
        self.send_weight(8)
        self.send_pair(9)
        self.attend(1, self.flush)
        self.pass_weight(6)
        self.collect(0, 1, self.out_terms)
        self.collect_far(0, 1)
        self.spread_on(2, 1, self.proj_back)
        self.send_weight(9, False)
        self.second_norm(0)
        self.pass_weight(7)
        self.send_weight(10)
        self.pass_weight(8)
        self.send_weight(11)
        self.second_norm(1)
        self.relay_weight(6)
        self.pass_weight(9)
        self.spread_on(1, 0, self.normed_two)
        self.pass_weight(10)
        self.spread_end(1, 0, self.normed_two)
        self.spread_end(2, 0, self.proj_back)
        self.await_weight(4)
        self.await_weight(5)
        self.feed(0, 0)
        self.await_weight(6)
        self.await_weight(7)
        self.feed(0, 1)
        self.spread_on(1, 1, self.normed_two)
        self.pass_weight(11)
        self.relay_weight(9)

        def up_grad(chunk, send=True):
            cols = slice(chunk * TILE, (chunk + 1) * TILE)
            self.grad_make(4 + 2 * chunk, self.normed_two, self.pre_back[:, cols], send)

        def down_grad(chunk, send=True):
            cols = slice(chunk * TILE, (chunk + 1) * TILE)
            self.grad_make(5 + 2 * chunk, self.proj_back, self.activated[:, cols], send)

        self.await_weight(8)
        self.await_weight(9)
        self.feed(0, 2)
        self.flush()
        self.spread_end(1, 1, self.normed_two)
        self.spread_end(2, 1, self.proj_back)
        self.feed(1, 0)
        up_grad(0)
        down_grad(0)
        self.await_weight(10)
        self.await_weight(11)
        self.feed(0, last)
        self.collect(2, 0, self.wide_terms(self.pre_back, 4))
        self.collect_far(2, 0)
        self.feed(1, 1)
        up_grad(1)
        down_grad(1)
        self.feed(1, 2)
        self.feed(1, last)
        self.collect(2, 1, self.wide_terms(self.pre_back, 4))
        self.second_norm_back(0)
        up_grad(2)
        down_grad(2)
        self.collect_far(2, 1)
        self.collect(1, 0, self.wide_terms(self.activated, 5))
        self.grad_pass(6)
        self.spread_on(3, 0, self.attended_back)
        up_grad(3)
        self.spread_end(3, 0, self.attended_back)

        def between_first():
            self.grad_pass(7)
            self.second_norm_back(1)
            self.grad_relay(4)

        self.attend_back(0, between_first)
        down_grad(3)
        self.collect(3, 0, self.input_terms)
        self.grad_pass(9)
        self.spread_on(3, 1, self.attended_back)
        self.collect_far(3, 0)
        self.spread_sent(2)
        self.grad_relay(5)
        self.spread_end(3, 1, self.attended_back)
        self.grad_make(PO, self.attended_back, self.mixed[...])
        self.grad_pass(10)

        def between_second():
            self.grad_pass(11)
            self.grad_relay(6)
            self.grad_relay(7)
            self.grad_relay(8)

        self.attend_back(1, between_second)
        self.collect(3, 1, self.input_terms)
        self.collect_far(3, 1)
        self.grad_make(PV, self.normed_one, self.values[...])
        self.grad_pass(PO)
        self.grad_cross(4)
        self.grad_cross(5)
        self.grad_make(PQ, self.normed_one, self.queries[...])
        self.grad_make(PK, self.normed_one, self.keys[...])
        self.collect(1, 1, self.wide_terms(self.activated, 5))
        self.collect_far(1, 0)
        self.collect_far(1, 1)
        self.grad_relay(9)
        self.grad_pass(PV)
        self.grad_cross(8)
        self.grad_relay(10)
        self.grad_relay(11)
        self.first_norm_back(0)
        self.first_norm_back(1)
        self.give_vectors()
        self.grad_pass(PQ)
        self.grad_relay(PO)
        self.grad_relay(PV)
        self.grad_pass(PK)
        self.give_result(0)
        for piece in range(4, pieces):
            self.grad_end(piece)
        self.end_vectors()
        self.give_result(1)
        self.last_vectors()
        for piece in (PO, PV, PQ, PK):
            self.grad_end(piece)
        for kind in (0, 1, 3):
            self.spread_sent(kind)
        for one in self.late + self.stage_sends[0] + self.stage_sends[1]:
            one.wait_send()
        for piece in range(pieces):
            self.weight_sent(piece)
            self.grad_sent(piece)
        if self.own_vectors:
            for step in range(1, self.dps):
                self.vector_copy(step).wait_send()
                self.share_copy(step).wait_send()
            for step in range(1, 4):
                self.group_copy(step).wait_send()


def layer_kernel(size, names, *refs):
    named = dict(zip(names, refs))
    named["small"] = [named[name] for name in names if name.startswith("small_")]
    Layer(size, named).run()


def fused_layer(size, counts, tau, images, out_grad, small, weights):
    width, shard, part, rows, pad = (size[key] for key in ("width", "shard", "part", "rows", "pad"))
    lines, dps, pieces = size["lines"], size["dps"], 4 + 2 * size["chunks"]
    units = size["chunks"] * TILE
    vmem = pl.BlockSpec(memory_space=pltpu.VMEM)
    anywhere = pl.BlockSpec(memory_space=pl.ANY)
    vector_shape = (16, 128) if size["own_vectors"] else (16, width)
    outputs = {
        "rows_g": ((2,) + images.shape, BF16),
        "weight_g": ((shard, pieces * TILE + 2 * TILE), F32),
        "vector_g": (vector_shape, F32),
    }
    four = lines == 4
    channels = pieces + (len(PAIR_FIRST) if four else 0)
    pair_slots = pieces * lines - (len(LINE_FIRST) * (lines - 1) if four else 0)
    sum_channels = pieces + (len(LINE_FIRST) if four else 0)
    lines_in = 4 if four else lines - 1
    dma = pltpu.SemaphoreType.DMA
    vm = pltpu.VMEM
    scratch = {
        "weights": vm((pieces, width, TILE), BF16),
        "normed_one": vm((2 * rows, width), BF16),
        "normed_two": vm((2 * rows, width), BF16),
        "proj_back": vm((2 * rows, width), BF16),
        "attended_back": vm((2 * rows, width), BF16),
        "queries": vm((2 * rows, TILE), BF16),
        "keys": vm((2 * rows, TILE), BF16),
        "values": vm((2 * rows, TILE), BF16),
        "mixed": vm((2 * rows, TILE), BF16),
        "mixed_turned": vm((2, TILE, rows), F32),
        "log_total": vm((2, size["heads"], rows), F32),
        "activated": vm((2 * rows, units), BF16),
        "pre_back": vm((2 * rows, units), BF16),
        "turned": vm((TILE, 2 * rows), BF16),
        "mixed_back": vm((rows, TILE), BF16),
        "key_sum": vm((rows, TILE), F32),
        "value_sum": vm((rows, TILE), F32),
        "probs": vm((rows, rows), BF16),
        "score_back": vm((rows, rows), BF16),
        "stage": vm((2, 2, pad, width), BF16),
        "keep": vm((2, 2, 2, pad, width), F32),
        "sib_in": vm((4, 2, 2, pad, width), BF16),
        "far_in": vm((4, 2, pad, width), BF16),
        "after_attn": vm((2, part, width), F32),
        "attn_back": vm((2, part, width), F32),
        "wide_sums": vm((pieces - 4, width, TILE), BF16),
        "pair_in": vm((pair_slots, shard, TILE), BF16),
        "line_in": vm((sum_channels, lines_in, shard, TILE), BF16),
        "vectors": vm((16, width), F32),
        "sums": vm((16, width), F32),
        "wz_send": dma((channels, lines_in)),
        "wz_recv": dma((channels, lines - 1)),
        "wx_send": dma((pieces, lines)),
        "wx_recv": dma((pieces, lines)),
        "wl_sem": dma((pieces,)),
        "ag_send": dma((4, 2, 3)),
        "ag_recv": dma((4, 2, 3)),
        "rs_send": dma((4, 2, 3)),
        "rs_recv": dma((4, 2, 3)),
        "gx_send": dma((pieces, lines)),
        "gx_recv": dma((pieces, lines)),
        "gz_send": dma((sum_channels, lines - 1)),
        "gz_recv": dma((sum_channels, lines_in)),
    }
    if size["own_vectors"]:
        scratch |= {
            "own_packed": vm((16, 128), F32),
            "vectors_in": vm((dps, 16, 128), F32),
            "shares": vm((dps, 16, 128), F32),
            "shares_in": vm((dps - 1, 16, 128), F32),
            "group": vm((4, 16, 128), F32),
            "v_send": dma((2, dps - 1)),
            "v_recv": dma((2, dps - 1)),
            "m_send": dma((3,)),
            "m_recv": dma((3,)),
        }
    inputs = ["counts", "tau", "images", "out_grad"] + [f"small_{at}" for at in range(len(small))]
    inputs += ["query_w", "key_w", "value_w", "out_w", "up_w", "down_w"]
    names = inputs + list(outputs) + list(scratch)
    return pl.pallas_call(
        functools.partial(layer_kernel, size, names),
        out_shape=[jax.ShapeDtypeStruct(*spec) for spec in outputs.values()],
        in_specs=[pl.BlockSpec(memory_space=pltpu.SMEM)] * 2
        + [vmem] * (2 + len(small))
        + [anywhere] * 6,
        out_specs=[vmem] * len(outputs),
        scratch_shapes=list(scratch.values()),
        compiler_params=pltpu.CompilerParams(
            collective_id=0, has_side_effects=True, vmem_limit_bytes=65024 * 2**10
        ),
    )(counts, tau, images, out_grad, *small, *weights)


def on_device(
    images,
    counts,
    first_gain,
    first_shift,
    query_weight,
    query_bias,
    key_weight,
    value_weight,
    value_bias,
    out_weight,
    out_bias,
    second_gain,
    second_shift,
    up_weight,
    up_bias,
    down_weight,
    down_bias,
    clip_tau,
    out_grad,
):
    part, width = images.shape[2:]
    dps = lax.axis_size("dp")
    dp_at = lax.axis_index("dp")
    shard = query_weight.shape[0]
    pad = (part + 15) // 16 * 16
    size = {
        "width": width,
        "shard": shard,
        "part": part,
        "pad": pad,
        "rows": pad * lax.axis_size("mp"),
        "dps": dps,
        "lines": dps // 2,
        "heads": query_weight.shape[1] // HD,
        "chunks": up_weight.shape[1] // TILE,
        "own_vectors": shard == 128,
    }
    bias_cols = query_bias.shape[1]
    parts = [first_gain, first_shift, out_bias, second_gain, second_shift, down_bias, up_bias[0]]
    if size["own_vectors"]:
        small = [one.reshape(1, -1) for one in parts] + [query_bias, value_bias]
    else:
        whole = [lax.all_gather(one, "dp", axis=0, tiled=True) for one in parts]
        rest = [
            jnp.pad(lax.all_gather(one[0], "dp", axis=0, tiled=True), (0, width - TILE))
            for one in (query_bias, value_bias)
        ]
        filler = jnp.zeros((width,), BF16)
        small = [jnp.stack(whole + [filler] + rest + [filler] * 6).astype(F32)]
    weights = (query_weight, key_weight, value_weight, out_weight, up_weight, down_weight)
    rows_g, weight_g, vector_g = fused_layer(
        size, counts.reshape(-1), clip_tau.reshape(1, 1), images, out_grad, small, weights
    )
    columns, units = query_weight.shape[1], up_weight.shape[1]
    edges = [0, columns, 2 * columns, 3 * columns, 4 * columns]
    edges += [edges[-1] + units, edges[-1] + 2 * units]
    query_g, key_g, value_g, out_g, up_g, down_g = (
        weight_g[:, low:high] for low, high in zip(edges[:-1], edges[1:])
    )
    if size["own_vectors"]:
        vectors = [vector_g[row] for row in range(7)]
        query_bias_g = vector_g[DQB : DQB + 1, :bias_cols]
        value_bias_g = vector_g[DVB : DVB + 1, :bias_cols]
        peaks = vector_g[PEAK, : size["heads"]]
        clipped_query = weight_g[:, edges[-1] : edges[-1] + columns]
        clipped_key = weight_g[:, edges[-1] + columns :]
        clipped_bias = vector_g[PEAK + 1 : PEAK + 2, :bias_cols]
    else:
        mine = vector_g[:DUB]
        mine = lax.psum(mine, "mp")
        mine = lax.psum_scatter(mine, "dp", scatter_dimension=1, tiled=True)
        up_bias_g = lax.psum_scatter(vector_g[DUB], "dp", scatter_dimension=0, tiled=True)
        vectors = [mine[row] for row in range(6)] + [up_bias_g]
        both = vector_g[DQB : DVB + 1, :TILE]
        both = lax.psum_scatter(both, "dp", scatter_dimension=1, tiled=True)
        query_bias_g, value_bias_g = both[0:1], both[1:2]
        peaks = lax.pmax(vector_g[PEAK, : size["heads"]], "dp")
        head_root = jnp.sqrt(clip_tau / jnp.maximum(peaks, clip_tau))
        column_root = jnp.repeat(head_root, HD)
        clipped_query = query_weight.astype(F32) * column_root[None, :]
        clipped_key = key_weight.astype(F32) * column_root[None, :]
        bias_root = lax.dynamic_slice(column_root, (dp_at * bias_cols,), (bias_cols,))
        clipped_bias = query_bias.astype(F32) * bias_root[None, :]
    return (
        rows_g[0],
        rows_g[1],
        vectors[DG1],
        vectors[DS1],
        query_g,
        query_bias_g,
        key_g,
        value_g,
        value_bias_g,
        out_g,
        vectors[DOB],
        vectors[DG2],
        vectors[DS2],
        up_g,
        vectors[DUB][None, :],
        down_g,
        vectors[DDB],
        peaks,
        clipped_query,
        clipped_key,
        clipped_bias,
    )


def solution(mesh):
    rows = P(None, "dp", "mp", None)
    wide, small, bias = P("dp", "mp"), P("dp"), P("mp", "dp")
    return jax.shard_map(
        on_device,
        mesh=mesh,
        in_specs=(
            rows,
            P(None, "dp"),
            small,
            small,
            wide,
            bias,
            wide,
            wide,
            bias,
            wide,
            small,
            small,
            small,
            wide,
            bias,
            wide,
            small,
            P(),
            rows,
        ),
        out_specs=(
            rows,
            rows,
            small,
            small,
            wide,
            bias,
            wide,
            wide,
            bias,
            wide,
            small,
            small,
            small,
            wide,
            bias,
            wide,
            small,
            P("mp"),
            wide,
            wide,
            bias,
        ),
        check_vma=False,
    )
```

```python
import functools
import math

import jax
import jax.numpy as jnp
from jax import lax
from jax.experimental import pallas as pl
from jax.experimental.pallas import tpu as pltpu
from jax.sharding import PartitionSpec as P

HD = 64
IMG_LEN = 577
F32 = jnp.float32
BF16 = jnp.bfloat16
MESH = pl.DeviceIdType.MESH
TILE = 256
PQ, PK, PV, PO = 0, 1, 2, 3
PAIR_FIRST = (6, 9)
LINE_FIRST = (4, 5, 8)
DIRECT = (0, 1)
G1, S1, OB, G2, S2, DB, UB, QB, VB = 0, 1, 2, 3, 4, 5, 6, 8, 9
DG1, DS1, DOB, DG2, DS2, DDB, DUB, DQB, DVB, PEAK = 0, 1, 2, 3, 4, 5, 6, 7, 8, 9


def dot_nn(left, right):
    return lax.dot_general(left, right, (((1,), (0,)), ((), ())), preferred_element_type=F32)


def dot_nt(left, right):
    return lax.dot_general(left, right, (((1,), (1,)), ((), ())), preferred_element_type=F32)


def dot_tn(left, right):
    return lax.dot_general(left, right, (((0,), (0,)), ((), ())), preferred_element_type=F32)


def standardize(rows):
    center = rows - jnp.mean(rows, axis=-1, keepdims=True)
    inverse = lax.rsqrt(jnp.mean(center * center, axis=-1, keepdims=True) + 1e-05)
    return center * inverse, inverse


def norm_back(incoming, scaled, inverse, gain):
    upward = incoming * gain
    return inverse * (
        upward
        - jnp.mean(upward, axis=-1, keepdims=True)
        - scaled * jnp.mean(upward * scaled, axis=-1, keepdims=True)
    )


def each(low, high, body):
    if high - low <= 8:
        for at in range(low, high):
            body(at)
    else:

        def step(at, carry):
            body(at)
            return carry

        lax.fori_loop(low, high, step, 0)


def tiles(width, body, at_once=2):
    def step(at, carry):
        for more in range(at_once):
            body(at_once * at + more)
        return carry

    lax.fori_loop(0, width // (at_once * TILE), step, 0)


def sum_rows(rows):
    return jnp.sum(rows, axis=0, keepdims=True)


class Layer:
    def __init__(self, size, refs):
        self.__dict__.update(size)
        self.__dict__.update(refs)
        self.dp_at = lax.axis_index("dp")
        self.mp_at = lax.axis_index("mp")
        self.line_at = self.dp_at // 2
        self.pair_at = lax.rem(self.dp_at, 2)
        self.chip_at = self.mp_at // 2
        self.core_at = lax.rem(self.mp_at, 2)
        self.sib = (self.dp_at, self.chip_at * 2 + 1 - self.core_at)
        self.across = (self.dp_at, (1 - self.chip_at) * 2 + self.core_at)
        self.pair = (self.line_at * 2 + 1 - self.pair_at, self.mp_at)
        self.middle = (self.line_at == 1) | (self.line_at == 2)
        self.pieces = 4 + 2 * self.chunks
        self.pair_first = PAIR_FIRST if self.lines == 4 else ()
        self.line_first = LINE_FIRST if self.lines == 4 else ()
        self.pair_slots = (self.pieces - len(self.line_first)) * self.lines
        self.rest = None
        self.stage_sends = [[], []]
        self.spread_sends = [[], [], [], []]
        self.late = []

    def line_of(self, step):
        return lax.rem(self.line_at + step + self.lines, self.lines)

    def line_peer(self, step):
        return (self.line_of(step) * 2 + self.pair_at, self.mp_at)

    def slot(self, line, pair):
        return pl.ds(pl.multiple_of((line * 2 + pair) * self.shard, self.shard), self.shard)

    def block(self, micro, chip, core):
        start = micro * self.rows + (chip * 2 + core) * self.pad
        return pl.ds(pl.multiple_of(start, 16), self.pad)

    def own_block(self, micro):
        return self.block(micro, self.chip_at, self.core_at)

    def source(self, piece):
        if piece < 4:
            return (self.query_w, self.key_w, self.value_w, self.out_w)[piece]
        which, chunk = (piece - 4) % 2, (piece - 4) // 2
        return (self.up_w, self.down_w)[which].at[:, pl.ds(chunk * TILE, TILE)]

    def copy(self, src, dst, send_sem, recv_sem, device):
        return pltpu.make_async_remote_copy(
            src_ref=src,
            dst_ref=dst,
            send_sem=send_sem,
            recv_sem=recv_sem,
            device_id=device,
            device_id_type=MESH,
        )

    def channels(self, piece):
        if piece in self.pair_first:
            return ((piece, False), (self.pieces + self.pair_first.index(piece), True))
        return ((piece, False),)

    def shard_place(self, piece, line, other):
        pair = 1 - self.pair_at if other else self.pair_at
        return self.weights.at[piece, self.slot(line, pair)]

    def broad(self, piece, channel, other, step):
        place = self.shard_place(piece, self.line_at, other)
        return self.copy(
            place if other else self.source(piece),
            place,
            self.wz_send.at[channel, step - 1],
            self.wz_recv.at[channel, step - 1],
            self.line_peer(step),
        )

    def broad_in(self, piece, channel, other, step):
        place = self.shard_place(piece, self.line_of(-step), other)
        return self.copy(
            place,
            place,
            self.wz_send.at[channel, step - 1],
            self.wz_recv.at[channel, step - 1],
            self.line_peer(-step),
        )

    def broad_each(self, piece, channel, other, act):
        def one(step):
            if self.lines == 4 and step != 2:
                @pl.when(self.line_at != (3 if step == 1 else 0))
                def _():
                    act(self.broad(piece, channel, other, step))
            else:
                act(self.broad(piece, channel, other, step))

        each(1, self.lines, one)

    def relay(self, piece, channel, other, act):
        if self.lines != 4:
            return

        @pl.when(self.middle)
        def _():
            place = self.shard_place(piece, 3 * (2 - self.line_at), other)
            end = (3 * (self.line_at - 1) * 2 + self.pair_at, self.mp_at)
            act(
                self.copy(
                    place,
                    place,
                    self.wz_send.at[channel, 3],
                    self.wz_recv.at[channel, 2 * (self.line_at - 1)],
                    end,
                )
            )

    def weight_pair(self, piece, step, own):
        place = self.shard_place(piece, self.line_of(-step), False)
        return self.copy(
            self.source(piece) if own else place,
            place,
            self.wx_send.at[piece, step],
            self.wx_recv.at[piece, step],
            self.pair,
        )

    def weight_pair_in(self, piece, step):
        place = self.shard_place(piece, self.line_of(-step), True)
        return self.copy(
            place, place, self.wx_send.at[piece, step], self.wx_recv.at[piece, step], self.pair
        )

    def weight_local(self, piece):
        return pltpu.make_async_copy(
            self.source(piece),
            self.shard_place(piece, self.line_at, False),
            self.wl_sem.at[piece],
        )

    def send_pair(self, piece):
        self.weight_pair(piece, 0, True).start()

    def send_weight(self, piece, pair=True):
        if pair:
            self.send_pair(piece)
        self.broad_each(piece, piece, False, lambda one: one.start())
        self.weight_local(piece).start()

    def pass_weight(self, piece):
        self.flush()
        if piece in self.pair_first:
            self.weight_pair_in(piece, 0).wait_recv()
            channel, other = self.channels(piece)[1]
            self.broad_each(piece, channel, other, lambda one: one.start())
            return

        if self.lines == 4:
            self.pass_shard(piece, 2)
            self.pass_shard(piece, jnp.where(self.line_at < 2, 3, 1))
            self.rest = piece
        else:
            each(1, self.lines, lambda step: self.pass_shard(piece, step))

    def pass_shard(self, piece, step):
        self.broad_in(piece, piece, False, step).wait_recv()
        if self.lines == 4 and isinstance(step, int):
            self.relay(piece, piece, False, lambda one: one.start())
        self.weight_pair(piece, step, False).start()

    def flush(self):
        if self.rest is not None:
            self.pass_shard(self.rest, jnp.where(self.line_at < 2, 1, 3))
        self.rest = None

    def relay_weight(self, piece):
        for channel, other in self.channels(piece):
            if piece in self.pair_first:
                self.broad_in(piece, channel, other, 2).wait_recv()
                self.relay(piece, channel, other, lambda one: one.start())

    def await_weight(self, piece):
        self.weight_local(piece).wait()
        if piece in self.pair_first:
            for channel, other in self.channels(piece):
                for step in (1, 3):
                    self.broad_in(piece, channel, other, step).wait_recv()
        else:
            each(0, self.lines, lambda step: self.weight_pair_in(piece, step).wait_recv())

    def weight_sent(self, piece):
        self.weight_pair(piece, 0, True).wait_send()
        for channel, other in self.channels(piece):
            self.broad_each(piece, channel, other, lambda one: one.wait_send())
            self.relay(piece, channel, other, lambda one: one.wait_send())
        if piece not in self.pair_first:
            each(1, self.lines, lambda step: self.weight_pair(piece, step, False).wait_send())

    def spread_copy(self, kind, micro, ref, which):
        place = ref.at[self.own_block(micro)]
        if which == 2:
            place = ref.at[self.block(micro, 1 - self.chip_at, self.core_at)]
        return self.copy(
            place,
            place,
            self.ag_send.at[kind, micro, which],
            self.ag_recv.at[kind, micro, which],
            self.across if which == 0 else self.sib,
        )

    def spread_in(self, kind, micro, ref, which):
        chip = self.chip_at if which == 1 else 1 - self.chip_at
        core = self.core_at if which == 0 else 1 - self.core_at
        place = ref.at[self.block(micro, chip, core)]
        return self.copy(
            place,
            place,
            self.ag_send.at[kind, micro, which],
            self.ag_recv.at[kind, micro, which],
            self.across if which == 0 else self.sib,
        )

    def spread(self, kind, micro, ref):
        for which in (0, 1):
            self.spread_copy(kind, micro, ref, which).start()
            self.spread_sends[kind].append((micro, ref, which))

    def spread_on(self, kind, micro, ref):
        self.spread_in(kind, micro, ref, 0).wait_recv()
        self.spread_copy(kind, micro, ref, 2).start()
        self.spread_sends[kind].append((micro, ref, 2))

    def spread_sent(self, kind):
        for micro, ref, which in self.spread_sends[kind]:
            self.spread_copy(kind, micro, ref, which).wait_send()
        self.spread_sends[kind] = []

    def spread_end(self, kind, micro, ref):
        self.spread_in(kind, micro, ref, 1).wait_recv()
        self.spread_in(kind, micro, ref, 2).wait_recv()

    def collect(self, kind, micro, terms):
        for one in self.stage_sends[micro]:
            one.wait_send()
        self.stage_sends[micro] = []
        held = 1 if kind == 1 else 0
        for half, chip in ((0, 1 - self.chip_at), (1, self.chip_at)):
            start = pl.multiple_of(micro * self.rows + chip * 2 * self.pad, 16)
            stage, keep = self.stage.at[micro, half], self.keep.at[held, micro, half]

            def tile_of(tile):
                cols = pl.ds(pl.multiple_of(tile * TILE, TILE), TILE)
                product = terms(pl.ds(start, 2 * self.pad), cols)
                low, high = product[: self.pad], product[self.pad :]
                keep[:, cols] = jnp.where(self.core_at == 0, low, high)
                stage[:, cols] = jnp.where(self.core_at == 0, high, low).astype(BF16)

            tiles(self.width, tile_of, 1 if kind == 1 else 4)
            one = self.copy(
                stage,
                self.sib_in.at[kind, micro, half],
                self.rs_send.at[kind, micro, half],
                self.rs_recv.at[kind, micro, half],
                self.sib,
            )
            one.start()
            self.stage_sends[micro].append(one)

    def collect_far(self, kind, micro):
        incoming = self.sib_in.at[kind, micro, 0]
        self.copy(
            incoming,
            incoming,
            self.rs_send.at[kind, micro, 0],
            self.rs_recv.at[kind, micro, 0],
            self.sib,
        ).wait_recv()
        held = self.keep[1 if kind == 1 else 0, micro, 0]
        incoming[...] = (held + incoming[...].astype(F32)).astype(BF16)
        one = self.copy(
            incoming,
            self.far_in.at[kind, micro],
            self.rs_send.at[kind, micro, 2],
            self.rs_recv.at[kind, micro, 2],
            self.across,
        )
        one.start()
        self.late.append(one)

    def collected(self, kind, micro):
        near, far = self.sib_in.at[kind, micro, 1], self.far_in.at[kind, micro]
        self.copy(
            near, near, self.rs_send.at[kind, micro, 1], self.rs_recv.at[kind, micro, 1], self.sib
        ).wait_recv()
        self.copy(
            far, far, self.rs_send.at[kind, micro, 2], self.rs_recv.at[kind, micro, 2], self.across
        ).wait_recv()
        total = self.keep[1 if kind == 1 else 0, micro, 1] + near[...].astype(F32)
        return (total + far[...].astype(F32))[: self.part]

    def summed(self, piece):
        if piece < 4:
            return self.proj_back.at[: self.width, piece * TILE : (piece + 1) * TILE]
        return self.wide_sums.at[piece - 4]

    def sum_place(self, piece, line, other):
        pair = 1 - self.pair_at if other else self.pair_at
        return self.summed(piece).at[self.slot(line, pair)]

    def sum_channels(self, piece):
        if piece in self.line_first:
            return ((piece, False), (self.pieces + self.line_first.index(piece), True))
        return ((piece, False),)

    def relayed(self, piece):
        return self.lines == 4 and piece not in DIRECT

    def out_columns(self, piece):
        at = piece if piece < 4 else 4 + self.chunks * ((piece - 4) % 2) + (piece - 4) // 2
        return self.weight_g.at[:, pl.ds(at * TILE, TILE)]

    def pair_place(self, piece, line):
        if piece in self.line_first:
            return self.pair_in.at[self.pair_slots + self.line_first.index(piece)]
        before = sum(1 for other in self.line_first if other < piece)
        return self.pair_in.at[(piece - before) * self.lines + line]

    def grad_pair(self, piece, line):
        at = 0 if piece in self.line_first else line
        return self.copy(
            self.sum_place(piece, line, True),
            self.pair_place(piece, line),
            self.gx_send.at[piece, at],
            self.gx_recv.at[piece, at],
            self.pair,
        )

    def line_source(self, piece, line, other):
        if piece in self.line_first:
            return self.sum_place(piece, line, other)
        return self.pair_place(piece, line)

    def grad_line(self, piece, channel, other, step):
        line = self.line_of(step)
        target, at = line, step - 1
        if self.relayed(piece) and step != 2:
            far = self.line_at == (3 if step == 1 else 0)
            target = jnp.where(far, 2 if step == 1 else 1, line)
            at = jnp.where(far, 3, step - 1)
        return self.copy(
            self.line_source(piece, line, other),
            self.line_in.at[channel, at],
            self.gz_send.at[channel, step - 1],
            self.gz_recv.at[channel, at],
            (target * 2 + self.pair_at, self.mp_at),
        )

    def grad_line_in(self, channel, at):
        place = self.line_in.at[channel, at]
        return self.copy(
            place, place, self.gz_send.at[channel, 0], self.gz_recv.at[channel, at], self.pair
        )

    def grad_make(self, piece, left, right, send=True):
        out = self.summed(piece)

        def one(tile):
            cols = pl.ds(pl.multiple_of(tile * TILE, TILE), TILE)
            out[cols, :] = dot_tn(left[:, cols], right).astype(BF16)

        tiles(self.width, one)
        if send:
            self.grad_send(piece)

    def grad_send(self, piece):
        if piece in self.line_first:
            for channel, other in self.sum_channels(piece):
                for step in (1, 3):
                    self.grad_line(piece, channel, other, step).start()

                @pl.when(jnp.logical_not(self.middle))
                def _():
                    self.grad_line(piece, channel, other, 2).start()
        else:
            each(0, self.lines, lambda line: self.grad_pair(piece, line).start())

    def grad_pass(self, piece):
        def one(step, wait=True):
            line = self.line_of(step)
            if wait:
                self.grad_pair(piece, line).wait_recv()
            ref = self.pair_place(piece, line)
            total = self.sum_place(piece, line, False)[...].astype(F32) + ref[...].astype(F32)
            ref[...] = total.astype(BF16)
            self.grad_line(piece, piece, False, step).start()

        if piece in self.line_first:
            return
        if self.relayed(piece):
            one(1)
            one(3)
            self.grad_pair(piece, self.line_of(2)).wait_recv()
            pl.when(jnp.logical_not(self.middle))(lambda: one(2, False))
        else:
            each(1, self.lines, one)

    def grad_relay(self, piece):
        if not self.relayed(piece):
            return

        @pl.when(self.middle)
        def _():
            for channel, other in self.sum_channels(piece):
                line = self.line_of(2)
                self.grad_line_in(channel, 3).wait_recv()
                ref = self.line_source(piece, line, other)
                total = ref[...].astype(F32) + self.line_in[channel, 3].astype(F32)
                if piece not in self.line_first:
                    total = total + self.sum_place(piece, line, False)[...].astype(F32)
                ref[...] = total.astype(BF16)
                self.grad_line(piece, channel, other, 2).start()

    def line_total(self, piece, channel, ref):
        for step in range(1, self.lines):

            def one():
                self.grad_line_in(channel, step - 1).wait_recv()
                ref[...] += self.line_in[channel, step - 1].astype(F32)

            if self.relayed(piece) and step != 2:
                pl.when(self.line_at != (0 if step == 1 else 3))(one)
            else:
                one()

    def grad_cross(self, piece):
        if piece not in self.line_first:
            return
        ref = self.sum_place(piece, self.line_at, True)
        total = self.out_columns(piece)
        total[...] = ref[...].astype(F32)
        self.line_total(piece, self.sum_channels(piece)[1][0], total)
        ref[...] = total[...].astype(BF16)
        self.grad_pair(piece, self.line_at).start()

    def grad_end(self, piece):
        ref = self.out_columns(piece)
        self.grad_pair(piece, self.line_at).wait_recv()
        came = self.pair_place(piece, self.line_at)[...].astype(F32)
        ref[...] = self.sum_place(piece, self.line_at, False)[...].astype(F32) + came
        self.line_total(piece, piece, ref)

    def grad_sent(self, piece):
        if piece in self.line_first:
            self.grad_pair(piece, self.line_at).wait_send()
        else:
            each(0, self.lines, lambda line: self.grad_pair(piece, line).wait_send())
        for channel, other in self.sum_channels(piece):
            each(
                1,
                self.lines,
                lambda step: self.grad_line(piece, channel, other, step).wait_send(),
            )

    def clip(self, peaks):
        root = jnp.sqrt(self.tau[0, 0] / jnp.maximum(peaks, self.tau[0, 0]))
        head = lax.broadcasted_iota(jnp.int32, (1, TILE), 1) // HD
        roots = jnp.zeros((1, TILE), F32)
        for at in range(self.heads):
            roots = jnp.where(head == at, root[:, at : at + 1], roots)
        first = (4 + 2 * self.chunks) * TILE
        mine = self.slot(self.line_at, self.pair_at)
        for at, piece in enumerate((PQ, PK)):
            cols = slice(first + at * TILE, first + (at + 1) * TILE)
            self.weight_g[:, cols] = self.weights[piece, mine, :].astype(F32) * roots
        low, high = self.own_packed[8:9, :], self.own_packed[9:10, :]
        bias = low * roots[:, 0:128] + high * roots[:, 128:256]
        return bias

    def vector_copy(self, step):
        return self.copy(
            self.own_packed,
            self.vectors_in.at[self.dp_at],
            self.v_send.at[0, step - 1],
            self.v_recv.at[0, step - 1],
            (lax.rem(self.dp_at + step, self.dps), self.mp_at),
        )

    def vector_copy_in(self, step):
        origin = lax.rem(self.dp_at - step + self.dps, self.dps)
        place = self.vectors_in.at[origin]
        return self.copy(
            place,
            place,
            self.v_send.at[0, step - 1],
            self.v_recv.at[0, step - 1],
            (origin, self.mp_at),
        )

    def share_copy(self, step):
        target = lax.rem(self.dp_at + step, self.dps)
        return self.copy(
            self.shares.at[target],
            self.shares_in.at[step - 1],
            self.v_send.at[1, step - 1],
            self.v_recv.at[1, step - 1],
            (target, self.mp_at),
        )

    def group_copy(self, step):
        return self.copy(
            self.group.at[0],
            self.group.at[step],
            self.m_send.at[step - 1],
            self.m_recv.at[step - 1],
            (self.dp_at, lax.rem(self.mp_at + step, 4)),
        )

    def pack_vectors(self):
        if not self.own_vectors:
            return
        rows = [ref[...].astype(F32) for ref in self.small[:7]] + [jnp.zeros((1, 128), F32)]
        shift = lax.rem(self.dp_at * 32, 128)
        for ref in self.small[7:]:
            wide = jnp.concatenate([ref[...].astype(F32), jnp.zeros((1, 96), F32)], axis=1)
            wide = pltpu.roll(wide, shift, 1)
            rows.append(jnp.where(self.dp_at < 4, wide, 0.0))
            rows.append(jnp.where(self.dp_at < 4, 0.0, wide))
        self.own_packed[...] = jnp.concatenate(rows + [jnp.zeros((4, 128), F32)], axis=0)

    def take_vectors(self):
        if not self.own_vectors:
            self.vectors[...] = self.small[0][...]
            return
        self.vectors_in[self.dp_at] = self.own_packed[...]
        for step in range(1, self.dps):
            self.vector_copy_in(step).wait_recv()
        rest = self.vectors_in[0, 8:16, :]
        for at in range(1, self.dps):
            rest = rest + self.vectors_in[at, 8:16, :]
        for at in range(self.dps):
            self.vectors[0:8, at * 128 : (at + 1) * 128] = self.vectors_in[at, 0:8, :]
        for row, first in ((QB, 0), (VB, 2)):
            self.vectors[row : row + 1, 0:128] = rest[first : first + 1]
            self.vectors[row : row + 1, 128:256] = rest[first + 1 : first + 2]

    def give_vectors(self):
        if not self.own_vectors:
            self.vector_g[...] = self.sums[...]
            return
        for at in range(self.dps):
            half = (at * 32 // 128) * 128
            self.shares[at, 0:7, :] = self.sums[0:7, at * 128 : (at + 1) * 128]
            self.shares[at, 7:9, :] = self.sums[7:9, half : half + 128]
            self.shares[at, 9:16, :] = self.sums[9:16, 0:128]
        for step in range(1, self.dps):
            self.share_copy(step).start()

    def end_vectors(self):
        if not self.own_vectors:
            return
        total = self.shares[self.dp_at]
        most = total[PEAK : PEAK + 1]
        for step in range(1, self.dps):
            self.share_copy(step).wait_recv()
            came = self.shares_in[step - 1]
            total = total + came
            most = jnp.maximum(most, came[PEAK : PEAK + 1])
        self.group[0] = jnp.concatenate([total[:PEAK], most, total[PEAK + 1 :]], axis=0)
        for step in range(1, 4):
            self.group_copy(step).start()

    def last_vectors(self):
        if not self.own_vectors:
            return
        total = self.group[0]
        most = total[PEAK : PEAK + 1]
        whole = total[0:6]
        for step in range(1, 4):
            self.group_copy(step).wait_recv()
            whole = whole + self.group[step, 0:6, :]
        narrow = jnp.concatenate([total[7:9], self.clip(most), jnp.zeros((5, 128), F32)], axis=0)
        shift = lax.rem(128 - lax.rem(self.dp_at * 32, 128), 128)
        narrow = pltpu.roll(narrow, shift, 1)
        self.vector_g[0:6, :] = whole
        self.vector_g[6:7, :] = total[6:7]
        self.vector_g[7:9, :] = narrow[0:2]
        self.vector_g[9:10, :] = most
        self.vector_g[10:11, :] = narrow[2:3]
        self.vector_g[11:16, :] = jnp.zeros((5, 128), F32)

    def vector(self, row, start=0, size=None):
        size = self.width if size is None else size
        return self.vectors[row : row + 1, pl.ds(start, size)]

    def add_sum(self, row, value, start=0):
        cols = pl.ds(start, value.shape[1])
        self.sums[row : row + 1, cols] = self.sums[row : row + 1, cols] + value

    def mask(self, micro):
        row = self.mp_at * self.part + lax.broadcasted_iota(jnp.int32, (self.part, 1), 0)
        live = jnp.where(self.counts[micro] > 0, 1.0, 0.0).astype(F32)
        return jnp.where(row < IMG_LEN, live, 0.0)

    def put_rows(self, ref, micro, rows):
        filler = jnp.zeros((self.pad - self.part, self.width), F32)
        ref[self.own_block(micro), :] = jnp.concatenate([rows, filler], axis=0).astype(BF16)

    def first_norm(self, micro):
        scaled, _ = standardize(self.images[micro, 0].astype(F32))
        self.put_rows(self.normed_one, micro, scaled * self.vector(G1) + self.vector(S1))
        self.spread(0, micro, self.normed_one)

    def out_rows(self, micro):
        return self.out_grad[micro, 0].astype(F32) * self.mask(micro)

    def project_back(self, micro):
        rows = self.out_rows(micro)
        self.put_rows(self.proj_back, micro, rows)
        self.add_sum(DDB, sum_rows(rows.astype(BF16).astype(F32)))
        self.spread(2, micro, self.proj_back)

    def second_norm(self, micro):
        rows = self.images[micro, 0].astype(F32) + self.collected(0, micro) + self.vector(OB)
        self.after_attn[micro] = rows
        scaled, _ = standardize(rows)
        self.put_rows(self.normed_two, micro, scaled * self.vector(G2) + self.vector(S2))
        self.spread(1, micro, self.normed_two)

    def give_result(self, micro):
        rows = self.after_attn[micro] + self.collected(1, micro) + self.vector(DB)
        self.rows_g[0, micro, 0] = (self.mask(micro) * rows).astype(BF16)

    def second_norm_back(self, micro):
        incoming = self.collected(2, micro)
        scaled, inverse = standardize(self.after_attn[micro])
        rows = self.out_rows(micro) + norm_back(incoming, scaled, inverse, self.vector(G2))
        self.attn_back[micro] = rows
        self.add_sum(DOB, sum_rows(rows.astype(BF16).astype(F32)))
        self.add_sum(DG2, sum_rows(incoming * scaled))
        self.add_sum(DS2, sum_rows(incoming))
        self.put_rows(self.attended_back, micro, rows)
        self.spread(3, micro, self.attended_back)

    def first_norm_back(self, micro):
        incoming = self.collected(3, micro)
        scaled, inverse = standardize(self.images[micro, 0].astype(F32))
        self.add_sum(DG1, sum_rows(incoming * scaled))
        self.add_sum(DS1, sum_rows(incoming))
        rows = self.attn_back[micro] + norm_back(incoming, scaled, inverse, self.vector(G1))
        self.rows_g[1, micro, 0] = rows.astype(BF16)

    def image_rows(self, micro):
        return pl.ds(micro * self.rows, self.rows)

    def counted(self, axis):
        shape = (self.rows, 1) if axis == 0 else (1, self.rows)
        row = lax.broadcasted_iota(jnp.int32, shape, axis)
        block = row // self.pad
        inside = row - block * self.pad
        return (inside < self.part) & (block * self.part + inside < IMG_LEN)

    def head_columns(self, head):
        column = lax.broadcasted_iota(jnp.int32, (self.rows, TILE), 1)
        return column // HD == head

    def project_heads(self, micro):
        scale = 1.0 / math.sqrt(HD)
        part = self.rows // 2

        def half(at, carry):
            rows = pl.ds(pl.multiple_of(micro * self.rows + at * part, 16), part)
            normed = self.normed_one[rows, :]
            query = dot_nn(normed, self.weights[PQ]) + self.vector(QB, 0, TILE)
            self.queries[rows, :] = (query.astype(BF16).astype(F32) * scale).astype(BF16)
            self.keys[rows, :] = dot_nn(normed, self.weights[PK]).astype(BF16)
            value = dot_nn(normed, self.weights[PV]) + self.vector(VB, 0, TILE)
            self.values[rows, :] = value.astype(BF16)
            return carry

        lax.fori_loop(0, 2, half, 0)

    def attend(self, micro, between):
        rows = self.image_rows(micro)
        values = self.turned.at[:, : self.rows]
        values[...] = self.values[rows, :].T
        live = jnp.where(self.counts[micro] > 0, 0.0, -1e30).astype(F32)
        split = (self.rows // 2 + 127) // 128 * 128

        def one_head(head):
            query = jnp.where(self.head_columns(head), self.queries[rows, :], jnp.zeros((), BF16))
            cols = pl.ds(pl.multiple_of(head * HD, HD), HD)
            top = total = mixed = None
            for low, high in ((0, split), (split, self.rows)):
                part = pl.ds(micro * self.rows + low, high - low)
                scores = dot_nt(self.keys[part, :], query)
                scores = jnp.where(self.counted(0)[low:high], scores, -1e30)
                most = jnp.max(scores, axis=0, keepdims=True)
                if top is None:
                    expo = jnp.exp(scores - most)
                    total = jnp.sum(expo, axis=0, keepdims=True)
                    mixed = dot_nn(values[cols, low:high], expo.astype(BF16))
                    top = most
                else:
                    most = jnp.maximum(top, most)
                    again = jnp.exp(top - most)
                    expo = jnp.exp(scores - most)
                    total = total * again + jnp.sum(expo, axis=0, keepdims=True)
                    added = dot_nn(values[cols, low:high], expo.astype(BF16))
                    mixed = mixed * again + added
                    top = most
            self.log_total[micro, pl.ds(head, 1), :] = top + jnp.log(total)
            self.mixed_turned[micro, cols, :] = mixed * (1.0 / total)
            peak = jnp.max(jnp.where(self.counted(1), top, -1e30), axis=1, keepdims=True)
            peak = jnp.where(live < 0.0, -1e30, peak)
            lane = lax.broadcasted_iota(jnp.int32, (1, 128), 1)
            seen = self.sums[PEAK : PEAK + 1, 0:128]
            self.sums[PEAK : PEAK + 1, 0:128] = jnp.where(
                lane == head, jnp.maximum(seen, peak), seen
            )

        def two_heads(at, carry):
            pl.when(at == 1)(between)
            one_head(2 * at)
            one_head(2 * at + 1)
            return carry

        lax.fori_loop(0, self.heads // 2, two_heads, 0)
        self.mixed[rows, :] = self.mixed_turned[micro].T.astype(BF16)

    def attend_back(self, micro, between):
        rows = self.image_rows(micro)
        self.mixed_back[...] = dot_nn(self.attended_back[rows, :], self.weights[PO]).astype(BF16)
        keys = self.turned.at[:, : self.rows]
        outwards = self.turned.at[:, self.rows :]
        keys[...] = self.keys[rows, :].T
        outwards[...] = self.mixed_back[...].T
        self.key_sum[...] = jnp.zeros_like(self.key_sum)
        self.value_sum[...] = jnp.zeros_like(self.value_sum)
        chunk = self.rows // 2

        def one_head(head, carry):
            columns = self.head_columns(head)
            none = jnp.zeros((), BF16)
            query = jnp.where(columns, self.queries[rows, :], none)
            outward = jnp.where(columns, self.mixed_back[...], none)
            cols = pl.ds(pl.multiple_of(head * HD, HD), HD)
            dots = outwards[cols, :].astype(F32) * self.mixed_turned[micro, cols, :]
            delta = jnp.sum(dots, axis=0, keepdims=True)
            log_total = self.log_total[micro, pl.ds(head, 1), :]
            for at in range(2):
                part = pl.ds(micro * self.rows + at * chunk, chunk)
                here = pl.ds(at * chunk, chunk)
                scores = dot_nt(self.keys[part, :], query)
                counted = self.counted(0)[at * chunk : (at + 1) * chunk]
                probs = jnp.where(counted, jnp.exp(scores - log_total), 0.0)
                prob_back = dot_nt(self.values[part, :], outward)
                self.probs[here, :] = probs.astype(BF16)
                self.score_back[here, :] = (probs * (prob_back - delta)).astype(BF16)
            self.value_sum[...] += dot_nn(self.probs[...], outward)
            self.key_sum[...] += dot_nn(self.score_back[...], query)
            self.mixed_turned[micro, cols, :] = dot_nn(keys[cols, :], self.score_back[...])
            return carry

        def with_between(head, carry):
            pl.when(head == self.heads // 2)(between)
            return one_head(head, carry)

        if micro == 0:
            lax.fori_loop(0, self.heads // 2, one_head, 0)
            between()
            lax.fori_loop(self.heads // 2, self.heads, one_head, 0)
        else:
            lax.fori_loop(0, self.heads, with_between, 0)
        scale = 1.0 / math.sqrt(HD)
        query_back = (self.mixed_turned[micro] * scale).T.astype(BF16)
        value_back = self.value_sum[...].astype(BF16)
        self.queries[rows, :] = query_back
        self.keys[rows, :] = self.key_sum[...].astype(BF16)
        self.values[rows, :] = value_back
        self.add_sum(DQB, sum_rows(query_back.astype(F32)))
        self.add_sum(DVB, sum_rows(value_back.astype(F32)))

    def feed(self, micro, chunk):
        cols = pl.ds(chunk * TILE, TILE)
        up, down = self.weights.at[4 + 2 * chunk], self.weights.at[5 + 2 * chunk]
        part = self.rows // 2

        def half(at, carry):
            rows = pl.ds(pl.multiple_of(micro * self.rows + at * part, 16), part)
            hidden = dot_nn(self.normed_two[rows, :], up[...])
            hidden = hidden + self.vector(UB, chunk * TILE, TILE)
            gate = jax.nn.sigmoid(1.702 * hidden)
            self.activated[rows, cols] = (hidden * gate).astype(BF16)
            back = dot_nn(self.proj_back[rows, :], down[...])
            back = back * (gate + 1.702 * hidden * gate * (1.0 - gate))
            back = back.astype(BF16)
            self.pre_back[rows, cols] = back
            self.add_sum(DUB, sum_rows(back.astype(F32)), chunk * TILE)
            return carry

        lax.fori_loop(0, 2, half, 0)

    def out_terms(self, rows, cols):
        return dot_nt(self.mixed[rows, :], self.weights[PO, cols, :])

    def wide_terms(self, ref, first):
        def terms(rows, cols):
            total = None
            for chunk in range(self.chunks):
                one = dot_nt(
                    ref[rows, chunk * TILE : (chunk + 1) * TILE],
                    self.weights[first + 2 * chunk, cols, :],
                )
                total = one if total is None else total + one
            return total

        return terms

    def input_terms(self, rows, cols):
        total = dot_nt(self.queries[rows, :], self.weights[PQ, cols, :])
        total = total + dot_nt(self.keys[rows, :], self.weights[PK, cols, :])
        return total + dot_nt(self.values[rows, :], self.weights[PV, cols, :])

    def enter(self):
        barrier = pltpu.get_barrier_semaphore()
        peers = [self.sib, self.across]
        if self.own_vectors:
            peers.append((self.dp_at, (1 - self.chip_at) * 2 + 1 - self.core_at))
        for peer in peers:
            pl.semaphore_signal(barrier, inc=1, device_id=peer, device_id_type=MESH)
        if self.own_vectors:

            def hail(step):
                peer = (lax.rem(self.dp_at + step, self.dps), self.mp_at)
                pl.semaphore_signal(barrier, inc=1, device_id=peer, device_id_type=MESH)

            each(1, self.dps, hail)
            pl.semaphore_wait(barrier, 3 + self.dps - 1)
        else:
            pl.semaphore_signal(barrier, inc=1, device_id=self.pair, device_id_type=MESH)

            def hail(step):
                peer = self.line_peer(step)
                pl.semaphore_signal(barrier, inc=1, device_id=peer, device_id_type=MESH)

            each(1, self.lines, hail)
            pl.semaphore_wait(barrier, 2 + self.lines)

    def run(self):
        pieces = self.pieces
        last = self.chunks - 1
        self.pack_vectors()
        self.enter()
        if self.own_vectors:
            for step in range(1, self.dps):
                self.vector_copy(step).start()
        for piece in (PQ, PK, PV):
            self.send_weight(piece)
        self.sums[...] = jnp.zeros_like(self.sums)
        self.sums[PEAK : PEAK + 1, :] = jnp.full((1, self.width), -1e30, F32)
        self.take_vectors()
        for micro in (0, 1):
            self.first_norm(micro)
        self.pass_weight(PQ)
        self.pass_weight(PK)
        self.send_weight(PO)
        self.spread_on(0, 0, self.normed_one)
        self.pass_weight(PV)
        self.await_weight(PQ)
        self.spread_on(0, 1, self.normed_one)
        self.project_back(0)
        self.project_back(1)
        self.flush()
        self.send_weight(4)
        self.await_weight(PK)
        self.await_weight(PV)
        self.spread_end(0, 0, self.normed_one)
        self.project_heads(0)
        self.pass_weight(PO)
        self.send_weight(5)
        self.send_weight(6)
        self.spread_end(0, 1, self.normed_one)
        self.project_heads(1)
        self.flush()
        self.attend(0, lambda: None)
        self.await_weight(PO)
        self.collect(0, 0, self.out_terms)
        self.collect_far(0, 0)
        self.pass_weight(4)
        self.send_weight(7)
        self.spread_on(2, 0, self.proj_back)
        self.send_weight(8)
        self.send_pair(9)
        self.attend(1, lambda: self.pass_weight(5))
        self.pass_weight(6)
        self.collect(0, 1, self.out_terms)
        self.collect_far(0, 1)
        self.spread_on(2, 1, self.proj_back)
        self.send_weight(9, False)
        self.second_norm(0)
        self.pass_weight(7)
        self.send_weight(10)
        self.pass_weight(8)
        self.send_weight(11)
        self.second_norm(1)
        self.relay_weight(6)
        self.pass_weight(9)
        self.spread_on(1, 0, self.normed_two)
        self.pass_weight(10)
        self.spread_end(1, 0, self.normed_two)
        self.spread_end(2, 0, self.proj_back)
        self.await_weight(4)
        self.await_weight(5)
        self.feed(0, 0)
        self.await_weight(6)
        self.await_weight(7)
        self.feed(0, 1)
        self.spread_on(1, 1, self.normed_two)
        self.pass_weight(11)
        self.relay_weight(9)

        def up_grad(chunk, send=True):
            cols = slice(chunk * TILE, (chunk + 1) * TILE)
            self.grad_make(4 + 2 * chunk, self.normed_two, self.pre_back[:, cols], send)

        def down_grad(chunk, send=True):
            cols = slice(chunk * TILE, (chunk + 1) * TILE)
            self.grad_make(5 + 2 * chunk, self.proj_back, self.activated[:, cols], send)

        self.await_weight(8)
        self.await_weight(9)
        self.feed(0, 2)
        self.flush()
        self.spread_end(1, 1, self.normed_two)
        self.spread_end(2, 1, self.proj_back)
        self.feed(1, 0)
        up_grad(0)
        down_grad(0)
        self.await_weight(10)
        self.await_weight(11)
        self.feed(0, last)
        self.collect(2, 0, self.wide_terms(self.pre_back, 4))
        self.collect_far(2, 0)
        self.feed(1, 1)
        up_grad(1)
        down_grad(1)
        self.feed(1, 2)
        self.feed(1, last)
        self.collect(2, 1, self.wide_terms(self.pre_back, 4))
        self.second_norm_back(0)
        up_grad(2)
        down_grad(2)
        self.collect_far(2, 1)
        self.collect(1, 0, self.wide_terms(self.activated, 5))
        self.grad_pass(6)
        self.spread_on(3, 0, self.attended_back)
        up_grad(3)
        self.spread_end(3, 0, self.attended_back)

        def between_first():
            self.grad_pass(7)
            self.second_norm_back(1)
            self.grad_relay(4)

        self.attend_back(0, between_first)
        down_grad(3)
        self.collect(3, 0, self.input_terms)
        self.grad_pass(9)
        self.spread_on(3, 1, self.attended_back)
        self.collect_far(3, 0)
        self.spread_sent(2)
        self.grad_relay(5)
        self.spread_end(3, 1, self.attended_back)
        self.grad_make(PO, self.attended_back, self.mixed[...])
        self.grad_pass(10)

        def between_second():
            self.grad_pass(11)
            self.grad_relay(6)
            self.grad_relay(7)
            self.grad_relay(8)

        self.attend_back(1, between_second)
        self.collect(3, 1, self.input_terms)
        self.collect_far(3, 1)
        self.grad_make(PV, self.normed_one, self.values[...])
        self.grad_pass(PO)
        self.grad_cross(4)
        self.grad_cross(5)
        self.grad_make(PQ, self.normed_one, self.queries[...])
        self.grad_make(PK, self.normed_one, self.keys[...])
        self.collect(1, 1, self.wide_terms(self.activated, 5))
        self.collect_far(1, 0)
        self.collect_far(1, 1)
        self.grad_relay(9)
        self.grad_pass(PV)
        self.grad_cross(8)
        self.grad_relay(10)
        self.grad_relay(11)
        self.first_norm_back(0)
        self.first_norm_back(1)
        self.give_vectors()
        self.grad_pass(PQ)
        self.grad_relay(PO)
        self.grad_relay(PV)
        self.grad_pass(PK)
        self.give_result(0)
        for piece in range(4, pieces):
            self.grad_end(piece)
        self.end_vectors()
        self.give_result(1)
        self.last_vectors()
        for piece in (PO, PV, PQ, PK):
            self.grad_end(piece)
        for kind in (0, 1, 3):
            self.spread_sent(kind)
        for one in self.late + self.stage_sends[0] + self.stage_sends[1]:
            one.wait_send()
        for piece in range(pieces):
            self.weight_sent(piece)
            self.grad_sent(piece)
        if self.own_vectors:
            for step in range(1, self.dps):
                self.vector_copy(step).wait_send()
                self.share_copy(step).wait_send()
            for step in range(1, 4):
                self.group_copy(step).wait_send()


def layer_kernel(size, names, *refs):
    named = dict(zip(names, refs))
    named["small"] = [named[name] for name in names if name.startswith("small_")]
    Layer(size, named).run()


def fused_layer(size, counts, tau, images, out_grad, small, weights):
    width, shard, part, rows, pad = (size[key] for key in ("width", "shard", "part", "rows", "pad"))
    lines, dps, pieces = size["lines"], size["dps"], 4 + 2 * size["chunks"]
    units = size["chunks"] * TILE
    vmem = pl.BlockSpec(memory_space=pltpu.VMEM)
    anywhere = pl.BlockSpec(memory_space=pl.ANY)
    vector_shape = (16, 128) if size["own_vectors"] else (16, width)
    outputs = {
        "rows_g": ((2,) + images.shape, BF16),
        "weight_g": ((shard, pieces * TILE + 2 * TILE), F32),
        "vector_g": (vector_shape, F32),
    }
    four = lines == 4
    channels = pieces + (len(PAIR_FIRST) if four else 0)
    pair_slots = pieces * lines - (len(LINE_FIRST) * (lines - 1) if four else 0)
    sum_channels = pieces + (len(LINE_FIRST) if four else 0)
    lines_in = 4 if four else lines - 1
    dma = pltpu.SemaphoreType.DMA
    vm = pltpu.VMEM
    scratch = {
        "weights": vm((pieces, width, TILE), BF16),
        "normed_one": vm((2 * rows, width), BF16),
        "normed_two": vm((2 * rows, width), BF16),
        "proj_back": vm((2 * rows, width), BF16),
        "attended_back": vm((2 * rows, width), BF16),
        "queries": vm((2 * rows, TILE), BF16),
        "keys": vm((2 * rows, TILE), BF16),
        "values": vm((2 * rows, TILE), BF16),
        "mixed": vm((2 * rows, TILE), BF16),
        "mixed_turned": vm((2, TILE, rows), F32),
        "log_total": vm((2, size["heads"], rows), F32),
        "activated": vm((2 * rows, units), BF16),
        "pre_back": vm((2 * rows, units), BF16),
        "turned": vm((TILE, 2 * rows), BF16),
        "mixed_back": vm((rows, TILE), BF16),
        "key_sum": vm((rows, TILE), F32),
        "value_sum": vm((rows, TILE), F32),
        "probs": vm((rows, rows), BF16),
        "score_back": vm((rows, rows), BF16),
        "stage": vm((2, 2, pad, width), BF16),
        "keep": vm((2, 2, 2, pad, width), F32),
        "sib_in": vm((4, 2, 2, pad, width), BF16),
        "far_in": vm((4, 2, pad, width), BF16),
        "after_attn": vm((2, part, width), F32),
        "attn_back": vm((2, part, width), F32),
        "wide_sums": vm((pieces - 4, width, TILE), BF16),
        "pair_in": vm((pair_slots, shard, TILE), BF16),
        "line_in": vm((sum_channels, lines_in, shard, TILE), BF16),
        "vectors": vm((16, width), F32),
        "sums": vm((16, width), F32),
        "wz_send": dma((channels, lines_in)),
        "wz_recv": dma((channels, lines - 1)),
        "wx_send": dma((pieces, lines)),
        "wx_recv": dma((pieces, lines)),
        "wl_sem": dma((pieces,)),
        "ag_send": dma((4, 2, 3)),
        "ag_recv": dma((4, 2, 3)),
        "rs_send": dma((4, 2, 3)),
        "rs_recv": dma((4, 2, 3)),
        "gx_send": dma((pieces, lines)),
        "gx_recv": dma((pieces, lines)),
        "gz_send": dma((sum_channels, lines - 1)),
        "gz_recv": dma((sum_channels, lines_in)),
    }
    if size["own_vectors"]:
        scratch |= {
            "own_packed": vm((16, 128), F32),
            "vectors_in": vm((dps, 16, 128), F32),
            "shares": vm((dps, 16, 128), F32),
            "shares_in": vm((dps - 1, 16, 128), F32),
            "group": vm((4, 16, 128), F32),
            "v_send": dma((2, dps - 1)),
            "v_recv": dma((2, dps - 1)),
            "m_send": dma((3,)),
            "m_recv": dma((3,)),
        }
    inputs = ["counts", "tau", "images", "out_grad"] + [f"small_{at}" for at in range(len(small))]
    inputs += ["query_w", "key_w", "value_w", "out_w", "up_w", "down_w"]
    names = inputs + list(outputs) + list(scratch)
    return pl.pallas_call(
        functools.partial(layer_kernel, size, names),
        out_shape=[jax.ShapeDtypeStruct(*spec) for spec in outputs.values()],
        in_specs=[pl.BlockSpec(memory_space=pltpu.SMEM)] * 2
        + [vmem] * (2 + len(small))
        + [anywhere] * 6,
        out_specs=[vmem] * len(outputs),
        scratch_shapes=list(scratch.values()),
        compiler_params=pltpu.CompilerParams(
            collective_id=0, has_side_effects=True, vmem_limit_bytes=65024 * 2**10
        ),
    )(counts, tau, images, out_grad, *small, *weights)


def on_device(
    images,
    counts,
    first_gain,
    first_shift,
    query_weight,
    query_bias,
    key_weight,
    value_weight,
    value_bias,
    out_weight,
    out_bias,
    second_gain,
    second_shift,
    up_weight,
    up_bias,
    down_weight,
    down_bias,
    clip_tau,
    out_grad,
):
    part, width = images.shape[2:]
    dps = lax.axis_size("dp")
    dp_at = lax.axis_index("dp")
    shard = query_weight.shape[0]
    pad = (part + 15) // 16 * 16
    size = {
        "width": width,
        "shard": shard,
        "part": part,
        "pad": pad,
        "rows": pad * lax.axis_size("mp"),
        "dps": dps,
        "lines": dps // 2,
        "heads": query_weight.shape[1] // HD,
        "chunks": up_weight.shape[1] // TILE,
        "own_vectors": shard == 128,
    }
    bias_cols = query_bias.shape[1]
    parts = [first_gain, first_shift, out_bias, second_gain, second_shift, down_bias, up_bias[0]]
    if size["own_vectors"]:
        small = [one.reshape(1, -1) for one in parts] + [query_bias, value_bias]
    else:
        whole = [lax.all_gather(one, "dp", axis=0, tiled=True) for one in parts]
        rest = [
            jnp.pad(lax.all_gather(one[0], "dp", axis=0, tiled=True), (0, width - TILE))
            for one in (query_bias, value_bias)
        ]
        filler = jnp.zeros((width,), BF16)
        small = [jnp.stack(whole + [filler] + rest + [filler] * 6).astype(F32)]
    weights = (query_weight, key_weight, value_weight, out_weight, up_weight, down_weight)
    rows_g, weight_g, vector_g = fused_layer(
        size, counts.reshape(-1), clip_tau.reshape(1, 1), images, out_grad, small, weights
    )
    columns, units = query_weight.shape[1], up_weight.shape[1]
    edges = [0, columns, 2 * columns, 3 * columns, 4 * columns]
    edges += [edges[-1] + units, edges[-1] + 2 * units]
    query_g, key_g, value_g, out_g, up_g, down_g = (
        weight_g[:, low:high] for low, high in zip(edges[:-1], edges[1:])
    )
    if size["own_vectors"]:
        vectors = [vector_g[row] for row in range(7)]
        query_bias_g = vector_g[DQB : DQB + 1, :bias_cols]
        value_bias_g = vector_g[DVB : DVB + 1, :bias_cols]
        peaks = vector_g[PEAK, : size["heads"]]
        clipped_query = weight_g[:, edges[-1] : edges[-1] + columns]
        clipped_key = weight_g[:, edges[-1] + columns :]
        clipped_bias = vector_g[PEAK + 1 : PEAK + 2, :bias_cols]
    else:
        mine = vector_g[:DUB]
        mine = lax.psum(mine, "mp")
        mine = lax.psum_scatter(mine, "dp", scatter_dimension=1, tiled=True)
        up_bias_g = lax.psum_scatter(vector_g[DUB], "dp", scatter_dimension=0, tiled=True)
        vectors = [mine[row] for row in range(6)] + [up_bias_g]
        both = vector_g[DQB : DVB + 1, :TILE]
        both = lax.psum_scatter(both, "dp", scatter_dimension=1, tiled=True)
        query_bias_g, value_bias_g = both[0:1], both[1:2]
        peaks = lax.pmax(vector_g[PEAK, : size["heads"]], "dp")
        head_root = jnp.sqrt(clip_tau / jnp.maximum(peaks, clip_tau))
        column_root = jnp.repeat(head_root, HD)
        clipped_query = query_weight.astype(F32) * column_root[None, :]
        clipped_key = key_weight.astype(F32) * column_root[None, :]
        bias_root = lax.dynamic_slice(column_root, (dp_at * bias_cols,), (bias_cols,))
        clipped_bias = query_bias.astype(F32) * bias_root[None, :]
    return (
        rows_g[0],
        rows_g[1],
        vectors[DG1],
        vectors[DS1],
        query_g,
        query_bias_g,
        key_g,
        value_g,
        value_bias_g,
        out_g,
        vectors[DOB],
        vectors[DG2],
        vectors[DS2],
        up_g,
        vectors[DUB][None, :],
        down_g,
        vectors[DDB],
        peaks,
        clipped_query,
        clipped_key,
        clipped_bias,
    )


def solution(mesh):
    rows = P(None, "dp", "mp", None)
    wide, small, bias = P("dp", "mp"), P("dp"), P("mp", "dp")
    return jax.shard_map(
        on_device,
        mesh=mesh,
        in_specs=(
            rows,
            P(None, "dp"),
            small,
            small,
            wide,
            bias,
            wide,
            wide,
            bias,
            wide,
            small,
            small,
            small,
            wide,
            bias,
            wide,
            small,
            P(),
            rows,
        ),
        out_specs=(
            rows,
            rows,
            small,
            small,
            wide,
            bias,
            wide,
            wide,
            bias,
            wide,
            small,
            small,
            small,
            wide,
            bias,
            wide,
            small,
            P("mp"),
            wide,
            wide,
            bias,
        ),
        check_vma=False,
    )
```
